32 devices in a mesh: rep: 2 (over y), hid: 4 (over z), wid: 4 (over x, core).
Axes of the slice: x: 2, y: 2, z: 4, core: 2. Of those that a mesh axis runs over, the one named last changes fastest.
Arguments:
- tokens: bfloat16 [128, 8192], P(('rep', 'hid'), 'wid'), parts along dimension 0, may hold values from -6 to 6
- gate_weight: bfloat16 [8192, 26624], P('wid', 'hid'), may hold values from -0.0625 to 0.0625
- up_weight: bfloat16 [8192, 26624], P('wid', 'hid'), may hold values from -0.0625 to 0.0625
- down_weight: bfloat16 [26624, 8192], P('hid', 'wid'), may hold values from -0.0390625 to 0.0390625
Outputs:
- mixed: bfloat16 [128, 8192], P(('rep', 'hid'), 'wid'), parts along dimension 0
The draws below stay inside these ranges and needn't reach their ends.
There are 2 independent parts, one for each index of `rep`. The reference program is written for one: setup_inputs(seed, part) draws one part's arguments, and reference() takes and returns one part's arrays. A program takes and returns all parts, laid end to end along the dimension named above; an argument that names none is the same for every part. Nothing has to cross between parts.
All inputs are finite; a program needn't handle non-finite values.
Results may differ from the reference program's by a relative error of at most 0.02.
Values may be sent and summed in bfloat16 or wider, within the bound.
No kernel may reach another device: no remote copies, remote signals or barrier semaphores. Data moves between devices by JAX's collectives and lax.ppermute only.
A program may use at most 192 MiB of HBM per device.

```python
import jax
import jax.numpy as jnp
from jax import lax

D = 8192
FF = 26624
TOKENS = 64
N_HID = 4
N_WID = 4


def shard_levels(own_key, dims, shards, smallest, top_value):
    factor_of, own = 1.0, jax.random.fold_in(own_key, 6)
    for position, parts in shards:
        heights = jnp.exp(jax.random.uniform(jax.random.fold_in(own, position), (parts,), jnp.float32, smallest / len(shards), top_value / len(shards)))
        factor_of = factor_of * jnp.repeat(heights, dims[position] // parts).reshape([-1 if axis == position else 1 for axis in range(len(dims))])
    return factor_of


def centred(own_key, extent, deviation, limit, split=(), dtype=jnp.bfloat16):
    drawn = deviation * jax.random.normal(own_key, extent, jnp.float32)
    if split:
        drawn = drawn * shard_levels(own_key, extent, split, -0.22, 0.18)
    return jnp.clip(drawn, -limit, limit).astype(dtype)


def setup_inputs(seed: int = 0, part: int = 0) -> dict:
    streams_of = jax.random.split(jax.random.key(seed), 5)
    part_keys = jax.random.split(jax.random.fold_in(streams_of[4], part), 5)
    return {
        "tokens": centred(part_keys[0], (TOKENS, D), 1.0, 6.0, ((0, 4), (1, 4))),
        "gate_weight": centred(streams_of[1], (D, FF), D ** -0.5, 0.0625, ((0, 4), (1, 4))),
        "up_weight": centred(streams_of[2], (D, FF), D ** -0.5, 0.0625, ((0, 4), (1, 4))),
        "down_weight": centred(streams_of[3], (FF, D), FF ** -0.5, 0.0390625, ((0, 4), (1, 4))),
    }


def reference(tokens, gate_weight, up_weight, down_weight):
    group = D // N_WID
    gate = jnp.zeros((tokens.shape[0], FF), jnp.float32)
    up_sum = jnp.zeros((tokens.shape[0], FF), jnp.float32)
    for block in range(N_WID):
        rows = tokens[:, block * group:(block + 1) * group]
        gate_part = jnp.dot(rows, gate_weight[block * group:(block + 1) * group], preferred_element_type=jnp.float32).astype(jnp.bfloat16)
        up_part = jnp.dot(rows, up_weight[block * group:(block + 1) * group], preferred_element_type=jnp.float32).astype(jnp.bfloat16)
        gate_part, up_part = lax.optimization_barrier((gate_part, up_part))
        gate = gate + gate_part.astype(jnp.float32)
        up_sum = up_sum + up_part.astype(jnp.float32)
    hidden = (jax.nn.silu(gate) * up_sum).astype(jnp.bfloat16)
    width = FF // N_HID
    mixed = jnp.zeros((tokens.shape[0], D), jnp.float32)
    for block in range(N_HID):
        out_part = jnp.dot(hidden[:, block * width:(block + 1) * width], down_weight[block * width:(block + 1) * width], preferred_element_type=jnp.float32).astype(jnp.bfloat16)
        out_part = lax.optimization_barrier(out_part)
        mixed = mixed + out_part.astype(jnp.float32)
    return mixed.astype(jnp.bfloat16)
```

```python
import functools

import jax
import jax.numpy as jnp
from jax import lax
from jax.experimental import pallas as pl
from jax.experimental.pallas import tpu as pltpu
from jax.sharding import PartitionSpec as P

TILE = 256
CHUNKS = 2


def plain(tokens, gate_weight, up_weight, down_weight):
    piece = lax.all_gather(tokens, "hid", axis=0, tiled=True)
    gate_rows = jnp.dot(piece, gate_weight, preferred_element_type=jnp.float32)
    up_rows = jnp.dot(piece, up_weight, preferred_element_type=jnp.float32)
    partial_terms = jnp.stack([gate_rows, up_rows], 0)
    summed = lax.psum(partial_terms.astype(jnp.bfloat16), "wid").astype(jnp.float32)
    hidden = (jax.nn.silu(summed[0]) * summed[1]).astype(jnp.bfloat16)
    return lax.psum_scatter(
        jnp.dot(hidden, down_weight, preferred_element_type=jnp.float32).astype(jnp.bfloat16),
        "hid",
        scatter_dimension=0,
        tiled=True,
    )


ORDER = (0, 2, 1, 3)
PLACE = (0, 2, 1, 3)


def gate_up_kernel(n_blocks, rows, scalars, *refs):
    blocks, (gate_ref, up_ref, mine_ref, theirs_ref, x_ref) = refs[:n_blocks], refs[n_blocks:]

    @pl.when(pl.program_id(0) == 0)
    def _():
        for b in range(n_blocks):
            start = pl.multiple_of(scalars[1 + b] * rows, rows)
            x_ref[pl.ds(start, rows), :] = blocks[b][...]

    half = x_ref.shape[0] // 2
    for k, w_ref in enumerate((gate_ref, up_ref)):
        part = jnp.dot(x_ref[...], w_ref[...], preferred_element_type=jnp.float32).astype(jnp.bfloat16)
        mine_ref[k] = part[:half]
        theirs_ref[k] = part[half:]


def gate_up(scalars, blocks, gate_weight, up_weight, first, tiles):
    depth = gate_weight.shape[0]
    rows = blocks[0].shape[0]
    n = len(blocks)
    total = n * rows
    width = tiles * TILE
    weight_spec = pl.BlockSpec((depth, TILE), lambda i, s: (0, s[0] + first + i))
    out_spec = pl.BlockSpec((2, total // 2, TILE), lambda i, s: (0, 0, i))
    return pl.pallas_call(
        functools.partial(gate_up_kernel, n, rows),
        grid_spec=pltpu.PrefetchScalarGridSpec(
            num_scalar_prefetch=1,
            grid=(tiles,),
            in_specs=[pl.BlockSpec((rows, depth), lambda i, s: (0, 0))] * n + [weight_spec] * 2,
            out_specs=[out_spec] * 2,
            scratch_shapes=[pltpu.VMEM((total, depth), jnp.bfloat16)],
        ),
        out_shape=[jax.ShapeDtypeStruct((2, total // 2, width), jnp.bfloat16)] * 2,
        compiler_params=pltpu.CompilerParams(vmem_limit_bytes=32 * 2**20),
        cost_estimate=pl.CostEstimate(
            flops=4 * total * depth * width, bytes_accessed=4 * depth * width, transcendentals=0
        ),
        name="gate_up",
    )(scalars, *blocks, gate_weight, up_weight)


def down_kernel(n_pieces, n_blocks, has_acc, last, scalars, *refs):
    pieces, refs = refs[:n_pieces], refs[n_pieces:]
    w_ref, refs = refs[0], refs[1:]
    prev_ref, refs = (refs[0], refs[1:]) if has_acc else (None, refs)
    outs, acc_ref = (refs[:-1], refs[-1]) if last else ((), refs[0])
    step = pl.program_id(0)

    @pl.when(step == 0)
    def _():
        acc_ref[...] = prev_ref[...] if has_acc else jnp.zeros_like(acc_ref)

    at = 0
    for piece in pieces:
        n = piece.shape[0]
        acc_ref[at : at + n, :] += jnp.dot(piece[...], w_ref[...], preferred_element_type=jnp.float32)
        at += n

    if last:

        @pl.when(step == pl.num_programs(0) - 1)
        def _():
            for b in range(n_blocks):
                rows = outs[b].shape[0]
                start = pl.multiple_of(scalars[1 + b] * rows, rows)
                outs[b][...] = acc_ref[pl.ds(start, rows), :].astype(jnp.bfloat16)


def down(scalars, pieces, down_weight, prev, first, tiles, n_blocks, last):
    width = down_weight.shape[1]
    total = sum(p.shape[0] for p in pieces)
    rows = total // n_blocks
    whole = pl.BlockSpec((total, width), lambda i, s: (0, 0))
    in_specs = [pl.BlockSpec((p.shape[0], TILE), lambda i, s: (0, i)) for p in pieces]
    in_specs.append(pl.BlockSpec((TILE, width), lambda i, s: (s[0] + first + i, 0)))
    args = [*pieces, down_weight]
    if prev is not None:
        in_specs.append(whole)
        args.append(prev)
    if last:
        out_specs = [pl.BlockSpec((rows, width), lambda i, s: (0, 0))] * n_blocks
        out_shape = [jax.ShapeDtypeStruct((rows, width), jnp.bfloat16)] * n_blocks
        scratch = [pltpu.VMEM((total, width), jnp.float32)]
    else:
        out_specs, out_shape, scratch = whole, jax.ShapeDtypeStruct((total, width), jnp.float32), []
    return pl.pallas_call(
        functools.partial(down_kernel, len(pieces), n_blocks, prev is not None, last),
        grid_spec=pltpu.PrefetchScalarGridSpec(
            num_scalar_prefetch=1,
            grid=(tiles,),
            in_specs=in_specs,
            out_specs=out_specs,
            scratch_shapes=scratch,
        ),
        out_shape=out_shape,
        compiler_params=pltpu.CompilerParams(vmem_limit_bytes=32 * 2**20),
        cost_estimate=pl.CostEstimate(
            flops=2 * total * width * tiles * TILE, bytes_accessed=2 * width * tiles * TILE, transcendentals=0
        ),
        name="down",
    )(scalars, *args)


def split_by_rep(n_rep, n_hid, n_wid, tokens, gate_weight, up_weight, down_weight):
    rep, hid, wid = lax.axis_index("rep"), lax.axis_index("hid"), lax.axis_index("wid")
    n = n_rep * n_hid
    per = n // n_wid
    tiles = gate_weight.shape[1] // (n_rep * TILE)

    def shift(b, back):
        r, h = divmod(b, n_hid)
        sign = -1 if back else 1
        pairs = []
        for i in range(n_rep):
            for j in range(n_hid):
                here = i * n_hid + j
                there = ((i + r) % n_rep) * n_hid + (j + h) % n_hid
                pairs.append((here, there) if back else (there, here))
        return pairs

    place = jnp.asarray(PLACE, jnp.int32)
    owner = jnp.arange(n, dtype=jnp.int32)
    at = place[wid ^ (owner // per)] * per + owner % per
    scalars = jnp.concatenate([jnp.asarray([rep * tiles], jnp.int32), at])

    blocks = [tokens] + [lax.ppermute(tokens, ("rep", "hid"), shift(b, False)) for b in range(1, n)]

    core = [(w, w ^ 1) for w in range(n_wid)]
    chip = [(w, w ^ 2) for w in range(n_wid)]
    f32 = jnp.float32

    bounds = [tiles * c // CHUNKS for c in range(CHUNKS + 1)]
    acc = None
    for c in range(CHUNKS):
        first, count = bounds[c], bounds[c + 1] - bounds[c]
        mine, theirs = gate_up(scalars, blocks, gate_weight, up_weight, first, count)
        got = lax.ppermute(theirs, "wid", core)
        quarter = mine.shape[1] // 2
        to_chip = (mine[:, quarter:].astype(f32) + got[:, quarter:].astype(f32)).astype(jnp.bfloat16)
        from_chip = lax.ppermute(to_chip, "wid", chip)
        summed = mine[:, :quarter].astype(f32) + got[:, :quarter].astype(f32) + from_chip.astype(f32)
        own = (jax.nn.silu(summed[0]) * summed[1]).astype(jnp.bfloat16)
        other = lax.ppermute(own, "wid", chip)
        own_core = lax.ppermute(own, "wid", core)
        other_core = lax.ppermute(other, "wid", core)
        acc = down(
            scalars, [own, other, own_core, other_core], down_weight, acc, first, count, n, c == CHUNKS - 1
        )

    mixed = acc[0].astype(f32)
    for b in range(1, n):
        mixed = mixed + lax.ppermute(acc[b], ("rep", "hid"), shift(b, True)).astype(f32)
    return mixed.astype(jnp.bfloat16)


def solution(mesh):
    n_rep, n_hid, n_wid = (mesh.shape[a] for a in ("rep", "hid", "wid"))

    def on_device(tokens, gate_weight, up_weight, down_weight):
        fits = (
            n_wid == len(ORDER)
            and n_rep * n_hid % n_wid == 0
            and gate_weight.shape[1] % (n_rep * TILE) == 0
            and tokens.shape[0] % 16 == 0
        )
        if not fits:
            return plain(tokens, gate_weight, up_weight, down_weight)
        return split_by_rep(n_rep, n_hid, n_wid, tokens, gate_weight, up_weight, down_weight)

    return jax.shard_map(
        on_device,
        mesh=mesh,
        in_specs=(P(("rep", "hid"), "wid"), P("wid", "hid"), P("wid", "hid"), P("hid", "wid")),
        out_specs=P(("rep", "hid"), "wid"),
        check_vma=False,
    )
```

```python
import functools

import jax
import jax.numpy as jnp
from jax import lax
from jax.experimental import pallas as pl
from jax.experimental.pallas import tpu as pltpu
from jax.sharding import PartitionSpec as P

TILE = 256
CHUNKS = 2


def plain(tokens, gate_weight, up_weight, down_weight):
    piece = lax.all_gather(tokens, "hid", axis=0, tiled=True)
    gate_rows = jnp.dot(piece, gate_weight, preferred_element_type=jnp.float32)
    up_rows = jnp.dot(piece, up_weight, preferred_element_type=jnp.float32)
    partial_terms = jnp.stack([gate_rows, up_rows], 0)
    summed = lax.psum(partial_terms.astype(jnp.bfloat16), "wid").astype(jnp.float32)
    hidden = (jax.nn.silu(summed[0]) * summed[1]).astype(jnp.bfloat16)
    return lax.psum_scatter(
        jnp.dot(hidden, down_weight, preferred_element_type=jnp.float32).astype(jnp.bfloat16),
        "hid",
        scatter_dimension=0,
        tiled=True,
    )


SEND_ORDER = (7, 6, 5, 4, 3, 2, 1, 0)
ROWS = 16


def pieces_of(width, most):
    first = width % most
    edges = ([0] if first else []) + list(range(first, width + 1, most))
    return list(zip(edges[:-1], edges[1:]))


def place(wid, b):
    step = wid ^ (b % 4)
    return (step % 2) * 4 + (step // 2) * 2 + b // 4


def gate_up_kernel(n_blocks, rows, first, width, where, *refs):
    blocks, refs = refs[:n_blocks], refs[n_blocks:]
    gate_ref, up_ref, mine_ref, theirs_ref, x_ref, w_ref, sems = refs
    start = pl.multiple_of(where[0] + first, TILE)
    cuts = pieces_of(width, 2 * TILE)

    def copy(i, k):
        a, b = cuts[i]
        source = (gate_ref, up_ref)[k].at[:, pl.ds(start + a, b - a)]
        return pltpu.make_async_copy(source, w_ref.at[k, :, a:b], sems.at[k, i])

    for i in range(len(cuts)):
        for k in range(2):
            copy(i, k).start()
    for b in range(n_blocks):
        at = pl.multiple_of(place(where[1], b) * rows, rows)
        x_ref[pl.ds(at, rows), :] = blocks[b][...]
    half = x_ref.shape[0] // 2
    for i, (a, b) in enumerate(cuts):
        for k in range(2):
            copy(i, k).wait()
            part = jnp.dot(x_ref[...], w_ref[k, :, a:b], preferred_element_type=jnp.float32).astype(jnp.bfloat16)
            mine_ref[k, :, a:b] = part[:half]
            theirs_ref[k, :, a:b] = part[half:]


def gate_up(where, blocks, gate_weight, up_weight, first, width):
    depth = gate_weight.shape[0]
    rows = blocks[0].shape[0]
    n = len(blocks)
    total = n * rows
    n_cuts = len(pieces_of(width, 2 * TILE))
    vmem, hbm = pl.BlockSpec(memory_space=pltpu.VMEM), pl.BlockSpec(memory_space=pltpu.HBM)
    return pl.pallas_call(
        functools.partial(gate_up_kernel, n, rows, first, width),
        in_specs=[pl.BlockSpec(memory_space=pltpu.SMEM)] + [vmem] * n + [hbm] * 2,
        out_specs=[vmem] * 2,
        scratch_shapes=[
            pltpu.VMEM((total, depth), jnp.bfloat16),
            pltpu.VMEM((2, depth, width), jnp.bfloat16),
            pltpu.SemaphoreType.DMA((2, n_cuts)),
        ],
        out_shape=[jax.ShapeDtypeStruct((2, total // 2, width), jnp.bfloat16)] * 2,
        compiler_params=pltpu.CompilerParams(vmem_limit_bytes=28 * 2**20),
        cost_estimate=pl.CostEstimate(
            flops=4 * total * depth * width, bytes_accessed=4 * depth * width, transcendentals=0
        ),
        name="gate_up",
    )(where, *blocks, gate_weight, up_weight)


def down_kernel(n_pieces, has_acc, last, first, depth, where, *refs):
    pieces, refs = refs[:n_pieces], refs[n_pieces:]
    down_ref, refs = refs[0], refs[1:]
    prev_ref, refs = (refs[0], refs[1:]) if has_acc else (None, refs)
    outs, (acc_ref, lhs_ref, w_ref, sems) = refs[:-4], refs[-4:]
    start = pl.multiple_of(where[0] + first, TILE)
    cuts = pieces_of(depth, 2 * TILE)

    def copy(i):
        a, b = cuts[i]
        return pltpu.make_async_copy(down_ref.at[pl.ds(start + a, b - a), :], w_ref.at[a:b, :], sems.at[i])

    for i in range(len(cuts)):
        copy(i).start()
    at = 0
    for piece in pieces:
        lhs_ref[at : at + piece.shape[0], :] = piece[...]
        at += piece.shape[0]
    for i, (a, b) in enumerate(cuts):
        copy(i).wait()
        part = jnp.dot(lhs_ref[:, a:b], w_ref[a:b, :], preferred_element_type=jnp.float32)
        if i > 0:
            part = part + acc_ref[...]
        elif has_acc:
            part = part + prev_ref[...]
        acc_ref[...] = part
    if last:
        order = iter(SEND_ORDER)
        for out in outs:
            for at in range(0, out.shape[0], ROWS):
                source = pl.multiple_of(place(where[1], next(order)) * ROWS, ROWS)
                out[at : at + ROWS, :] = acc_ref[pl.ds(source, ROWS), :].astype(out.dtype)


def down(where, pieces, down_weight, prev, first, depth, out_rows):
    width = down_weight.shape[1]
    total = sum(p.shape[0] for p in pieces)
    last = bool(out_rows)
    vmem, hbm = pl.BlockSpec(memory_space=pltpu.VMEM), pl.BlockSpec(memory_space=pltpu.HBM)
    args = [*pieces, down_weight] + ([] if prev is None else [prev])
    sums = jax.ShapeDtypeStruct((total, width), jnp.float32)
    scratch = [
        pltpu.VMEM((total, depth), jnp.bfloat16),
        pltpu.VMEM((depth, width), jnp.bfloat16),
        pltpu.SemaphoreType.DMA((len(pieces_of(depth, 2 * TILE)),)),
    ]
    if last:
        scratch = [pltpu.VMEM(sums.shape, sums.dtype)] + scratch
    return pl.pallas_call(
        functools.partial(down_kernel, len(pieces), prev is not None, last, first, depth),
        in_specs=[pl.BlockSpec(memory_space=pltpu.SMEM)]
        + [vmem] * len(pieces)
        + [hbm]
        + ([] if prev is None else [vmem]),
        out_specs=[vmem] * len(out_rows) if last else vmem,
        scratch_shapes=scratch,
        out_shape=[jax.ShapeDtypeStruct((r, width), jnp.bfloat16) for r in out_rows] if last else sums,
        compiler_params=pltpu.CompilerParams(vmem_limit_bytes=20 * 2**20),
        cost_estimate=pl.CostEstimate(
            flops=2 * total * width * depth, bytes_accessed=2 * width * depth, transcendentals=0
        ),
        name="down",
    )(where, *args)


def split_by_rep(n_wid, tokens, gate_weight, up_weight, down_weight):
    rep, wid = lax.axis_index("rep"), lax.axis_index("wid")
    f32, bf16 = jnp.float32, jnp.bfloat16
    rows = tokens.shape[0]
    width = gate_weight.shape[1] // 2

    def swap(x, axis, step):
        n = {"rep": 2, "hid": 4, "wid": n_wid}[axis]
        return lax.ppermute(x, axis, [(i, i ^ step) for i in range(n)])

    near = [tokens, swap(tokens, "hid", 1), swap(tokens, "hid", 2)]
    near.append(swap(near[2], "hid", 1))
    blocks = near + [swap(x, "rep", 1) for x in near]

    where = jnp.stack([rep * width, wid]).astype(jnp.int32)
    gate_weight, up_weight, down_weight = (
        pltpu.with_memory_space_constraint(w, pltpu.HBM) for w in (gate_weight, up_weight, down_weight)
    )

    tiles = width // TILE
    bounds = [tiles * c // CHUNKS * TILE for c in range(CHUNKS + 1)]
    acc = None
    for c in range(CHUNKS):
        first, count = bounds[c], bounds[c + 1] - bounds[c]
        mine, theirs = gate_up(where, blocks, gate_weight, up_weight, first, count)
        got = swap(theirs, "wid", 1)
        quarter = 2 * rows
        to_chip = (mine[:, quarter:].astype(f32) + got[:, quarter:].astype(f32)).astype(bf16)
        from_chip = swap(to_chip, "wid", 2)
        summed = mine[:, :quarter].astype(f32) + got[:, :quarter].astype(f32) + from_chip.astype(f32)
        own = (jax.nn.silu(summed[0]) * summed[1]).astype(bf16)
        other = swap(own, "wid", 2)
        pieces = [own, other, swap(own, "wid", 1), swap(other, "wid", 1)]
        out_rows = [2 * rows, 2 * rows, 4 * rows] if c == CHUNKS - 1 else []
        acc = down(where, pieces, down_weight, acc, first, count, out_rows)

    far_32, far_10, kept = acc
    kept = kept.astype(f32)
    sums_32 = kept[: 2 * rows] + swap(far_32, "rep", 1).astype(f32)
    sums_10 = kept[2 * rows :] + swap(far_10, "rep", 1).astype(f32)
    via = sums_32[rows:] + swap(sums_32[:rows].astype(bf16), "hid", 1).astype(f32)
    mixed = sums_10[rows:] + swap(sums_10[:rows].astype(bf16), "hid", 1).astype(f32)
    mixed = mixed + swap(via.astype(bf16), "hid", 2).astype(f32)
    return mixed.astype(bf16)


def solution(mesh):
    n_rep, n_hid, n_wid = (mesh.shape[a] for a in ("rep", "hid", "wid"))

    def on_device(tokens, gate_weight, up_weight, down_weight):
        fits = (
            (n_rep, n_hid, n_wid) == (2, 4, 4)
            and gate_weight.shape[1] % (n_rep * TILE) == 0
            and tokens.shape[0] == ROWS
        )
        if not fits:
            return plain(tokens, gate_weight, up_weight, down_weight)
        return split_by_rep(n_wid, tokens, gate_weight, up_weight, down_weight)

    return jax.shard_map(
        on_device,
        mesh=mesh,
        in_specs=(P(("rep", "hid"), "wid"), P("wid", "hid"), P("wid", "hid"), P("hid", "wid")),
        out_specs=P(("rep", "hid"), "wid"),
        check_vma=False,
    )
```

```python
import functools

import jax
import jax.numpy as jnp
from jax import lax
from jax.experimental import pallas as pl
from jax.experimental.pallas import tpu as pltpu
from jax.sharding import PartitionSpec as P

TILE = 256
CHUNKS = 3
ROWS = 16


def plain(tokens, gate_weight, up_weight, down_weight):
    piece = lax.all_gather(tokens, "hid", axis=0, tiled=True)
    gate_rows = jnp.dot(piece, gate_weight, preferred_element_type=jnp.float32)
    up_rows = jnp.dot(piece, up_weight, preferred_element_type=jnp.float32)
    partial_terms = jnp.stack([gate_rows, up_rows], 0)
    summed = lax.psum(partial_terms.astype(jnp.bfloat16), "wid").astype(jnp.float32)
    hidden = (jax.nn.silu(summed[0]) * summed[1]).astype(jnp.bfloat16)
    return lax.psum_scatter(
        jnp.dot(hidden, down_weight, preferred_element_type=jnp.float32).astype(jnp.bfloat16),
        "hid",
        scatter_dimension=0,
        tiled=True,
    )


def pieces_of(width, most):
    first = width % most
    edges = ([0] if first else []) + list(range(first, width + 1, most))
    return list(zip(edges[:-1], edges[1:]))


def place(wid, d):
    step = wid ^ d
    return (step % 2) * 2 + step // 2


def spec(space):
    return pl.BlockSpec(memory_space=space)


def params(mib):
    return pltpu.CompilerParams(vmem_limit_bytes=mib * 2**20)


def fetch_kernel(first, width, where, *refs):
    n = len(refs) // 2
    sources, outs, sems = refs[:n], refs[n : 2 * n], refs[-1]
    start = pl.multiple_of(where[0] + first, TILE)
    copies = []
    for source, out in zip(sources, outs):
        if source.shape != out.shape:
            source = source.at[:, pl.ds(start, width)]
        copies.append(pltpu.make_async_copy(source, out, sems.at[len(copies)]))
        copies[-1].start()
    for copy in copies:
        copy.wait()


def fetch(where, arrays, first, width):
    shapes = [a.shape if a.shape[0] == ROWS else (a.shape[0], width) for a in arrays]
    size = sum(2 * x * y for x, y in shapes)
    return pl.pallas_call(
        functools.partial(fetch_kernel, first, width),
        in_specs=[spec(pltpu.SMEM)] + [spec(pltpu.HBM)] * len(arrays),
        out_specs=[spec(pltpu.VMEM)] * len(arrays),
        out_shape=[pltpu.VMEM(x, jnp.bfloat16) for x in shapes],
        scratch_shapes=[pltpu.SemaphoreType.DMA((len(arrays),))],
        compiler_params=params(1),
        cost_estimate=pl.CostEstimate(flops=0, bytes_accessed=size, transcendentals=0),
        name="fetch",
    )(where, *arrays)


def gate_up_kernel(n_blocks, where, *refs):
    blocks, (gate_ref, up_ref, mine_ref, theirs_ref, x_ref) = refs[:n_blocks], refs[n_blocks:]
    for b in range(n_blocks):
        at = place(where[1], b % 4) * 2 + b // 4
        x_ref[pl.ds(pl.multiple_of(at * ROWS, ROWS), ROWS), :] = blocks[b][...]
    half = x_ref.shape[0] // 2
    for a, b in pieces_of(gate_ref.shape[1], 2 * TILE):
        for k, w_ref in enumerate((gate_ref, up_ref)):
            part = jnp.dot(x_ref[...], w_ref[:, a:b], preferred_element_type=jnp.float32).astype(jnp.bfloat16)
            mine_ref[k, :, a:b] = part[:half]
            theirs_ref[k, :, a:b] = part[half:]


def gate_up(where, blocks, gate, up):
    depth, width = gate.shape
    n = len(blocks)
    total = n * ROWS
    return pl.pallas_call(
        functools.partial(gate_up_kernel, n),
        in_specs=[spec(pltpu.SMEM)] + [spec(pltpu.VMEM)] * (n + 2),
        out_specs=[spec(pltpu.VMEM)] * 2,
        scratch_shapes=[pltpu.VMEM((total, depth), jnp.bfloat16)],
        out_shape=[jax.ShapeDtypeStruct((2, total // 2, width), jnp.bfloat16)] * 2,
        compiler_params=params(4),
        cost_estimate=pl.CostEstimate(
            flops=4 * total * depth * width, bytes_accessed=4 * depth * width, transcendentals=0
        ),
        name="gate_up",
    )(where, *blocks, gate, up)


def down_kernel(n_pieces, has_acc, last, first, half, where, *refs):
    pieces, refs = refs[:n_pieces], refs[n_pieces:]
    down_ref, refs = refs[0], refs[1:]
    prev_ref, refs = (refs[0], refs[1:]) if has_acc else (None, refs)
    outs, (acc_ref, lhs_ref) = refs[:-2], refs[-2:]
    depth = lhs_ref.shape[2]
    for p, piece in enumerate(pieces):
        for k in range(2):
            lhs_ref[k, p * ROWS : (p + 1) * ROWS, :] = piece[k * ROWS : (k + 1) * ROWS, :]
    for a, b in pieces_of(down_ref.shape[1], 2 * TILE):
        part = prev_ref[:, a:b] if has_acc else 0.0
        for k in range(2):
            start = where[0] + first if k == 0 else half - where[0] + first
            rows = pl.ds(pl.multiple_of(start, TILE), depth)
            part += jnp.dot(lhs_ref[k], down_ref[rows, a:b], preferred_element_type=jnp.float32)
        acc_ref[:, a:b] = part
    if last:
        for d, out in enumerate(outs):
            source = pl.multiple_of(place(where[1], d) * ROWS, ROWS)
            out[...] = acc_ref[pl.ds(source, ROWS), :].astype(out.dtype)


def down(where, pieces, down_weight, prev, first, last):
    width = down_weight.shape[1]
    n, depth = len(pieces), pieces[0].shape[1]
    total = n * ROWS
    args = [*pieces, down_weight] + ([] if prev is None else [prev])
    sums = jax.ShapeDtypeStruct((total, width), jnp.float32)
    scratch = [pltpu.VMEM((2, total, depth), jnp.bfloat16)]
    if last:
        scratch = [pltpu.VMEM(sums.shape, sums.dtype)] + scratch
    return pl.pallas_call(
        functools.partial(down_kernel, n, prev is not None, last, first, down_weight.shape[0] // 2),
        in_specs=[spec(pltpu.SMEM)] + [spec(pltpu.VMEM)] * len(args),
        out_specs=[spec(pltpu.VMEM)] * n if last else spec(pltpu.VMEM),
        scratch_shapes=scratch,
        out_shape=[jax.ShapeDtypeStruct((ROWS, width), jnp.bfloat16)] * n if last else sums,
        compiler_params=params(4),
        cost_estimate=pl.CostEstimate(
            flops=4 * total * width * depth, bytes_accessed=4 * width * depth, transcendentals=0
        ),
        name="down",
    )(where, *args)


def split_by_rep(n_wid, tokens, gate_weight, up_weight, down_weight):
    rep, wid = lax.axis_index("rep"), lax.axis_index("wid")
    f32, bf16 = jnp.float32, jnp.bfloat16
    width = gate_weight.shape[1] // 2
    where = jnp.stack([rep * width, wid]).astype(jnp.int32)

    def swap(x, axis, step):
        n = {"rep": 2, "hid": 4, "wid": n_wid}[axis]
        return lax.ppermute(x, axis, [(i, i ^ step) for i in range(n)])

    tiles = width // TILE
    bounds = [tiles * c // CHUNKS * TILE for c in range(CHUNKS + 1)]
    sources = [pltpu.with_memory_space_constraint(w, pltpu.HBM) for w in (gate_weight, up_weight, tokens)]
    weights = [
        fetch(where, sources[: 2 if c else 3], bounds[c], bounds[c + 1] - bounds[c]) for c in range(CHUNKS)
    ]
    own_tokens = weights[0][2]
    down_weight = pltpu.with_memory_space_constraint(down_weight, pltpu.VMEM)

    far = swap(tokens, "hid", 2)
    near = [tokens, swap(tokens, "hid", 1), far, swap(far, "hid", 1)]
    blocks = [own_tokens] + near[1:] + [swap(x, "rep", 1) for x in near]

    quarter = 2 * ROWS
    parts, to_chips = [], []

    def send_to_chip(c):
        mine, got = parts[c]
        to_chips.append((mine[:, quarter:].astype(f32) + got[:, quarter:].astype(f32)).astype(bf16))

    turn = where
    for c in range(CHUNKS):
        if c >= 2:
            send_to_chip(c - 2)
            turn, to_chips[-1] = lax.optimization_barrier((turn, to_chips[-1]))
        mine, theirs = gate_up(turn, blocks, *weights[c][:2])
        parts.append((mine, swap(theirs, "wid", 1)))
    while len(to_chips) < CHUNKS:
        send_to_chip(len(to_chips))

    acc = None
    for c in range(CHUNKS):
        mine, got = parts[c]
        from_chip = swap(to_chips[c], "wid", 2)
        summed = mine[:, :quarter].astype(f32) + got[:, :quarter].astype(f32) + from_chip.astype(f32)
        hidden = (jax.nn.silu(summed[0]) * summed[1]).astype(bf16)
        own = jnp.concatenate([hidden[:ROWS], swap(hidden[ROWS:], "rep", 1)], 0)
        other = swap(own, "wid", 2)
        pieces = [own, other, swap(own, "wid", 1), swap(other, "wid", 1)]
        acc = down(where, pieces, down_weight, acc, bounds[c], c == CHUNKS - 1)

    mixed = acc[0].astype(f32)
    for d in (3, 2, 1):
        mixed = mixed + swap(acc[d], "hid", d).astype(f32)
    return mixed.astype(bf16)


def solution(mesh):
    n_rep, n_hid, n_wid = (mesh.shape[a] for a in ("rep", "hid", "wid"))

    def on_device(tokens, gate_weight, up_weight, down_weight):
        fits = (
            (n_rep, n_hid, n_wid) == (2, 4, 4)
            and gate_weight.shape[1] % (n_rep * TILE) == 0
            and tokens.shape[0] == ROWS
        )
        if not fits:
            return plain(tokens, gate_weight, up_weight, down_weight)
        return split_by_rep(n_wid, tokens, gate_weight, up_weight, down_weight)

    return jax.shard_map(
        on_device,
        mesh=mesh,
        in_specs=(P(("rep", "hid"), "wid"), P("wid", "hid"), P("wid", "hid"), P("hid", "wid")),
        out_specs=P(("rep", "hid"), "wid"),
        check_vma=False,
    )
```

```python
import functools

import jax
import jax.numpy as jnp
from jax import lax
from jax.experimental import pallas as pl
from jax.experimental.pallas import tpu as pltpu
from jax.sharding import PartitionSpec as P

TILE = 256
CHUNKS = 3
ROWS = 16


def plain(tokens, gate_weight, up_weight, down_weight):
    piece = lax.all_gather(tokens, "hid", axis=0, tiled=True)
    gate_rows = jnp.dot(piece, gate_weight, preferred_element_type=jnp.float32)
    up_rows = jnp.dot(piece, up_weight, preferred_element_type=jnp.float32)
    partial_terms = jnp.stack([gate_rows, up_rows], 0)
    summed = lax.psum(partial_terms.astype(jnp.bfloat16), "wid").astype(jnp.float32)
    hidden = (jax.nn.silu(summed[0]) * summed[1]).astype(jnp.bfloat16)
    return lax.psum_scatter(
        jnp.dot(hidden, down_weight, preferred_element_type=jnp.float32).astype(jnp.bfloat16),
        "hid",
        scatter_dimension=0,
        tiled=True,
    )


def pieces_of(width, most):
    first = width % most
    edges = ([0] if first else []) + list(range(first, width + 1, most))
    return list(zip(edges[:-1], edges[1:]))


def place(wid, d):
    step = wid ^ d
    return (step % 2) * 2 + step // 2


def spec(space):
    return pl.BlockSpec(memory_space=space)


def params(mib):
    return pltpu.CompilerParams(vmem_limit_bytes=mib * 2**20)


def fetch_kernel(first, width, where, *refs):
    n = len(refs) // 2 - 1
    sources, outs, flag, sems = refs[:n], refs[n : 2 * n], refs[-2], refs[-1]
    start = pl.multiple_of(where[0] + first, TILE)
    copies = []
    for source, out in zip(sources, outs):
        step = out.shape[0] if source.shape == out.shape else TILE
        for at in range(0, out.shape[0], step):
            rows = slice(at, at + step)
            part = source if source.shape == out.shape else source.at[rows, pl.ds(start, width)]
            copies.append(pltpu.make_async_copy(part, out.at[rows, :], sems.at[len(copies)]))
            copies[-1].start()
    flag[...] = jnp.zeros_like(flag)
    for copy in copies:
        copy.wait()


def fetch(where, arrays, first, width):
    shapes = [a.shape if a.shape[0] == ROWS else (a.shape[0], width) for a in arrays]
    size = sum(2 * x * y for x, y in shapes)
    n = len(arrays)
    return pl.pallas_call(
        functools.partial(fetch_kernel, first, width),
        in_specs=[spec(pltpu.SMEM)] + [spec(pltpu.HBM)] * n,
        out_specs=[spec(pltpu.VMEM)] * (n + 1),
        out_shape=[pltpu.VMEM(x, jnp.bfloat16) for x in shapes] + [pltpu.VMEM((8, 128), jnp.float32)],
        scratch_shapes=[pltpu.SemaphoreType.DMA((sum(-(-x // TILE) for x, _ in shapes),))],
        compiler_params=params(1),
        cost_estimate=pl.CostEstimate(flops=0, bytes_accessed=size, transcendentals=0),
        name="fetch",
    )(where, *arrays)


def gate_up_kernel(n_blocks, where, *refs):
    blocks, (gate_ref, up_ref), (mine_ref, theirs_ref, x_ref) = refs[:n_blocks], refs[n_blocks:][:2], refs[-3:]
    for b in range(n_blocks):
        at = place(where[1], b % 4) * 2 + b // 4
        x_ref[pl.ds(pl.multiple_of(at * ROWS, ROWS), ROWS), :] = blocks[b][...]
    half = x_ref.shape[0] // 2
    for a, b in pieces_of(gate_ref.shape[1], 2 * TILE):
        for k, w_ref in enumerate((gate_ref, up_ref)):
            part = jnp.dot(x_ref[...], w_ref[:, a:b], preferred_element_type=jnp.float32).astype(jnp.bfloat16)
            mine_ref[k, :, a:b] = part[:half]
            theirs_ref[k, :, a:b] = part[half:]


def gate_up(where, blocks, gate, up, behind):
    depth, width = gate.shape
    n = len(blocks)
    total = n * ROWS
    return pl.pallas_call(
        functools.partial(gate_up_kernel, n),
        in_specs=[spec(pltpu.SMEM)] + [spec(pltpu.VMEM)] * (n + 2) + [spec(pl.ANY)] * len(behind),
        out_specs=[spec(pltpu.VMEM)] * 2,
        scratch_shapes=[pltpu.VMEM((total, depth), jnp.bfloat16)],
        out_shape=[jax.ShapeDtypeStruct((2, total // 2, width), jnp.bfloat16)] * 2,
        compiler_params=params(4),
        cost_estimate=pl.CostEstimate(
            flops=4 * total * depth * width, bytes_accessed=4 * depth * width, transcendentals=0
        ),
        name="gate_up",
    )(where, *blocks, gate, up, *behind)


def down_kernel(n_pieces, has_acc, last, first, half, where, *refs):
    pieces, refs = refs[:n_pieces], refs[n_pieces:]
    down_ref, refs = refs[0], refs[1:]
    prev_ref, refs = (refs[0], refs[1:]) if has_acc else (None, refs)
    outs, (acc_ref, lhs_ref) = refs[:-2], refs[-2:]
    depth = lhs_ref.shape[2]
    for p, piece in enumerate(pieces):
        for k in range(2):
            lhs_ref[k, p * ROWS : (p + 1) * ROWS, :] = piece[k * ROWS : (k + 1) * ROWS, :]
    for a, b in pieces_of(down_ref.shape[1], 2 * TILE):
        part = prev_ref[:, a:b] if has_acc else 0.0
        for k in range(2):
            start = where[0] + first if k == 0 else half - where[0] + first
            rows = pl.ds(pl.multiple_of(start, TILE), depth)
            part += jnp.dot(lhs_ref[k], down_ref[rows, a:b], preferred_element_type=jnp.float32)
        acc_ref[:, a:b] = part
    if last:
        for d, out in enumerate(outs):
            source = pl.multiple_of(place(where[1], d) * ROWS, ROWS)
            out[...] = acc_ref[pl.ds(source, ROWS), :].astype(out.dtype)


def down(where, pieces, down_weight, prev, first, last):
    width = down_weight.shape[1]
    n, depth = len(pieces), pieces[0].shape[1]
    total = n * ROWS
    args = [*pieces, down_weight] + ([] if prev is None else [prev])
    sums = jax.ShapeDtypeStruct((total, width), jnp.float32)
    scratch = [pltpu.VMEM((2, total, depth), jnp.bfloat16)]
    if last:
        scratch = [pltpu.VMEM(sums.shape, sums.dtype)] + scratch
    return pl.pallas_call(
        functools.partial(down_kernel, n, prev is not None, last, first, down_weight.shape[0] // 2),
        in_specs=[spec(pltpu.SMEM)] + [spec(pltpu.VMEM)] * len(args),
        out_specs=[spec(pltpu.VMEM)] * n if last else spec(pltpu.VMEM),
        scratch_shapes=scratch,
        out_shape=[jax.ShapeDtypeStruct((ROWS, width), jnp.bfloat16)] * n if last else sums,
        compiler_params=params(4),
        cost_estimate=pl.CostEstimate(
            flops=4 * total * width * depth, bytes_accessed=4 * width * depth, transcendentals=0
        ),
        name="down",
    )(where, *args)


def split_by_rep(n_wid, tokens, gate_weight, up_weight, down_weight):
    rep, wid = lax.axis_index("rep"), lax.axis_index("wid")
    f32, bf16 = jnp.float32, jnp.bfloat16
    width = gate_weight.shape[1] // 2
    where = jnp.stack([rep * width, wid]).astype(jnp.int32)

    def swap(x, axis, step):
        n = {"rep": 2, "hid": 4, "wid": n_wid}[axis]
        return lax.ppermute(x, axis, [(i, i ^ step) for i in range(n)])

    tiles = width // TILE
    bounds = [tiles * c // CHUNKS * TILE for c in range(CHUNKS + 1)]
    sources = [pltpu.with_memory_space_constraint(w, pltpu.HBM) for w in (gate_weight, up_weight, tokens)]
    weights = [
        fetch(where, sources[: 2 if c else 3], bounds[c], bounds[c + 1] - bounds[c]) for c in range(CHUNKS)
    ]
    own_tokens = weights[0][2]
    down_weight = pltpu.with_memory_space_constraint(down_weight, pltpu.VMEM)

    near = [swap(tokens, "hid", d) for d in (3, 2, 1)] + [own_tokens]
    blocks = near[::-1] + [swap(x, "rep", 1) for x in near[::-1]]

    quarter = 2 * ROWS
    parts, to_chips = [], []

    def send_to_chip(c):
        mine, got = parts[c]
        to_chips.append((mine[:, quarter:].astype(f32) + got[:, quarter:].astype(f32)).astype(bf16))

    behind = [w[-1] for w in weights[1:]]
    for c in range(CHUNKS):
        if c >= 2:
            send_to_chip(c - 2)
            behind = [to_chips[-1]]
        elif c == 1:
            behind = [parts[0][0]]
        mine, theirs = gate_up(where, blocks, *weights[c][:2], behind)
        parts.append((mine, swap(theirs, "wid", 1)))
    while len(to_chips) < CHUNKS:
        send_to_chip(len(to_chips))

    acc = None
    for c in range(CHUNKS):
        mine, got = parts[c]
        from_chip = swap(to_chips[c], "wid", 2)
        summed = mine[:, :quarter].astype(f32) + got[:, :quarter].astype(f32) + from_chip.astype(f32)
        hidden = (jax.nn.silu(summed[0]) * summed[1]).astype(bf16)
        own = jnp.concatenate([hidden[:ROWS], swap(hidden[ROWS:], "rep", 1)], 0)
        other = swap(own, "wid", 2)
        pieces = [own, other, swap(own, "wid", 1), swap(other, "wid", 1)]
        acc = down(where, pieces, down_weight, acc, bounds[c], c == CHUNKS - 1)

    mixed = acc[0].astype(f32)
    for d in (3, 2, 1):
        mixed = mixed + swap(acc[d], "hid", d).astype(f32)
    return mixed.astype(bf16)


def solution(mesh):
    n_rep, n_hid, n_wid = (mesh.shape[a] for a in ("rep", "hid", "wid"))

    def on_device(tokens, gate_weight, up_weight, down_weight):
        fits = (
            (n_rep, n_hid, n_wid) == (2, 4, 4)
            and gate_weight.shape[1] % (n_rep * TILE) == 0
            and tokens.shape[0] == ROWS
        )
        if not fits:
            return plain(tokens, gate_weight, up_weight, down_weight)
        return split_by_rep(n_wid, tokens, gate_weight, up_weight, down_weight)

    return jax.shard_map(
        on_device,
        mesh=mesh,
        in_specs=(P(("rep", "hid"), "wid"), P("wid", "hid"), P("wid", "hid"), P("hid", "wid")),
        out_specs=P(("rep", "hid"), "wid"),
        check_vma=False,
    )
```

```python
import functools

import jax
import jax.numpy as jnp
from jax import lax
from jax.experimental import pallas as pl
from jax.experimental.pallas import tpu as pltpu
from jax.sharding import PartitionSpec as P

TILE = 256
CHUNKS = 3
ROWS = 16


def plain(tokens, gate_weight, up_weight, down_weight):
    piece = lax.all_gather(tokens, "hid", axis=0, tiled=True)
    gate_rows = jnp.dot(piece, gate_weight, preferred_element_type=jnp.float32)
    up_rows = jnp.dot(piece, up_weight, preferred_element_type=jnp.float32)
    partial_terms = jnp.stack([gate_rows, up_rows], 0)
    summed = lax.psum(partial_terms.astype(jnp.bfloat16), "wid").astype(jnp.float32)
    hidden = (jax.nn.silu(summed[0]) * summed[1]).astype(jnp.bfloat16)
    return lax.psum_scatter(
        jnp.dot(hidden, down_weight, preferred_element_type=jnp.float32).astype(jnp.bfloat16),
        "hid",
        scatter_dimension=0,
        tiled=True,
    )


def pieces_of(width, most):
    first = width % most
    edges = ([0] if first else []) + list(range(first, width + 1, most))
    return list(zip(edges[:-1], edges[1:]))


def place(wid, d):
    step = wid ^ d
    return (step % 2) * 2 + step // 2


def spec(space):
    return pl.BlockSpec(memory_space=space)


def params(mib):
    return pltpu.CompilerParams(vmem_limit_bytes=mib * 2**20)


def column_copies(source_ref, start, out_ref, cuts, sems):
    return [
        pltpu.make_async_copy(source_ref.at[:, pl.ds(start + a, b - a)], out_ref.at[:, a:b], sems.at[i])
        for i, (a, b) in enumerate(cuts)
    ]


def fetch_kernel(where, gate_ref, up_ref, tokens_ref, gate_out, up_out, tokens_out, sems):
    start = pl.multiple_of(where[0], TILE)
    copies = [pltpu.make_async_copy(tokens_ref, tokens_out, sems.at[2, 0])]
    for k, (source, out) in enumerate(((gate_ref, gate_out), (up_ref, up_out))):
        copies += column_copies(source, start, out, pieces_of(out.shape[1], 2 * TILE), sems.at[k])
    for copy in copies:
        copy.start()
    for copy in copies:
        copy.wait()


def fetch(where, gate, up, tokens, width):
    depth = gate.shape[0]
    return pl.pallas_call(
        fetch_kernel,
        in_specs=[spec(pltpu.SMEM)] + [spec(pltpu.HBM)] * 3,
        out_specs=[spec(pltpu.VMEM)] * 3,
        out_shape=[pltpu.VMEM(x, jnp.bfloat16) for x in ((depth, width), (depth, width), tokens.shape)],
        scratch_shapes=[pltpu.SemaphoreType.DMA((3, len(pieces_of(width, 2 * TILE))))],
        compiler_params=params(1),
        cost_estimate=pl.CostEstimate(flops=0, bytes_accessed=4 * depth * width, transcendentals=0),
        name="fetch",
    )(where, gate, up, tokens)


def gate_up_kernel(n_blocks, first, streamed, where, *refs):
    blocks, weights = refs[:n_blocks], refs[n_blocks : n_blocks + 2]
    if streamed:
        mine_ref, theirs_ref, x_ref, w_ref, sems = refs[-5:]
    else:
        mine_ref, theirs_ref, x_ref = refs[-3:]
    cuts = pieces_of(mine_ref.shape[2], 2 * TILE)
    if streamed:
        start = pl.multiple_of(where[0] + first, TILE)
        copies = [column_copies(weights[k], start, w_ref.at[k], cuts, sems.at[k]) for k in range(2)]
        for i in range(len(cuts)):
            for k in range(2):
                copies[k][i].start()
    for b in range(n_blocks):
        at = place(where[1], b % 4) * 2 + b // 4
        x_ref[pl.ds(pl.multiple_of(at * ROWS, ROWS), ROWS), :] = blocks[b][...]
    half = x_ref.shape[0] // 2
    for i, (a, b) in enumerate(cuts):
        for k in range(2):
            if streamed:
                copies[k][i].wait()
                weight = w_ref[k, :, a:b]
            else:
                weight = weights[k][:, first + a : first + b]
            part = jnp.dot(x_ref[...], weight, preferred_element_type=jnp.float32).astype(jnp.bfloat16)
            mine_ref[k, :, a:b] = part[:half]
            theirs_ref[k, :, a:b] = part[half:]


def gate_up(where, blocks, gate, up, first, width, streamed, behind):
    depth = gate.shape[0]
    n = len(blocks)
    total = n * ROWS
    scratch = [pltpu.VMEM((total, depth), jnp.bfloat16)]
    if streamed:
        scratch.append(pltpu.VMEM((2, depth, width), jnp.bfloat16))
        scratch.append(pltpu.SemaphoreType.DMA((2, len(pieces_of(width, 2 * TILE)))))
    return pl.pallas_call(
        functools.partial(gate_up_kernel, n, first, streamed),
        in_specs=[spec(pltpu.SMEM)]
        + [spec(pltpu.VMEM)] * n
        + [spec(pltpu.HBM if streamed else pltpu.VMEM)] * 2
        + [spec(pl.ANY)] * len(behind),
        out_specs=[spec(pltpu.VMEM)] * 2,
        scratch_shapes=scratch,
        out_shape=[jax.ShapeDtypeStruct((2, total // 2, width), jnp.bfloat16)] * 2,
        compiler_params=params(16 if streamed else 4),
        cost_estimate=pl.CostEstimate(
            flops=4 * total * depth * width, bytes_accessed=4 * depth * width, transcendentals=0
        ),
        name="gate_up",
    )(where, *blocks, gate, up, *behind)


def join_kernel(*refs):
    out_ref = refs[-1]
    half = out_ref.shape[0] // 2
    out_ref[:half, :] = refs[0][...]
    out_ref[half:, :] = refs[1][...]


def join(own, other, behind):
    rows, width = own.shape
    return pl.pallas_call(
        join_kernel,
        in_specs=[spec(pltpu.VMEM)] * 2 + [spec(pl.ANY)],
        out_specs=spec(pltpu.VMEM),
        out_shape=jax.ShapeDtypeStruct((2 * rows, width), own.dtype),
        compiler_params=params(1),
        cost_estimate=pl.CostEstimate(flops=0, bytes_accessed=8 * rows * width, transcendentals=0),
        name="join",
    )(own, other, behind)


def down_kernel(n_pieces, has_acc, last, first, half, where, *refs):
    pieces, refs = refs[:n_pieces], refs[n_pieces:]
    down_ref, refs = refs[0], refs[1:]
    prev_ref, refs = (refs[0], refs[1:]) if has_acc else (None, refs)
    outs, (acc_ref, lhs_ref) = refs[:-2], refs[-2:]
    depth = lhs_ref.shape[2]
    p = 0
    for piece in pieces:
        for at in range(0, piece.shape[0], 2 * ROWS):
            for k in range(2):
                rows = slice(at + k * ROWS, at + (k + 1) * ROWS)
                lhs_ref[k, p * ROWS : (p + 1) * ROWS, :] = piece[rows, :]
            p += 1
    for a, b in pieces_of(down_ref.shape[1], 2 * TILE):
        part = prev_ref[:, a:b] if has_acc else 0.0
        for k in range(2):
            start = where[0] + first if k == 0 else half - where[0] + first
            rows = pl.ds(pl.multiple_of(start, TILE), depth)
            part += jnp.dot(lhs_ref[k], down_ref[rows, a:b], preferred_element_type=jnp.float32)
        acc_ref[:, a:b] = part
    if last:
        for d, out in enumerate(outs):
            source = pl.multiple_of(place(where[1], d) * ROWS, ROWS)
            out[...] = acc_ref[pl.ds(source, ROWS), :].astype(out.dtype)


def down(where, pieces, down_weight, prev, first, last):
    width = down_weight.shape[1]
    n, depth = len(pieces), pieces[0].shape[1]
    total = sum(p.shape[0] for p in pieces) // 2
    args = [*pieces, down_weight] + ([] if prev is None else [prev])
    sums = jax.ShapeDtypeStruct((total, width), jnp.float32)
    scratch = [pltpu.VMEM((2, total, depth), jnp.bfloat16)]
    if last:
        scratch = [pltpu.VMEM(sums.shape, sums.dtype)] + scratch
    return pl.pallas_call(
        functools.partial(down_kernel, n, prev is not None, last, first, down_weight.shape[0] // 2),
        in_specs=[spec(pltpu.SMEM)] + [spec(pltpu.VMEM)] * len(args),
        out_specs=[spec(pltpu.VMEM)] * 4 if last else spec(pltpu.VMEM),
        scratch_shapes=scratch,
        out_shape=[jax.ShapeDtypeStruct((ROWS, width), jnp.bfloat16)] * 4 if last else sums,
        compiler_params=params(4),
        cost_estimate=pl.CostEstimate(
            flops=4 * total * width * depth, bytes_accessed=4 * width * depth, transcendentals=0
        ),
        name="down",
    )(where, *args)


def split_by_rep(n_wid, tokens, gate_weight, up_weight, down_weight):
    rep, wid = lax.axis_index("rep"), lax.axis_index("wid")
    f32, bf16 = jnp.float32, jnp.bfloat16
    width = gate_weight.shape[1] // 2
    where = jnp.stack([rep * width, wid]).astype(jnp.int32)

    def swap(x, axis, step):
        n = {"rep": 2, "hid": 4, "wid": n_wid}[axis]
        return lax.ppermute(x, axis, [(i, i ^ step) for i in range(n)])

    tiles = width // TILE
    bounds = [tiles * c // CHUNKS * TILE for c in range(CHUNKS + 1)]
    gate_weight, up_weight = (pltpu.with_memory_space_constraint(w, pltpu.HBM) for w in (gate_weight, up_weight))
    hbm_tokens = pltpu.with_memory_space_constraint(tokens, pltpu.HBM)
    *early, own_tokens = fetch(where, gate_weight, up_weight, hbm_tokens, bounds[-2])
    down_weight = pltpu.with_memory_space_constraint(down_weight, pltpu.VMEM)

    near = [swap(tokens, "hid", d) for d in (3, 2, 1)] + [own_tokens]
    blocks = near[::-1] + [swap(x, "rep", 1) for x in near[::-1]]

    quarter = 2 * ROWS
    parts, to_chips = [], []

    def send_to_chip(c):
        mine, got = parts[c]
        to_chips.append((mine[:, quarter:].astype(f32) + got[:, quarter:].astype(f32)).astype(bf16))

    for c in range(CHUNKS):
        while len(to_chips) < c and c == CHUNKS - 1:
            send_to_chip(len(to_chips))
        behind = to_chips[:] if to_chips else [p[0] for p in parts]
        last = c == CHUNKS - 1
        weights = (gate_weight, up_weight) if last else early
        mine, theirs = gate_up(where, blocks, *weights, bounds[c], bounds[c + 1] - bounds[c], last, behind)
        parts.append((mine, swap(theirs, "wid", 1)))
    while len(to_chips) < CHUNKS:
        send_to_chip(len(to_chips))

    acc = None
    for c in range(CHUNKS):
        mine, got = parts[c]
        from_chip = swap(to_chips[c], "wid", 2)
        summed = mine[:, :quarter].astype(f32) + got[:, :quarter].astype(f32) + from_chip.astype(f32)
        hidden = (jax.nn.silu(summed[0]) * summed[1]).astype(bf16)
        own = jnp.concatenate([hidden[:ROWS], swap(hidden[ROWS:], "rep", 1)], 0)
        other = swap(own, "wid", 2)
        if c < CHUNKS - 1:
            pieces = [own, other, swap(own, "wid", 1), swap(other, "wid", 1)]
        else:
            pieces = [own, other, swap(join(own, other, acc), "wid", 1)]
        acc = down(where, pieces, down_weight, acc, bounds[c], c == CHUNKS - 1)

    mixed = acc[0].astype(f32)
    for d in (3, 2, 1):
        mixed = mixed + swap(acc[d], "hid", d).astype(f32)
    return mixed.astype(bf16)


def solution(mesh):
    n_rep, n_hid, n_wid = (mesh.shape[a] for a in ("rep", "hid", "wid"))

    def on_device(tokens, gate_weight, up_weight, down_weight):
        fits = (
            (n_rep, n_hid, n_wid) == (2, 4, 4)
            and gate_weight.shape[1] % (n_rep * TILE) == 0
            and tokens.shape[0] == ROWS
        )
        if not fits:
            return plain(tokens, gate_weight, up_weight, down_weight)
        return split_by_rep(n_wid, tokens, gate_weight, up_weight, down_weight)

    return jax.shard_map(
        on_device,
        mesh=mesh,
        in_specs=(P(("rep", "hid"), "wid"), P("wid", "hid"), P("wid", "hid"), P("hid", "wid")),
        out_specs=P(("rep", "hid"), "wid"),
        check_vma=False,
    )
```

```python
import functools

import jax
import jax.numpy as jnp
from jax import lax
from jax.experimental import pallas as pl
from jax.experimental.pallas import tpu as pltpu
from jax.sharding import PartitionSpec as P

TILE = 256
LAST = 3
ROWS = 16


def plain(tokens, gate_weight, up_weight, down_weight):
    piece = lax.all_gather(tokens, "hid", axis=0, tiled=True)
    gate_rows = jnp.dot(piece, gate_weight, preferred_element_type=jnp.float32)
    up_rows = jnp.dot(piece, up_weight, preferred_element_type=jnp.float32)
    partial_terms = jnp.stack([gate_rows, up_rows], 0)
    summed = lax.psum(partial_terms.astype(jnp.bfloat16), "wid").astype(jnp.float32)
    hidden = (jax.nn.silu(summed[0]) * summed[1]).astype(jnp.bfloat16)
    return lax.psum_scatter(
        jnp.dot(hidden, down_weight, preferred_element_type=jnp.float32).astype(jnp.bfloat16),
        "hid",
        scatter_dimension=0,
        tiled=True,
    )


def pieces_of(width, most):
    first = width % most
    edges = ([0] if first else []) + list(range(first, width + 1, most))
    return list(zip(edges[:-1], edges[1:]))


def place(wid, d):
    step = wid ^ d
    return (step % 2) * 2 + step // 2


def spec(space):
    return pl.BlockSpec(memory_space=space)


def params(mib):
    return pltpu.CompilerParams(vmem_limit_bytes=mib * 2**20)


def column_copies(source_ref, out_ref, segments, sems):
    copies, cuts, at = [], [], 0
    for start, width in segments:
        for a, b in pieces_of(width, 2 * TILE):
            source = source_ref.at[:, pl.ds(pl.multiple_of(start + a, TILE), b - a)]
            copies.append(pltpu.make_async_copy(source, out_ref.at[:, at + a : at + b], sems.at[len(copies)]))
            cuts.append((at + a, at + b))
        at += width
    return copies, cuts


def fetch_kernel(first, where, gate_ref, up_ref, tokens_ref, gate_out, up_out, tokens_out, sems):
    copies = [pltpu.make_async_copy(tokens_ref, tokens_out, sems.at[2, 0])]
    for k, (source, out) in enumerate(((gate_ref, gate_out), (up_ref, up_out))):
        copies += column_copies(source, out, [(where[0] + first, out.shape[1])], sems.at[k])[0]
    for copy in copies:
        copy.start()
    for copy in copies:
        copy.wait()


def fetch(where, gate, up, tokens, first, width):
    depth = gate.shape[0]
    return pl.pallas_call(
        functools.partial(fetch_kernel, first),
        in_specs=[spec(pltpu.SMEM)] + [spec(pltpu.HBM)] * 3,
        out_specs=[spec(pltpu.VMEM)] * 3,
        out_shape=[pltpu.VMEM(x, jnp.bfloat16) for x in ((depth, width), (depth, width), tokens.shape)],
        scratch_shapes=[pltpu.SemaphoreType.DMA((3, len(pieces_of(width, 2 * TILE))))],
        compiler_params=params(1),
        cost_estimate=pl.CostEstimate(flops=0, bytes_accessed=4 * depth * width, transcendentals=0),
        name="fetch",
    )(where, gate, up, tokens)


def join_kernel(n, first, *refs):
    out_ref, at = refs[-1], 0
    for ref in refs[:n]:
        out_ref[at : at + ref.shape[0], :] = ref[:, first : first + out_ref.shape[1]]
        at += ref.shape[0]


def join(arrays, behind, first=0, width=None):
    rows, width = sum(a.shape[0] for a in arrays), width or arrays[0].shape[1]
    return pl.pallas_call(
        functools.partial(join_kernel, len(arrays), first),
        in_specs=[spec(pltpu.VMEM)] * len(arrays) + [spec(pl.ANY)] * len(behind),
        out_specs=spec(pltpu.VMEM),
        out_shape=jax.ShapeDtypeStruct((rows, width), arrays[0].dtype),
        compiler_params=params(1),
        cost_estimate=pl.CostEstimate(flops=0, bytes_accessed=4 * rows * width, transcendentals=0),
        name="join",
    )(*arrays, *behind)


def gate_up_kernel(n_arrays, n_pairs, segments, where, *refs):
    arrays, weights = refs[:n_arrays], refs[n_arrays : n_arrays + 2 * n_pairs]
    if segments:
        mine_ref, theirs_ref, x_ref, w_ref, sems = refs[-5:]
        copies = [column_copies(weights[k], w_ref.at[k], segments, sems.at[k]) for k in range(2)]
        cuts = copies[0][1]
        for i in range(len(cuts)):
            for k in range(2):
                copies[k][0][i].start()
    else:
        mine_ref, theirs_ref, x_ref = refs[-3:]
        step = weights[0].shape[1]
        cuts = [(p * step + a, p * step + b) for p in range(n_pairs) for a, b in pieces_of(step, 2 * TILE)]
    per = x_ref.shape[0] // (4 * ROWS)
    b = 0
    for array in arrays:
        for at in range(0, array.shape[0], ROWS):
            to = (place(where[1], b % 4) * per + b // 4) * ROWS
            x_ref[pl.ds(pl.multiple_of(to, ROWS), ROWS), :] = array[at : at + ROWS, :]
            b += 1
    half = x_ref.shape[0] // 2
    for i, (a, b) in enumerate(cuts):
        for k in range(2):
            if segments:
                copies[k][0][i].wait()
                weight = w_ref[k, :, a:b]
            else:
                p = a // step
                weight = weights[2 * p + k][:, a - p * step : b - p * step]
            part = jnp.dot(x_ref[...], weight, preferred_element_type=jnp.float32).astype(jnp.bfloat16)
            mine_ref[k, :, a:b] = part[:half]
            theirs_ref[k, :, a:b] = part[half:]


def gate_up(where, arrays, weights, segments, behind):
    depth = weights[0].shape[0]
    width = sum(w for _, w in segments) if segments else sum(w.shape[1] for w in weights[::2])
    total = sum(a.shape[0] for a in arrays)
    scratch = [pltpu.VMEM((total, depth), jnp.bfloat16)]
    if segments:
        n_cuts = sum(len(pieces_of(w, 2 * TILE)) for _, w in segments)
        scratch.append(pltpu.VMEM((2, depth, width), jnp.bfloat16))
        scratch.append(pltpu.SemaphoreType.DMA((2, n_cuts)))
    return pl.pallas_call(
        functools.partial(gate_up_kernel, len(arrays), len(weights) // 2, segments),
        in_specs=[spec(pltpu.SMEM)]
        + [spec(pltpu.VMEM)] * len(arrays)
        + [spec(pltpu.HBM if segments else pltpu.VMEM)] * len(weights)
        + [spec(pl.ANY)] * len(behind),
        out_specs=[spec(pltpu.VMEM)] * 2,
        scratch_shapes=scratch,
        out_shape=[jax.ShapeDtypeStruct((2, total // 2, width), jnp.bfloat16)] * 2,
        compiler_params=params(16 if segments else 4),
        cost_estimate=pl.CostEstimate(
            flops=4 * total * depth * width, bytes_accessed=4 * depth * width, transcendentals=0
        ),
        name="gate_up",
    )(where, *arrays, *weights, *behind)


def combine_kernel(n_outs, mine_ref, got_ref, chip_ref, *refs):
    outs = refs[-n_outs:]
    rows = chip_ref.shape[1]
    for a, b in pieces_of(chip_ref.shape[2], TILE):
        gate, up = (
            mine_ref[k, :rows, a:b].astype(jnp.float32)
            + got_ref[k, :rows, a:b].astype(jnp.float32)
            + chip_ref[k, :, a:b].astype(jnp.float32)
            for k in range(2)
        )
        hidden = (gate / (1 + jnp.exp(-gate)) * up).astype(jnp.bfloat16)
        for i, out in enumerate(outs):
            out[:, a:b] = hidden[i * ROWS : (i + 1) * ROWS]


def combine(mine, got, from_chip, behind):
    _, rows, width = from_chip.shape
    n_outs = rows // ROWS
    return pl.pallas_call(
        functools.partial(combine_kernel, n_outs),
        in_specs=[spec(pltpu.VMEM)] * 3 + [spec(pl.ANY)] * len(behind),
        out_specs=[spec(pltpu.VMEM)] * n_outs,
        out_shape=[jax.ShapeDtypeStruct((ROWS, width), jnp.bfloat16)] * n_outs,
        compiler_params=params(1),
        cost_estimate=pl.CostEstimate(
            flops=10 * rows * width, bytes_accessed=14 * rows * width, transcendentals=rows * width
        ),
        name="combine",
    )(mine, got, from_chip, *behind)


def down_kernel(n_pieces, has_acc, last, first, half, where, *refs):
    pieces, refs = refs[:n_pieces], refs[n_pieces:]
    down_ref, refs = refs[0], refs[1:]
    prev_ref, refs = (refs[0], refs[1:]) if has_acc else (None, refs)
    outs, (acc_ref, lhs_ref) = refs[:-2], refs[-2:]
    depth = lhs_ref.shape[2]
    p = 0
    for piece in pieces:
        for at in range(0, piece.shape[0], ROWS if last else 2 * ROWS):
            for k in range(2):
                if last:
                    block = piece[at : at + ROWS, k * depth : (k + 1) * depth]
                else:
                    block = piece[at + k * ROWS : at + (k + 1) * ROWS, :]
                lhs_ref[k, p * ROWS : (p + 1) * ROWS, :] = block
            p += 1
    if last:
        starts = [first, half + first]
    else:
        starts = [where[0] + first, half - where[0] + first]
    for a, b in pieces_of(down_ref.shape[1], 2 * TILE):
        part = prev_ref[:, a:b] if has_acc else 0.0
        for k in range(2):
            rows = pl.ds(pl.multiple_of(starts[k], TILE), depth)
            part += jnp.dot(lhs_ref[k], down_ref[rows, a:b], preferred_element_type=jnp.float32)
        acc_ref[:, a:b] = part
    if last:
        for d, out in enumerate(outs):
            source = pl.multiple_of(place(where[1], d) * ROWS, ROWS)
            out[...] = acc_ref[pl.ds(source, ROWS), :].astype(out.dtype)


def down(where, pieces, down_weight, prev, first, depth, last):
    width = down_weight.shape[1]
    total = 4 * ROWS
    args = [*pieces, down_weight] + ([] if prev is None else [prev])
    sums = jax.ShapeDtypeStruct((total, width), jnp.float32)
    scratch = [pltpu.VMEM((2, total, depth), jnp.bfloat16)]
    if last:
        scratch = [pltpu.VMEM(sums.shape, sums.dtype)] + scratch
    return pl.pallas_call(
        functools.partial(
            down_kernel, len(pieces), prev is not None, last, first, down_weight.shape[0] // 2
        ),
        in_specs=[spec(pltpu.SMEM)] + [spec(pltpu.VMEM)] * len(args),
        out_specs=[spec(pltpu.VMEM)] * 4 if last else spec(pltpu.VMEM),
        scratch_shapes=scratch,
        out_shape=[jax.ShapeDtypeStruct((ROWS, width), jnp.bfloat16)] * 4 if last else sums,
        compiler_params=params(4),
        cost_estimate=pl.CostEstimate(
            flops=4 * total * width * depth, bytes_accessed=4 * width * depth, transcendentals=0
        ),
        name="down",
    )(where, *args)


def split_by_rep(tokens, gate_weight, up_weight, down_weight):
    rep, wid = lax.axis_index("rep"), lax.axis_index("wid")
    f32, bf16 = jnp.float32, jnp.bfloat16
    half = gate_weight.shape[1] // 2
    where = jnp.stack([rep * half, wid]).astype(jnp.int32)

    def swap(x, axis, step):
        n = {"rep": 2, "hid": 4, "wid": 4}[axis]
        return lax.ppermute(x, axis, [(i, i ^ step) for i in range(n)])

    tiles = half // TILE
    bounds = [0, (tiles - LAST) // 2 * TILE, (tiles - LAST) * TILE, half]
    widths = [b - a for a, b in zip(bounds[:-1], bounds[1:])]
    gate_weight, up_weight, hbm_tokens = (
        pltpu.with_memory_space_constraint(w, pltpu.HBM) for w in (gate_weight, up_weight, tokens)
    )
    down_weight = pltpu.with_memory_space_constraint(down_weight, pltpu.VMEM)

    far_own = swap(tokens, "rep", 1)
    by_hid = [swap(tokens, "hid", d) for d in (3, 2, 1)][::-1]
    early = [fetch(where, gate_weight, up_weight, hbm_tokens, bounds[c], widths[c]) for c in range(2)]
    own = early[0][2]
    near = join(by_hid, [own, far_own])
    far = swap(near, "rep", 1)

    def reduce_pair(mine, theirs):
        got = swap(theirs, "wid", 1)
        rows = mine.shape[1] // 2
        return mine, got, (mine[:, rows:].astype(f32) + got[:, rows:].astype(f32)).astype(bf16)

    weights = [w for fetched in early for w in fetched[:2]]
    *parts, to_chip = reduce_pair(*gate_up(where, [own, near, far_own, far], weights, [], []))
    from_chip = swap(to_chip, "wid", 2)
    segments = [(bounds[2], widths[2]), (half + bounds[2], widths[2])]
    *last_parts, last_to_chip = reduce_pair(
        *gate_up(where, [own, near], [gate_weight, up_weight], segments, [to_chip])
    )
    last_from_chip = swap(last_to_chip, "wid", 2)

    keep, give = combine(*parts, from_chip, [last_to_chip])
    got = swap(give, "rep", 1)
    acc = None
    for c in range(2):
        mixed = join([keep, got], [], bounds[c], widths[c])
        other = swap(mixed, "wid", 2)
        pieces = [mixed, other, swap(mixed, "wid", 1), swap(other, "wid", 1)]
        acc = down(where, pieces, down_weight, acc, bounds[c], widths[c], False)
        if c == 0:
            first_sum = acc
    (mixed,) = combine(*last_parts, last_from_chip, [])
    other = swap(mixed, "wid", 2)
    pieces = [mixed, other, swap(join([mixed, other], [first_sum]), "wid", 1)]
    acc = down(where, pieces, down_weight, acc, bounds[2], widths[2], True)

    mixed = acc[0].astype(f32)
    for d in (3, 2, 1):
        mixed = mixed + swap(acc[d], "hid", d).astype(f32)
    return mixed.astype(bf16)


def solution(mesh):
    n_rep, n_hid, n_wid = (mesh.shape[a] for a in ("rep", "hid", "wid"))

    def on_device(tokens, gate_weight, up_weight, down_weight):
        fits = (
            (n_rep, n_hid, n_wid) == (2, 4, 4)
            and gate_weight.shape[1] % (n_rep * TILE) == 0
            and tokens.shape[0] == ROWS
        )
        if not fits:
            return plain(tokens, gate_weight, up_weight, down_weight)
        return split_by_rep(tokens, gate_weight, up_weight, down_weight)

    return jax.shard_map(
        on_device,
        mesh=mesh,
        in_specs=(P(("rep", "hid"), "wid"), P("wid", "hid"), P("wid", "hid"), P("hid", "wid")),
        out_specs=P(("rep", "hid"), "wid"),
        check_vma=False,
    )
```

```python
import functools

import jax
import jax.numpy as jnp
from jax import lax
from jax.experimental import pallas as pl
from jax.experimental.pallas import tpu as pltpu
from jax.sharding import PartitionSpec as P

TILE = 256
LAST = 3
ROWS = 16
COST = pl.CostEstimate(flops=0, bytes_accessed=1024, transcendentals=0)


def plain(tokens, gate_weight, up_weight, down_weight):
    piece = lax.all_gather(tokens, "hid", axis=0, tiled=True)
    gate_rows = jnp.dot(piece, gate_weight, preferred_element_type=jnp.float32)
    up_rows = jnp.dot(piece, up_weight, preferred_element_type=jnp.float32)
    partial_terms = jnp.stack([gate_rows, up_rows], 0)
    summed = lax.psum(partial_terms.astype(jnp.bfloat16), "wid").astype(jnp.float32)
    hidden = (jax.nn.silu(summed[0]) * summed[1]).astype(jnp.bfloat16)
    return lax.psum_scatter(
        jnp.dot(hidden, down_weight, preferred_element_type=jnp.float32).astype(jnp.bfloat16),
        "hid",
        scatter_dimension=0,
        tiled=True,
    )


def pieces_of(width, most):
    first = width % most
    edges = ([0] if first else []) + list(range(first, width + 1, most))
    return list(zip(edges[:-1], edges[1:]))


def place(wid, d):
    step = wid ^ d
    return (step % 2) * 2 + step // 2


def spec(space):
    return pl.BlockSpec(memory_space=space)


def params(mib):
    return pltpu.CompilerParams(vmem_limit_bytes=mib * 2**20)


def column_copies(source_ref, out_ref, segments, sems):
    copies, cuts, at = [], [], 0
    for start, width in segments:
        for a, b in pieces_of(width, 2 * TILE):
            source = source_ref.at[:, pl.ds(pl.multiple_of(start + a, TILE), b - a)]
            copies.append(pltpu.make_async_copy(source, out_ref.at[:, at + a : at + b], sems.at[len(copies)]))
            cuts.append((at + a, at + b))
        at += width
    return copies, cuts


def fetch_kernel(first, where, gate_ref, up_ref, tokens_ref, gate_out, up_out, tokens_out, sems):
    copies = [pltpu.make_async_copy(tokens_ref, tokens_out, sems.at[2, 0])]
    for k, (source, out) in enumerate(((gate_ref, gate_out), (up_ref, up_out))):
        copies += column_copies(source, out, [(where[0] + first, out.shape[1])], sems.at[k])[0]
    for copy in copies:
        copy.start()
    for copy in copies:
        copy.wait()


def fetch(where, gate, up, tokens, first, width):
    depth = gate.shape[0]
    return pl.pallas_call(
        functools.partial(fetch_kernel, first),
        in_specs=[spec(pltpu.SMEM)] + [spec(pltpu.HBM)] * 3,
        out_specs=[spec(pltpu.VMEM)] * 3,
        out_shape=[pltpu.VMEM(x, jnp.bfloat16) for x in ((depth, width), (depth, width), tokens.shape)],
        scratch_shapes=[pltpu.SemaphoreType.DMA((3, len(pieces_of(width, 2 * TILE))))],
        compiler_params=params(1),
        cost_estimate=COST,
        name="fetch",
    )(where, gate, up, tokens)


def join_kernel(n, first, *refs):
    out_ref, at = refs[-1], 0
    for ref in refs[:n]:
        out_ref[at : at + ref.shape[0], :] = ref[:, first : first + out_ref.shape[1]]
        at += ref.shape[0]


def join(arrays, behind, first=0, width=None):
    rows, width = sum(a.shape[0] for a in arrays), width or arrays[0].shape[1]
    return pl.pallas_call(
        functools.partial(join_kernel, len(arrays), first),
        in_specs=[spec(pltpu.VMEM)] * len(arrays) + [spec(pl.ANY)] * len(behind),
        out_specs=spec(pltpu.VMEM),
        out_shape=jax.ShapeDtypeStruct((rows, width), arrays[0].dtype),
        compiler_params=params(1),
        cost_estimate=COST,
        name="join",
    )(*arrays, *behind)


def gate_up_kernel(n_arrays, n_pairs, segments, where, *refs):
    arrays, weights = refs[:n_arrays], refs[n_arrays : n_arrays + 2 * n_pairs]
    if segments:
        mine_ref, theirs_ref, x_ref, w_ref, sems = refs[-5:]
        copies = [column_copies(weights[k], w_ref.at[k], segments, sems.at[k]) for k in range(2)]
        cuts = copies[0][1]
        for i in range(len(cuts)):
            for k in range(2):
                copies[k][0][i].start()
    else:
        mine_ref, theirs_ref, x_ref = refs[-3:]
        step = weights[0].shape[1]
        cuts = [(p * step + a, p * step + b) for p in range(n_pairs) for a, b in pieces_of(step, 2 * TILE)]
    per = x_ref.shape[0] // (4 * ROWS)
    b = 0
    for array in arrays:
        for at in range(0, array.shape[0], ROWS):
            to = (place(where[1], b % 4) * per + b // 4) * ROWS
            x_ref[pl.ds(pl.multiple_of(to, ROWS), ROWS), :] = array[at : at + ROWS, :]
            b += 1
    half = x_ref.shape[0] // 2
    for i, (a, b) in enumerate(cuts):
        for k in range(2):
            if segments:
                copies[k][0][i].wait()
                weight = w_ref[k, :, a:b]
            else:
                p = a // step
                weight = weights[2 * p + k][:, a - p * step : b - p * step]
            part = jnp.dot(x_ref[...], weight, preferred_element_type=jnp.float32).astype(jnp.bfloat16)
            mine_ref[k, :, a:b] = part[:half]
            theirs_ref[k, :, a:b] = part[half:]


def gate_up(where, arrays, weights, segments, behind):
    depth = weights[0].shape[0]
    width = sum(w for _, w in segments) if segments else sum(w.shape[1] for w in weights[::2])
    total = sum(a.shape[0] for a in arrays)
    scratch = [pltpu.VMEM((total, depth), jnp.bfloat16)]
    if segments:
        n_cuts = sum(len(pieces_of(w, 2 * TILE)) for _, w in segments)
        scratch.append(pltpu.VMEM((2, depth, width), jnp.bfloat16))
        scratch.append(pltpu.SemaphoreType.DMA((2, n_cuts)))
    return pl.pallas_call(
        functools.partial(gate_up_kernel, len(arrays), len(weights) // 2, segments),
        in_specs=[spec(pltpu.SMEM)]
        + [spec(pltpu.VMEM)] * len(arrays)
        + [spec(pltpu.HBM if segments else pltpu.VMEM)] * len(weights)
        + [spec(pl.ANY)] * len(behind),
        out_specs=[spec(pltpu.VMEM)] * 2,
        scratch_shapes=scratch,
        out_shape=[jax.ShapeDtypeStruct((2, total // 2, width), jnp.bfloat16)] * 2,
        compiler_params=params(16 if segments else 4),
        cost_estimate=COST,
        name="gate_up",
    )(where, *arrays, *weights, *behind)


def pair_sum_kernel(mine_ref, got_ref, *refs):
    out_ref = refs[-1]
    rows = out_ref.shape[1]
    for k in range(2):
        total = mine_ref[k, rows:].astype(jnp.float32) + got_ref[k, rows:].astype(jnp.float32)
        out_ref[k] = total.astype(out_ref.dtype)


def pair_sum(mine, got, behind):
    _, rows, width = mine.shape
    return pl.pallas_call(
        pair_sum_kernel,
        in_specs=[spec(pltpu.VMEM)] * 2 + [spec(pl.ANY)] * len(behind),
        out_specs=spec(pltpu.VMEM),
        out_shape=jax.ShapeDtypeStruct((2, rows // 2, width), mine.dtype),
        compiler_params=params(2),
        cost_estimate=COST,
        name="pair_sum",
    )(mine, got, *behind)


def mark_kernel(_, out_ref):
    out_ref[...] = jnp.zeros_like(out_ref)


def mark(array):
    return pl.pallas_call(
        mark_kernel,
        in_specs=[spec(pl.ANY)],
        out_specs=spec(pltpu.VMEM),
        out_shape=jax.ShapeDtypeStruct((8, 128), jnp.float32),
        compiler_params=params(1),
        cost_estimate=COST,
        name="mark",
    )(array)


def combine_kernel(n_left, n_outs, mine_ref, got_ref, chip_ref, *refs):
    outs = refs[-n_outs:]
    rows, first = chip_ref.shape[1], 0
    for left in refs[:n_left]:
        first = left.shape[1]
        outs[0][:, :first] = left[...]
    for a, b in pieces_of(chip_ref.shape[2], TILE):
        gate, up = (
            mine_ref[k, :rows, a:b].astype(jnp.float32)
            + got_ref[k, :rows, a:b].astype(jnp.float32)
            + chip_ref[k, :, a:b].astype(jnp.float32)
            for k in range(2)
        )
        hidden = (gate / (1 + jnp.exp(-gate)) * up).astype(jnp.bfloat16)
        for i, out in enumerate(outs):
            out[:, first + a : first + b] = hidden[i * ROWS : (i + 1) * ROWS]


def combine(mine, got, from_chip, left, behind):
    _, rows, width = from_chip.shape
    n_outs = rows // ROWS
    width += sum(x.shape[1] for x in left)
    return pl.pallas_call(
        functools.partial(combine_kernel, len(left), n_outs),
        in_specs=[spec(pltpu.VMEM)] * (3 + len(left)) + [spec(pl.ANY)] * len(behind),
        out_specs=[spec(pltpu.VMEM)] * n_outs,
        out_shape=[jax.ShapeDtypeStruct((ROWS, width), jnp.bfloat16)] * n_outs,
        compiler_params=params(2),
        cost_estimate=COST,
        name="combine",
    )(mine, got, from_chip, *left, *behind)


def down_kernel(n_pieces, has_acc, last, segments, where, *refs):
    pieces, refs = refs[:n_pieces], refs[n_pieces:]
    down_ref, refs = refs[0], refs[1:]
    prev_ref, refs = (refs[0], refs[1:]) if has_acc else (None, refs)
    outs, (acc_ref, lhs_ref) = refs[:-2], refs[-2:]
    at = 0
    for piece in pieces:
        lhs_ref[at : at + piece.shape[0], :] = piece[...]
        at += piece.shape[0]
    for a, b in pieces_of(down_ref.shape[1], 2 * TILE):
        part = prev_ref[:, a:b] if has_acc else 0.0
        at = 0
        for sign, start, depth in segments:
            rows = pl.ds(pl.multiple_of(sign * where[0] + start, TILE) if sign else start, depth)
            part += jnp.dot(lhs_ref[:, at : at + depth], down_ref[rows, a:b], preferred_element_type=jnp.float32)
            at += depth
        acc_ref[:, a:b] = part
    if last:
        for d, out in enumerate(outs):
            source = pl.multiple_of(place(where[1], d) * ROWS, ROWS)
            out[...] = acc_ref[pl.ds(source, ROWS), :].astype(out.dtype)


def down(where, pieces, down_weight, prev, segments, last):
    width = down_weight.shape[1]
    total = 4 * ROWS
    args = [*pieces, down_weight] + ([] if prev is None else [prev])
    sums = jax.ShapeDtypeStruct((total, width), jnp.float32)
    scratch = [pltpu.VMEM((total, pieces[0].shape[1]), jnp.bfloat16)]
    if last:
        scratch = [pltpu.VMEM(sums.shape, sums.dtype)] + scratch
    return pl.pallas_call(
        functools.partial(down_kernel, len(pieces), prev is not None, last, segments),
        in_specs=[spec(pltpu.SMEM)] + [spec(pltpu.VMEM)] * len(args),
        out_specs=[spec(pltpu.VMEM)] * 4 if last else spec(pltpu.VMEM),
        scratch_shapes=scratch,
        out_shape=[jax.ShapeDtypeStruct((ROWS, width), jnp.bfloat16)] * 4 if last else sums,
        compiler_params=params(4),
        cost_estimate=COST,
        name="down",
    )(where, *args)


def split_by_rep(tokens, gate_weight, up_weight, down_weight):
    rep, wid = lax.axis_index("rep"), lax.axis_index("wid")
    f32, bf16 = jnp.float32, jnp.bfloat16
    half = gate_weight.shape[1] // 2
    where = jnp.stack([rep * half, wid]).astype(jnp.int32)

    def swap(x, axis, step):
        n = {"rep": 2, "hid": 4, "wid": 4}[axis]
        return lax.ppermute(x, axis, [(i, i ^ step) for i in range(n)])

    tiles = half // TILE
    bounds = [0, (tiles - LAST) // 2 * TILE, (tiles - LAST) * TILE, half]
    widths = [b - a for a, b in zip(bounds[:-1], bounds[1:])]
    gate_weight, up_weight, hbm_tokens = (
        pltpu.with_memory_space_constraint(w, pltpu.HBM) for w in (gate_weight, up_weight, tokens)
    )
    down_weight = pltpu.with_memory_space_constraint(down_weight, pltpu.VMEM)

    far_own = swap(tokens, "rep", 1)
    by_hid = [swap(tokens, "hid", d) for d in (3, 2, 1)][::-1]
    early = [fetch(where, gate_weight, up_weight, hbm_tokens, bounds[c], widths[c]) for c in range(2)]
    own = early[0][2]
    near = join(by_hid, [own, far_own])
    far = swap(near, "rep", 1)

    weights = [w for fetched in early for w in fetched[:2]]
    mine, theirs = gate_up(where, [own, near, far_own, far], weights, [], [])
    got = swap(theirs, "wid", 1)
    to_chip = pair_sum(mine, got, [])
    from_chip = swap(to_chip, "wid", 2)
    segments = [(bounds[2], widths[2]), (half + bounds[2], widths[2])]
    last_mine, theirs = gate_up(where, [own, near], [gate_weight, up_weight], segments, [to_chip])
    last_got = swap(theirs, "wid", 1)
    last_to_chip = pair_sum(last_mine, last_got, [mark(from_chip)])
    last_from_chip = swap(last_to_chip, "wid", 2)

    keep, give = combine(mine, got, from_chip, [], [])
    far_columns = swap(give, "rep", 1)
    (rest,) = combine(last_mine, last_got, last_from_chip, [far_columns], [])
    rest_segments = [(-1, half, bounds[2])] + [(0, start, width) for start, width in segments]
    acc, behind = None, []
    for hidden, parts in ((keep, [(1, 0, bounds[2])]), (rest, rest_segments)):
        other = swap(hidden, "wid", 2)
        crossed = swap(join([hidden, other], behind), "wid", 1)
        acc = down(where, [hidden, other, crossed], down_weight, acc, parts, bool(behind))
        behind = [acc]

    mixed = acc[0].astype(f32)
    for d in (3, 2, 1):
        mixed = mixed + swap(acc[d], "hid", d).astype(f32)
    return mixed.astype(bf16)


def solution(mesh):
    n_rep, n_hid, n_wid = (mesh.shape[a] for a in ("rep", "hid", "wid"))

    def on_device(tokens, gate_weight, up_weight, down_weight):
        fits = (
            (n_rep, n_hid, n_wid) == (2, 4, 4)
            and gate_weight.shape[1] % (n_rep * TILE) == 0
            and tokens.shape[0] == ROWS
        )
        if not fits:
            return plain(tokens, gate_weight, up_weight, down_weight)
        return split_by_rep(tokens, gate_weight, up_weight, down_weight)

    return jax.shard_map(
        on_device,
        mesh=mesh,
        in_specs=(P(("rep", "hid"), "wid"), P("wid", "hid"), P("wid", "hid"), P("hid", "wid")),
        out_specs=P(("rep", "hid"), "wid"),
        check_vma=False,
    )
```

```python
import functools

import jax
import jax.numpy as jnp
from jax import lax
from jax.experimental import pallas as pl
from jax.experimental.pallas import tpu as pltpu
from jax.sharding import PartitionSpec as P

TILE = 256
LAST = 3
ROWS = 16
COST = pl.CostEstimate(flops=0, bytes_accessed=1024, transcendentals=0)


def plain(tokens, gate_weight, up_weight, down_weight):
    piece = lax.all_gather(tokens, "hid", axis=0, tiled=True)
    gate_rows = jnp.dot(piece, gate_weight, preferred_element_type=jnp.float32)
    up_rows = jnp.dot(piece, up_weight, preferred_element_type=jnp.float32)
    partial_terms = jnp.stack([gate_rows, up_rows], 0)
    summed = lax.psum(partial_terms.astype(jnp.bfloat16), "wid").astype(jnp.float32)
    hidden = (jax.nn.silu(summed[0]) * summed[1]).astype(jnp.bfloat16)
    return lax.psum_scatter(
        jnp.dot(hidden, down_weight, preferred_element_type=jnp.float32).astype(jnp.bfloat16),
        "hid",
        scatter_dimension=0,
        tiled=True,
    )


def pieces_of(width, most):
    first = width % most
    edges = ([0] if first else []) + list(range(first, width + 1, most))
    return list(zip(edges[:-1], edges[1:]))


def place(wid, d):
    step = wid ^ d
    return (step % 2) * 2 + step // 2


def spec(space):
    return pl.BlockSpec(memory_space=space)


def params(mib):
    return pltpu.CompilerParams(vmem_limit_bytes=mib * 2**20)


def column_copies(source_ref, out_ref, segments, sems):
    copies, cuts, at = [], [], 0
    for start, width in segments:
        for a, b in pieces_of(width, 2 * TILE):
            source = source_ref.at[:, pl.ds(pl.multiple_of(start + a, TILE), b - a)]
            copies.append(pltpu.make_async_copy(source, out_ref.at[:, at + a : at + b], sems.at[len(copies)]))
            cuts.append((at + a, at + b))
        at += width
    return copies, cuts


def fetch_kernel(first, where, gate_ref, up_ref, tokens_ref, gate_out, up_out, tokens_out, sems):
    copies = [pltpu.make_async_copy(tokens_ref, tokens_out, sems.at[2, 0])]
    for k, (source, out) in enumerate(((gate_ref, gate_out), (up_ref, up_out))):
        copies += column_copies(source, out, [(where[0] + first, out.shape[1])], sems.at[k])[0]
    for copy in copies:
        copy.start()
    for copy in copies:
        copy.wait()


def fetch(where, gate, up, tokens, first, width):
    depth = gate.shape[0]
    return pl.pallas_call(
        functools.partial(fetch_kernel, first),
        in_specs=[spec(pltpu.SMEM)] + [spec(pltpu.HBM)] * 3,
        out_specs=[spec(pltpu.VMEM)] * 3,
        out_shape=[pltpu.VMEM(x, jnp.bfloat16) for x in ((depth, width), (depth, width), tokens.shape)],
        scratch_shapes=[pltpu.SemaphoreType.DMA((3, len(pieces_of(width, 2 * TILE))))],
        compiler_params=params(1),
        cost_estimate=COST,
        name="fetch",
    )(where, gate, up, tokens)


def join_kernel(n, first, *refs):
    out_ref, at = refs[-1], 0
    for ref in refs[:n]:
        out_ref[at : at + ref.shape[0], :] = ref[:, first : first + out_ref.shape[1]]
        at += ref.shape[0]


def join(arrays, behind, first=0, width=None):
    rows, width = sum(a.shape[0] for a in arrays), width or arrays[0].shape[1]
    return pl.pallas_call(
        functools.partial(join_kernel, len(arrays), first),
        in_specs=[spec(pltpu.VMEM)] * len(arrays) + [spec(pl.ANY)] * len(behind),
        out_specs=spec(pltpu.VMEM),
        out_shape=jax.ShapeDtypeStruct((rows, width), arrays[0].dtype),
        compiler_params=params(1),
        cost_estimate=COST,
        name="join",
    )(*arrays, *behind)


def gate_up_kernel(n_arrays, n_pairs, segments, where, *refs):
    arrays, weights = refs[:n_arrays], refs[n_arrays : n_arrays + 2 * n_pairs]
    if segments:
        mine_ref, theirs_ref, x_ref, w_ref, sems = refs[-5:]
        copies = [column_copies(weights[k], w_ref.at[k], segments, sems.at[k]) for k in range(2)]
        cuts = copies[0][1]
        for i in range(len(cuts)):
            for k in range(2):
                copies[k][0][i].start()
    else:
        mine_ref, theirs_ref, x_ref = refs[-3:]
        step = weights[0].shape[1]
        cuts = [(p * step + a, p * step + b) for p in range(n_pairs) for a, b in pieces_of(step, 2 * TILE)]
    per = x_ref.shape[0] // (4 * ROWS)
    b = 0
    for array in arrays:
        for at in range(0, array.shape[0], ROWS):
            to = (place(where[1], b % 4) * per + b // 4) * ROWS
            x_ref[pl.ds(pl.multiple_of(to, ROWS), ROWS), :] = array[at : at + ROWS, :]
            b += 1
    half = x_ref.shape[0] // 2
    for i, (a, b) in enumerate(cuts):
        for k in range(2):
            if segments:
                copies[k][0][i].wait()
                weight = w_ref[k, :, a:b]
            else:
                p = a // step
                weight = weights[2 * p + k][:, a - p * step : b - p * step]
            part = jnp.dot(x_ref[...], weight, preferred_element_type=jnp.float32).astype(jnp.bfloat16)
            mine_ref[k, :, a:b] = part[:half]
            theirs_ref[k, :, a:b] = part[half:]


def gate_up(where, arrays, weights, segments, behind):
    depth = weights[0].shape[0]
    width = sum(w for _, w in segments) if segments else sum(w.shape[1] for w in weights[::2])
    total = sum(a.shape[0] for a in arrays)
    scratch = [pltpu.VMEM((total, depth), jnp.bfloat16)]
    if segments:
        n_cuts = sum(len(pieces_of(w, 2 * TILE)) for _, w in segments)
        scratch.append(pltpu.VMEM((2, depth, width), jnp.bfloat16))
        scratch.append(pltpu.SemaphoreType.DMA((2, n_cuts)))
    return pl.pallas_call(
        functools.partial(gate_up_kernel, len(arrays), len(weights) // 2, segments),
        in_specs=[spec(pltpu.SMEM)]
        + [spec(pltpu.VMEM)] * len(arrays)
        + [spec(pltpu.HBM if segments else pltpu.VMEM)] * len(weights)
        + [spec(pl.ANY)] * len(behind),
        out_specs=[spec(pltpu.VMEM)] * 2,
        scratch_shapes=scratch,
        out_shape=[jax.ShapeDtypeStruct((2, total // 2, width), jnp.bfloat16)] * 2,
        compiler_params=params(16 if segments else 4),
        cost_estimate=COST,
        name="gate_up",
    )(where, *arrays, *weights, *behind)


def pair_sum_kernel(mine_ref, got_ref, *refs):
    out_ref = refs[-1]
    rows = out_ref.shape[1]
    for k in range(2):
        total = mine_ref[k, rows:].astype(jnp.float32) + got_ref[k, rows:].astype(jnp.float32)
        out_ref[k] = total.astype(out_ref.dtype)


def pair_sum(mine, got, behind):
    _, rows, width = mine.shape
    return pl.pallas_call(
        pair_sum_kernel,
        in_specs=[spec(pltpu.VMEM)] * 2 + [spec(pl.ANY)] * len(behind),
        out_specs=spec(pltpu.VMEM),
        out_shape=jax.ShapeDtypeStruct((2, rows // 2, width), mine.dtype),
        compiler_params=params(2),
        cost_estimate=COST,
        name="pair_sum",
    )(mine, got, *behind)


def later_kernel(array_ref, *refs):
    refs[-1][...] = array_ref[...]


def later(array, behind):
    return pl.pallas_call(
        later_kernel,
        in_specs=[spec(pltpu.VMEM)] + [spec(pl.ANY)] * len(behind),
        out_specs=spec(pltpu.VMEM),
        out_shape=jax.ShapeDtypeStruct(array.shape, array.dtype),
        compiler_params=params(1),
        cost_estimate=COST,
        name="later",
    )(array, *behind)


def combine_kernel(n_left, n_sums, n_outs, *refs):
    lefts, refs, outs = refs[:n_left], refs[n_left:], refs[-n_outs:]
    first = 0
    for left in lefts:
        outs[0][:, first : first + left.shape[1]] = left[...]
        first += left.shape[1]
    for i in range(n_sums):
        mine_ref, got_ref, chip_ref = refs[3 * i : 3 * i + 3]
        _, rows, width = chip_ref.shape
        for a, b in pieces_of(width, TILE):
            gate, up = (
                mine_ref[k, :rows, a:b].astype(jnp.float32)
                + got_ref[k, :rows, a:b].astype(jnp.float32)
                + chip_ref[k, :, a:b].astype(jnp.float32)
                for k in range(2)
            )
            hidden = (gate / (1 + jnp.exp(-gate)) * up).astype(jnp.bfloat16)
            for j, out in enumerate(outs):
                out[:, first + a : first + b] = hidden[j * ROWS : (j + 1) * ROWS]
        first += width


def combine(sums, left, behind):
    n_outs = sums[0][2].shape[1] // ROWS
    width = sum(x.shape[1] for x in left) + sum(chip.shape[2] for _, _, chip in sums)
    args = [*left, *(x for triple in sums for x in triple)]
    return pl.pallas_call(
        functools.partial(combine_kernel, len(left), len(sums), n_outs),
        in_specs=[spec(pltpu.VMEM)] * len(args) + [spec(pl.ANY)] * len(behind),
        out_specs=[spec(pltpu.VMEM)] * n_outs,
        out_shape=[jax.ShapeDtypeStruct((ROWS, width), jnp.bfloat16)] * n_outs,
        compiler_params=params(2),
        cost_estimate=COST,
        name="combine",
    )(*args, *behind)


def down_kernel(n_pieces, has_acc, last, segments, where, *refs):
    pieces, refs = refs[:n_pieces], refs[n_pieces:]
    down_ref, refs = refs[0], refs[1:]
    prev_ref, refs = (refs[0], refs[1:]) if has_acc else (None, refs)
    outs, (acc_ref, lhs_ref) = refs[:-2], refs[-2:]
    at = 0
    for piece in pieces:
        lhs_ref[at : at + piece.shape[0], :] = piece[...]
        at += piece.shape[0]
    for a, b in pieces_of(down_ref.shape[1], 2 * TILE):
        part = prev_ref[:, a:b] if has_acc else 0.0
        at = 0
        for sign, start, depth in segments:
            rows = pl.ds(pl.multiple_of(sign * where[0] + start, TILE) if sign else start, depth)
            part += jnp.dot(lhs_ref[:, at : at + depth], down_ref[rows, a:b], preferred_element_type=jnp.float32)
            at += depth
        acc_ref[:, a:b] = part
    if last:
        for d, out in enumerate(outs):
            source = pl.multiple_of(place(where[1], d) * ROWS, ROWS)
            out[...] = acc_ref[pl.ds(source, ROWS), :].astype(out.dtype)


def down(where, pieces, down_weight, prev, segments, last):
    width = down_weight.shape[1]
    total = 4 * ROWS
    args = [*pieces, down_weight] + ([] if prev is None else [prev])
    sums = jax.ShapeDtypeStruct((total, width), jnp.float32)
    scratch = [pltpu.VMEM((total, pieces[0].shape[1]), jnp.bfloat16)]
    if last:
        scratch = [pltpu.VMEM(sums.shape, sums.dtype)] + scratch
    return pl.pallas_call(
        functools.partial(down_kernel, len(pieces), prev is not None, last, segments),
        in_specs=[spec(pltpu.SMEM)] + [spec(pltpu.VMEM)] * len(args),
        out_specs=[spec(pltpu.VMEM)] * 4 if last else spec(pltpu.VMEM),
        scratch_shapes=scratch,
        out_shape=[jax.ShapeDtypeStruct((ROWS, width), jnp.bfloat16)] * 4 if last else sums,
        compiler_params=params(4),
        cost_estimate=COST,
        name="down",
    )(where, *args)


def split_by_rep(tokens, gate_weight, up_weight, down_weight):
    rep, wid = lax.axis_index("rep"), lax.axis_index("wid")
    f32, bf16 = jnp.float32, jnp.bfloat16
    half = gate_weight.shape[1] // 2
    where = jnp.stack([rep * half, wid]).astype(jnp.int32)

    def swap(x, axis, step):
        n = {"rep": 2, "hid": 4, "wid": 4}[axis]
        return lax.ppermute(x, axis, [(i, i ^ step) for i in range(n)])

    tiles = half // TILE
    bounds = [0, (tiles - LAST) // 2 * TILE, (tiles - LAST) * TILE, half]
    widths = [b - a for a, b in zip(bounds[:-1], bounds[1:])]
    gate_weight, up_weight, hbm_tokens = (
        pltpu.with_memory_space_constraint(w, pltpu.HBM) for w in (gate_weight, up_weight, tokens)
    )
    down_weight = pltpu.with_memory_space_constraint(down_weight, pltpu.VMEM)

    far_own = swap(tokens, "rep", 1)
    by_hid = [swap(tokens, "hid", d) for d in (3, 2, 1)][::-1]
    early = [fetch(where, gate_weight, up_weight, hbm_tokens, bounds[c], widths[c]) for c in range(2)]
    own = early[0][2]
    near = join(by_hid, [own, far_own])
    far = swap(near, "rep", 1)

    sums, to_chips, behind = [], [], [early[1][0]]
    for weights in early:
        mine, theirs = gate_up(where, [own, near, far_own, far], weights[:2], [], behind)
        behind = [mine]
        got = swap(theirs, "wid", 1)
        to_chips.append(pair_sum(mine, got, []))
        sums.append((mine, got, swap(to_chips[-1], "wid", 2)))
    segments = [(bounds[2], widths[2]), (half + bounds[2], widths[2])]
    mine, theirs = gate_up(where, [own, near], [gate_weight, up_weight], segments, to_chips)
    got = swap(later(theirs, [s[2] for s in sums]), "wid", 1)
    to_chip = pair_sum(mine, got, [])
    last_sum = (mine, got, swap(to_chip, "wid", 2))

    keep, give = combine(sums, [], [to_chip])
    (rest,) = combine([last_sum], [swap(give, "rep", 1)], [])
    rest_segments = [(-1, half, bounds[2])] + [(0, start, width) for start, width in segments]
    acc, behind = None, [rest]
    for hidden, parts in ((keep, [(1, 0, bounds[2])]), (rest, rest_segments)):
        other = swap(hidden, "wid", 2)
        crossed = swap(join([hidden, other], behind), "wid", 1)
        acc = down(where, [hidden, other, crossed], down_weight, acc, parts, hidden is rest)
        behind = [acc]

    mixed = acc[0].astype(f32)
    for d in (3, 2, 1):
        mixed = mixed + swap(acc[d], "hid", d).astype(f32)
    return mixed.astype(bf16)


def solution(mesh):
    n_rep, n_hid, n_wid = (mesh.shape[a] for a in ("rep", "hid", "wid"))

    def on_device(tokens, gate_weight, up_weight, down_weight):
        fits = (
            (n_rep, n_hid, n_wid) == (2, 4, 4)
            and gate_weight.shape[1] % (n_rep * TILE) == 0
            and tokens.shape[0] == ROWS
        )
        if not fits:
            return plain(tokens, gate_weight, up_weight, down_weight)
        return split_by_rep(tokens, gate_weight, up_weight, down_weight)

    return jax.shard_map(
        on_device,
        mesh=mesh,
        in_specs=(P(("rep", "hid"), "wid"), P("wid", "hid"), P("wid", "hid"), P("hid", "wid")),
        out_specs=P(("rep", "hid"), "wid"),
        check_vma=False,
    )
```

```python
import functools

import jax
import jax.numpy as jnp
from jax import lax
from jax.experimental import pallas as pl
from jax.experimental.pallas import tpu as pltpu
from jax.sharding import PartitionSpec as P

TILE = 256
LAST = 3
ROWS = 16
COST = pl.CostEstimate(flops=0, bytes_accessed=1024, transcendentals=0)


def plain(tokens, gate_weight, up_weight, down_weight):
    piece = lax.all_gather(tokens, "hid", axis=0, tiled=True)
    gate_rows = jnp.dot(piece, gate_weight, preferred_element_type=jnp.float32)
    up_rows = jnp.dot(piece, up_weight, preferred_element_type=jnp.float32)
    partial_terms = jnp.stack([gate_rows, up_rows], 0)
    summed = lax.psum(partial_terms.astype(jnp.bfloat16), "wid").astype(jnp.float32)
    hidden = (jax.nn.silu(summed[0]) * summed[1]).astype(jnp.bfloat16)
    return lax.psum_scatter(
        jnp.dot(hidden, down_weight, preferred_element_type=jnp.float32).astype(jnp.bfloat16),
        "hid",
        scatter_dimension=0,
        tiled=True,
    )


def pieces_of(width, most):
    first = width % most
    edges = ([0] if first else []) + list(range(first, width + 1, most))
    return list(zip(edges[:-1], edges[1:]))


def place(wid, d):
    step = wid ^ d
    return (step % 2) * 2 + step // 2


def spec(space):
    return pl.BlockSpec(memory_space=space)


def params(mib):
    return pltpu.CompilerParams(vmem_limit_bytes=mib * 2**20)


def column_copies(source_ref, out_ref, segments, sems):
    copies, cuts, at = [], [], 0
    for start, width in segments:
        for a, b in pieces_of(width, 2 * TILE):
            source = source_ref.at[:, pl.ds(pl.multiple_of(start + a, TILE), b - a)]
            copies.append(pltpu.make_async_copy(source, out_ref.at[:, at + a : at + b], sems.at[len(copies)]))
            cuts.append((at + a, at + b))
        at += width
    return copies, cuts


def fetch_kernel(first, where, gate_ref, up_ref, tokens_ref, gate_out, up_out, tokens_out, sems):
    copies = [pltpu.make_async_copy(tokens_ref, tokens_out, sems.at[2, 0])]
    for k, (source, out) in enumerate(((gate_ref, gate_out), (up_ref, up_out))):
        copies += column_copies(source, out, [(where[0] + first, out.shape[1])], sems.at[k])[0]
    for copy in copies:
        copy.start()
    for copy in copies:
        copy.wait()


def fetch(where, gate, up, tokens, first, width):
    depth = gate.shape[0]
    return pl.pallas_call(
        functools.partial(fetch_kernel, first),
        in_specs=[spec(pltpu.SMEM)] + [spec(pltpu.HBM)] * 3,
        out_specs=[spec(pltpu.VMEM)] * 3,
        out_shape=[pltpu.VMEM(x, jnp.bfloat16) for x in ((depth, width), (depth, width), tokens.shape)],
        scratch_shapes=[pltpu.SemaphoreType.DMA((3, len(pieces_of(width, 2 * TILE))))],
        compiler_params=params(1),
        cost_estimate=COST,
        name="fetch",
    )(where, gate, up, tokens)


def join_kernel(n, first, *refs):
    out_ref, at = refs[-1], 0
    for ref in refs[:n]:
        out_ref[at : at + ref.shape[0], :] = ref[:, first : first + out_ref.shape[1]]
        at += ref.shape[0]


def join(arrays, behind, first=0, width=None):
    rows, width = sum(a.shape[0] for a in arrays), width or arrays[0].shape[1]
    return pl.pallas_call(
        functools.partial(join_kernel, len(arrays), first),
        in_specs=[spec(pltpu.VMEM)] * len(arrays) + [spec(pl.ANY)] * len(behind),
        out_specs=spec(pltpu.VMEM),
        out_shape=jax.ShapeDtypeStruct((rows, width), arrays[0].dtype),
        compiler_params=params(1),
        cost_estimate=COST,
        name="join",
    )(*arrays, *behind)


def gate_up_kernel(n_arrays, n_pairs, segments, where, *refs):
    arrays, weights = refs[:n_arrays], refs[n_arrays : n_arrays + 2 * n_pairs]
    if segments:
        mine_ref, theirs_ref, x_ref, w_ref, sems = refs[-5:]
        copies = [column_copies(weights[k], w_ref.at[k], segments, sems.at[k]) for k in range(2)]
        cuts = copies[0][1]
        for i in range(len(cuts)):
            for k in range(2):
                copies[k][0][i].start()
    else:
        mine_ref, theirs_ref, x_ref = refs[-3:]
        step = weights[0].shape[1]
        cuts = [(p * step + a, p * step + b) for p in range(n_pairs) for a, b in pieces_of(step, 2 * TILE)]
    per = x_ref.shape[0] // (4 * ROWS)
    b = 0
    for array in arrays:
        for at in range(0, array.shape[0], ROWS):
            to = (place(where[1], b % 4) * per + b // 4) * ROWS
            x_ref[pl.ds(pl.multiple_of(to, ROWS), ROWS), :] = array[at : at + ROWS, :]
            b += 1
    half = x_ref.shape[0] // 2
    for i, (a, b) in enumerate(cuts):
        for k in range(2):
            if segments:
                copies[k][0][i].wait()
                weight = w_ref[k, :, a:b]
            else:
                p = a // step
                weight = weights[2 * p + k][:, a - p * step : b - p * step]
            part = jnp.dot(x_ref[...], weight, preferred_element_type=jnp.float32).astype(jnp.bfloat16)
            mine_ref[k, :, a:b] = part[:half]
            theirs_ref[k, :, a:b] = part[half:]


def gate_up(where, arrays, weights, segments, behind):
    depth = weights[0].shape[0]
    width = sum(w for _, w in segments) if segments else sum(w.shape[1] for w in weights[::2])
    total = sum(a.shape[0] for a in arrays)
    scratch = [pltpu.VMEM((total, depth), jnp.bfloat16)]
    if segments:
        n_cuts = sum(len(pieces_of(w, 2 * TILE)) for _, w in segments)
        scratch.append(pltpu.VMEM((2, depth, width), jnp.bfloat16))
        scratch.append(pltpu.SemaphoreType.DMA((2, n_cuts)))
    return pl.pallas_call(
        functools.partial(gate_up_kernel, len(arrays), len(weights) // 2, segments),
        in_specs=[spec(pltpu.SMEM)]
        + [spec(pltpu.VMEM)] * len(arrays)
        + [spec(pltpu.HBM if segments else pltpu.VMEM)] * len(weights)
        + [spec(pl.ANY)] * len(behind),
        out_specs=[spec(pltpu.VMEM)] * 2,
        scratch_shapes=scratch,
        out_shape=[jax.ShapeDtypeStruct((2, total // 2, width), jnp.bfloat16)] * 2,
        compiler_params=params(16 if segments else 4),
        cost_estimate=COST,
        name="gate_up",
    )(where, *arrays, *weights, *behind)


def pair_sum_kernel(mine_ref, got_ref, *refs):
    out_ref = refs[-1]
    rows = out_ref.shape[1]
    for k in range(2):
        total = mine_ref[k, rows:].astype(jnp.float32) + got_ref[k, rows:].astype(jnp.float32)
        out_ref[k] = total.astype(out_ref.dtype)


def pair_sum(mine, got, behind):
    _, rows, width = mine.shape
    return pl.pallas_call(
        pair_sum_kernel,
        in_specs=[spec(pltpu.VMEM)] * 2 + [spec(pl.ANY)] * len(behind),
        out_specs=spec(pltpu.VMEM),
        out_shape=jax.ShapeDtypeStruct((2, rows // 2, width), mine.dtype),
        compiler_params=params(2),
        cost_estimate=COST,
        name="pair_sum",
    )(mine, got, *behind)


def combine_kernel(n_left, n_outs, mine_ref, got_ref, chip_ref, *refs):
    outs = refs[-n_outs:]
    rows, first = chip_ref.shape[1], 0
    for left in refs[:n_left]:
        first = left.shape[1]
        outs[0][:, :first] = left[...]
    for a, b in pieces_of(chip_ref.shape[2], TILE):
        gate, up = (
            mine_ref[k, :rows, a:b].astype(jnp.float32)
            + got_ref[k, :rows, a:b].astype(jnp.float32)
            + chip_ref[k, :, a:b].astype(jnp.float32)
            for k in range(2)
        )
        hidden = (gate / (1 + jnp.exp(-gate)) * up).astype(jnp.bfloat16)
        for i, out in enumerate(outs):
            out[:, first + a : first + b] = hidden[i * ROWS : (i + 1) * ROWS]


def combine(mine, got, from_chip, left, behind):
    _, rows, width = from_chip.shape
    n_outs = rows // ROWS
    width += sum(x.shape[1] for x in left)
    return pl.pallas_call(
        functools.partial(combine_kernel, len(left), n_outs),
        in_specs=[spec(pltpu.VMEM)] * (3 + len(left)) + [spec(pl.ANY)] * len(behind),
        out_specs=[spec(pltpu.VMEM)] * n_outs,
        out_shape=[jax.ShapeDtypeStruct((ROWS, width), jnp.bfloat16)] * n_outs,
        compiler_params=params(2),
        cost_estimate=COST,
        name="combine",
    )(mine, got, from_chip, *left, *behind)


def down_kernel(n_pieces, has_acc, last, segments, columns, where, *refs):
    pieces, refs = refs[:n_pieces], refs[n_pieces:]
    down_ref, refs = refs[0], refs[1:]
    prev_ref, refs = (refs[0], refs[1:]) if has_acc else (None, refs)
    outs, (acc_ref, lhs_ref) = refs[:-2], refs[-2:]
    at = 0
    for piece in pieces:
        lhs_ref[at : at + piece.shape[0], :] = piece[...]
        at += piece.shape[0]
    left = columns[0]
    for a, b in pieces_of(acc_ref.shape[1], 2 * TILE):
        part = prev_ref[:, left + a : left + b] if has_acc else 0.0
        at = 0
        for sign, start, depth in segments:
            rows = pl.ds(pl.multiple_of(sign * where[0] + start, TILE) if sign else start, depth)
            part += jnp.dot(lhs_ref[:, at : at + depth], down_ref[rows, left + a : left + b], preferred_element_type=jnp.float32)
            at += depth
        acc_ref[:, a:b] = part
    if last:
        for d, out in enumerate(outs):
            source = pl.multiple_of(place(where[1], d) * ROWS, ROWS)
            out[...] = acc_ref[pl.ds(source, ROWS), :].astype(out.dtype)


def down(where, pieces, down_weight, prev, segments, columns, last):
    width = columns[1] - columns[0]
    total = 4 * ROWS
    args = [*pieces, down_weight] + ([] if prev is None else [prev])
    sums = jax.ShapeDtypeStruct((total, width), jnp.float32)
    scratch = [pltpu.VMEM((total, pieces[0].shape[1]), jnp.bfloat16)]
    if last:
        scratch = [pltpu.VMEM(sums.shape, sums.dtype)] + scratch
    return pl.pallas_call(
        functools.partial(down_kernel, len(pieces), prev is not None, last, segments, columns),
        in_specs=[spec(pltpu.SMEM)] + [spec(pltpu.VMEM)] * len(args),
        out_specs=[spec(pltpu.VMEM)] * 4 if last else spec(pltpu.VMEM),
        scratch_shapes=scratch,
        out_shape=[jax.ShapeDtypeStruct((ROWS, width), jnp.bfloat16)] * 4 if last else sums,
        compiler_params=params(4),
        cost_estimate=COST,
        name="down",
    )(where, *args)


def split_by_rep(tokens, gate_weight, up_weight, down_weight):
    rep, wid = lax.axis_index("rep"), lax.axis_index("wid")
    f32, bf16 = jnp.float32, jnp.bfloat16
    half = gate_weight.shape[1] // 2
    where = jnp.stack([rep * half, wid]).astype(jnp.int32)

    def swap(x, axis, step):
        n = {"rep": 2, "hid": 4, "wid": 4}[axis]
        return lax.ppermute(x, axis, [(i, i ^ step) for i in range(n)])

    tiles = half // TILE
    bounds = [0, (tiles - LAST) // 2 * TILE, (tiles - LAST) * TILE, half]
    widths = [b - a for a, b in zip(bounds[:-1], bounds[1:])]
    gate_weight, up_weight, hbm_tokens = (
        pltpu.with_memory_space_constraint(w, pltpu.HBM) for w in (gate_weight, up_weight, tokens)
    )
    down_weight = pltpu.with_memory_space_constraint(down_weight, pltpu.VMEM)

    far_own = swap(tokens, "rep", 1)
    by_hid = [swap(tokens, "hid", d) for d in (3, 2, 1)][::-1]
    early = [fetch(where, gate_weight, up_weight, hbm_tokens, bounds[c], widths[c]) for c in range(2)]
    own = early[0][2]
    near = join(by_hid, [own, far_own])
    far = swap(near, "rep", 1)

    weights = [w for fetched in early for w in fetched[:2]]
    mine, theirs = gate_up(where, [own, near, far_own, far], weights, [], [])
    got = swap(theirs, "wid", 1)
    to_chip = pair_sum(mine, got, [])
    from_chip = swap(to_chip, "wid", 2)
    segments = [(bounds[2], widths[2]), (half + bounds[2], widths[2])]
    last_mine, theirs = gate_up(where, [own, near], [gate_weight, up_weight], segments, [to_chip])
    last_got = swap(theirs, "wid", 1)
    keep, give = combine(mine, got, from_chip, [], [])
    last_to_chip = pair_sum(last_mine, last_got, [give])
    last_from_chip = swap(last_to_chip, "wid", 2)
    (rest,) = combine(last_mine, last_got, last_from_chip, [swap(give, "rep", 1)], [])

    def gather(hidden, behind):
        other = swap(hidden, "wid", 2)
        return [hidden, other, swap(hidden, "wid", 1), swap(join([other], behind), "wid", 1)]

    features = down_weight.shape[1]
    acc = down(where, gather(keep, [rest]), down_weight, None, [(1, 0, bounds[2])], (0, features), False)
    pieces = gather(rest, [acc])
    rest_segments = [(-1, half, bounds[2])] + [(0, start, width) for start, width in segments]
    mixed = []
    for columns in ((0, features // 2), (features // 2, features)):
        out = down(where, pieces, down_weight, acc, rest_segments, columns, True)
        total = out[0].astype(f32)
        for d in (3, 2, 1):
            total = total + swap(out[d], "hid", d).astype(f32)
        mixed.append(total.astype(bf16))
    return jnp.concatenate(mixed, 1)


def solution(mesh):
    n_rep, n_hid, n_wid = (mesh.shape[a] for a in ("rep", "hid", "wid"))

    def on_device(tokens, gate_weight, up_weight, down_weight):
        fits = (
            (n_rep, n_hid, n_wid) == (2, 4, 4)
            and gate_weight.shape[1] % (n_rep * TILE) == 0
            and tokens.shape[0] == ROWS
        )
        if not fits:
            return plain(tokens, gate_weight, up_weight, down_weight)
        return split_by_rep(tokens, gate_weight, up_weight, down_weight)

    return jax.shard_map(
        on_device,
        mesh=mesh,
        in_specs=(P(("rep", "hid"), "wid"), P("wid", "hid"), P("wid", "hid"), P("hid", "wid")),
        out_specs=P(("rep", "hid"), "wid"),
        check_vma=False,
    )
```

```python
import functools

import jax
import jax.numpy as jnp
from jax import lax
from jax.experimental import pallas as pl
from jax.experimental.pallas import tpu as pltpu
from jax.sharding import PartitionSpec as P

TILE = 256
LAST = 3
ROWS = 16
COST = pl.CostEstimate(flops=0, bytes_accessed=1024, transcendentals=0)


def plain(tokens, gate_weight, up_weight, down_weight):
    piece = lax.all_gather(tokens, "hid", axis=0, tiled=True)
    gate_rows = jnp.dot(piece, gate_weight, preferred_element_type=jnp.float32)
    up_rows = jnp.dot(piece, up_weight, preferred_element_type=jnp.float32)
    partial_terms = jnp.stack([gate_rows, up_rows], 0)
    summed = lax.psum(partial_terms.astype(jnp.bfloat16), "wid").astype(jnp.float32)
    hidden = (jax.nn.silu(summed[0]) * summed[1]).astype(jnp.bfloat16)
    return lax.psum_scatter(
        jnp.dot(hidden, down_weight, preferred_element_type=jnp.float32).astype(jnp.bfloat16),
        "hid",
        scatter_dimension=0,
        tiled=True,
    )


def pieces_of(width, most):
    first = width % most
    edges = ([0] if first else []) + list(range(first, width + 1, most))
    return list(zip(edges[:-1], edges[1:]))


def place(wid, d):
    step = wid ^ d
    return (step % 2) * 2 + step // 2


def spec(space):
    return pl.BlockSpec(memory_space=space)


def params(mib):
    return pltpu.CompilerParams(vmem_limit_bytes=mib * 2**20)


def column_copies(source_ref, out_ref, segments, sems):
    copies, cuts, at = [], [], 0
    for start, width in segments:
        for a, b in pieces_of(width, 2 * TILE):
            source = source_ref.at[:, pl.ds(pl.multiple_of(start + a, TILE), b - a)]
            copies.append(pltpu.make_async_copy(source, out_ref.at[:, at + a : at + b], sems.at[len(copies)]))
            cuts.append((at + a, at + b))
        at += width
    return copies, cuts


def fetch_kernel(first, where, gate_ref, up_ref, tokens_ref, gate_out, up_out, tokens_out, sems):
    copies = [pltpu.make_async_copy(tokens_ref, tokens_out, sems.at[2, 0])]
    for k, (source, out) in enumerate(((gate_ref, gate_out), (up_ref, up_out))):
        copies += column_copies(source, out, [(where[0] + first, out.shape[1])], sems.at[k])[0]
    for copy in copies:
        copy.start()
    for copy in copies:
        copy.wait()


def fetch(where, gate, up, tokens, first, width):
    depth = gate.shape[0]
    return pl.pallas_call(
        functools.partial(fetch_kernel, first),
        in_specs=[spec(pltpu.SMEM)] + [spec(pltpu.HBM)] * 3,
        out_specs=[spec(pltpu.VMEM)] * 3,
        out_shape=[pltpu.VMEM(x, jnp.bfloat16) for x in ((depth, width), (depth, width), tokens.shape)],
        scratch_shapes=[pltpu.SemaphoreType.DMA((3, len(pieces_of(width, 2 * TILE))))],
        compiler_params=params(1),
        cost_estimate=COST,
        name="fetch",
    )(where, gate, up, tokens)


def join_kernel(n, first, *refs):
    out_ref, at = refs[-1], 0
    for ref in refs[:n]:
        out_ref[at : at + ref.shape[0], :] = ref[:, first : first + out_ref.shape[1]]
        at += ref.shape[0]


def join(arrays, behind, first=0, width=None):
    rows, width = sum(a.shape[0] for a in arrays), width or arrays[0].shape[1]
    return pl.pallas_call(
        functools.partial(join_kernel, len(arrays), first),
        in_specs=[spec(pltpu.VMEM)] * len(arrays) + [spec(pl.ANY)] * len(behind),
        out_specs=spec(pltpu.VMEM),
        out_shape=jax.ShapeDtypeStruct((rows, width), arrays[0].dtype),
        compiler_params=params(1),
        cost_estimate=COST,
        name="join",
    )(*arrays, *behind)


def gate_up_kernel(n_arrays, n_pairs, segments, where, *refs):
    arrays, weights = refs[:n_arrays], refs[n_arrays : n_arrays + 2 * n_pairs]
    if segments:
        mine_ref, theirs_ref, x_ref, w_ref, sems = refs[-5:]
        copies = [column_copies(weights[k], w_ref.at[k], segments, sems.at[k]) for k in range(2)]
        cuts = copies[0][1]
        for i in range(len(cuts)):
            for k in range(2):
                copies[k][0][i].start()
    else:
        mine_ref, theirs_ref, x_ref = refs[-3:]
        step = weights[0].shape[1]
        cuts = [(p * step + a, p * step + b) for p in range(n_pairs) for a, b in pieces_of(step, 2 * TILE)]
    per = x_ref.shape[0] // (4 * ROWS)
    b = 0
    for array in arrays:
        for at in range(0, array.shape[0], ROWS):
            to = (place(where[1], b % 4) * per + b // 4) * ROWS
            x_ref[pl.ds(pl.multiple_of(to, ROWS), ROWS), :] = array[at : at + ROWS, :]
            b += 1
    half = x_ref.shape[0] // 2
    for i, (a, b) in enumerate(cuts):
        for k in range(2):
            if segments:
                copies[k][0][i].wait()
                weight = w_ref[k, :, a:b]
            else:
                p = a // step
                weight = weights[2 * p + k][:, a - p * step : b - p * step]
            part = jnp.dot(x_ref[...], weight, preferred_element_type=jnp.float32).astype(jnp.bfloat16)
            mine_ref[k, :, a:b] = part[:half]
            theirs_ref[k, :, a:b] = part[half:]


def gate_up(where, arrays, weights, segments, behind):
    depth = weights[0].shape[0]
    width = sum(w for _, w in segments) if segments else sum(w.shape[1] for w in weights[::2])
    total = sum(a.shape[0] for a in arrays)
    scratch = [pltpu.VMEM((total, depth), jnp.bfloat16)]
    if segments:
        n_cuts = sum(len(pieces_of(w, 2 * TILE)) for _, w in segments)
        scratch.append(pltpu.VMEM((2, depth, width), jnp.bfloat16))
        scratch.append(pltpu.SemaphoreType.DMA((2, n_cuts)))
    return pl.pallas_call(
        functools.partial(gate_up_kernel, len(arrays), len(weights) // 2, segments),
        in_specs=[spec(pltpu.SMEM)]
        + [spec(pltpu.VMEM)] * len(arrays)
        + [spec(pltpu.HBM if segments else pltpu.VMEM)] * len(weights)
        + [spec(pl.ANY)] * len(behind),
        out_specs=[spec(pltpu.VMEM)] * 2,
        scratch_shapes=scratch,
        out_shape=[jax.ShapeDtypeStruct((2, total // 2, width), jnp.bfloat16)] * 2,
        compiler_params=params(16 if segments else 4),
        cost_estimate=COST,
        name="gate_up",
    )(where, *arrays, *weights, *behind)


def pair_sum_kernel(mine_ref, got_ref, *refs):
    out_ref = refs[-1]
    rows = out_ref.shape[1]
    for k in range(2):
        total = mine_ref[k, rows:].astype(jnp.float32) + got_ref[k, rows:].astype(jnp.float32)
        out_ref[k] = total.astype(out_ref.dtype)


def pair_sum(mine, got, behind):
    _, rows, width = mine.shape
    return pl.pallas_call(
        pair_sum_kernel,
        in_specs=[spec(pltpu.VMEM)] * 2 + [spec(pl.ANY)] * len(behind),
        out_specs=spec(pltpu.VMEM),
        out_shape=jax.ShapeDtypeStruct((2, rows // 2, width), mine.dtype),
        compiler_params=params(2),
        cost_estimate=COST,
        name="pair_sum",
    )(mine, got, *behind)


def combine_kernel(n_left, n_outs, mine_ref, got_ref, chip_ref, *refs):
    outs = refs[-n_outs:]
    rows, first = chip_ref.shape[1], 0
    for left in refs[:n_left]:
        first = left.shape[1]
        outs[0][:, :first] = left[...]
    for a, b in pieces_of(chip_ref.shape[2], TILE):
        gate, up = (
            mine_ref[k, :rows, a:b].astype(jnp.float32)
            + got_ref[k, :rows, a:b].astype(jnp.float32)
            + chip_ref[k, :, a:b].astype(jnp.float32)
            for k in range(2)
        )
        hidden = (gate / (1 + jnp.exp(-gate)) * up).astype(jnp.bfloat16)
        for i, out in enumerate(outs):
            out[:, first + a : first + b] = hidden[i * ROWS : (i + 1) * ROWS]


def combine(mine, got, from_chip, left, behind):
    _, rows, width = from_chip.shape
    n_outs = rows // ROWS
    width += sum(x.shape[1] for x in left)
    return pl.pallas_call(
        functools.partial(combine_kernel, len(left), n_outs),
        in_specs=[spec(pltpu.VMEM)] * (3 + len(left)) + [spec(pl.ANY)] * len(behind),
        out_specs=[spec(pltpu.VMEM)] * n_outs,
        out_shape=[jax.ShapeDtypeStruct((ROWS, width), jnp.bfloat16)] * n_outs,
        compiler_params=params(2),
        cost_estimate=COST,
        name="combine",
    )(mine, got, from_chip, *left, *behind)


def down_kernel(n_pieces, has_acc, last, segments, columns, where, *refs):
    pieces, refs = refs[:n_pieces], refs[n_pieces:]
    down_ref, refs = refs[0], refs[1:]
    prev_ref, refs = (refs[0], refs[1:]) if has_acc else (None, refs)
    outs, (acc_ref, lhs_ref) = refs[:-2], refs[-2:]
    at = 0
    for piece in pieces:
        lhs_ref[at : at + piece.shape[0], :] = piece[...]
        at += piece.shape[0]
    left = columns[0]
    for a, b in pieces_of(acc_ref.shape[1], 2 * TILE):
        part = prev_ref[:, left + a : left + b] if has_acc else 0.0
        at = 0
        for sign, start, depth in segments:
            rows = pl.ds(pl.multiple_of(sign * where[0] + start, TILE) if sign else start, depth)
            part += jnp.dot(lhs_ref[:, at : at + depth], down_ref[rows, left + a : left + b], preferred_element_type=jnp.float32)
            at += depth
        acc_ref[:, a:b] = part
    if last:
        (out,) = outs
        for h in range(out.shape[0]):
            source = pl.multiple_of(place(where[1], where[2] ^ h) * ROWS, ROWS)
            out[h] = acc_ref[pl.ds(source, ROWS), :].astype(out.dtype)


def down(where, pieces, down_weight, prev, segments, columns, last):
    width = columns[1] - columns[0]
    total = 4 * ROWS
    args = [*pieces, down_weight] + ([] if prev is None else [prev])
    sums = jax.ShapeDtypeStruct((total, width), jnp.float32)
    scratch = [pltpu.VMEM((total, pieces[0].shape[1]), jnp.bfloat16)]
    if last:
        scratch = [pltpu.VMEM(sums.shape, sums.dtype)] + scratch
    return pl.pallas_call(
        functools.partial(down_kernel, len(pieces), prev is not None, last, segments, columns),
        in_specs=[spec(pltpu.SMEM)] + [spec(pltpu.VMEM)] * len(args),
        out_specs=spec(pltpu.VMEM),
        scratch_shapes=scratch,
        out_shape=jax.ShapeDtypeStruct((4, ROWS, width), jnp.bfloat16) if last else sums,
        compiler_params=params(4),
        cost_estimate=COST,
        name="down",
    )(where, *args)


def split_by_rep(tokens, gate_weight, up_weight, down_weight):
    rep, hid, wid = lax.axis_index("rep"), lax.axis_index("hid"), lax.axis_index("wid")
    f32, bf16 = jnp.float32, jnp.bfloat16
    half = gate_weight.shape[1] // 2
    where = jnp.stack([rep * half, wid, hid]).astype(jnp.int32)

    def swap(x, axis, step):
        n = {"rep": 2, "hid": 4, "wid": 4}[axis]
        return lax.ppermute(x, axis, [(i, i ^ step) for i in range(n)])

    tiles = half // TILE
    bounds = [0, (tiles - LAST) // 2 * TILE, (tiles - LAST) * TILE, half]
    widths = [b - a for a, b in zip(bounds[:-1], bounds[1:])]
    gate_weight, up_weight, hbm_tokens = (
        pltpu.with_memory_space_constraint(w, pltpu.HBM) for w in (gate_weight, up_weight, tokens)
    )
    down_weight = pltpu.with_memory_space_constraint(down_weight, pltpu.VMEM)

    far_own = swap(tokens, "rep", 1)
    by_hid = [swap(tokens, "hid", d) for d in (3, 2, 1)][::-1]
    early = [fetch(where, gate_weight, up_weight, hbm_tokens, bounds[c], widths[c]) for c in range(2)]
    own = early[0][2]
    near = join(by_hid, [own, far_own])
    far = swap(near, "rep", 1)

    weights = [w for fetched in early for w in fetched[:2]]
    mine, theirs = gate_up(where, [own, near, far_own, far], weights, [], [])
    got = swap(theirs, "wid", 1)
    to_chip = pair_sum(mine, got, [])
    from_chip = swap(to_chip, "wid", 2)
    segments = [(bounds[2], widths[2]), (half + bounds[2], widths[2])]
    last_mine, theirs = gate_up(where, [own, near], [gate_weight, up_weight], segments, [to_chip])
    last_got = swap(theirs, "wid", 1)
    keep, give = combine(mine, got, from_chip, [], [])
    last_to_chip = pair_sum(last_mine, last_got, [give])
    last_from_chip = swap(last_to_chip, "wid", 2)
    (rest,) = combine(last_mine, last_got, last_from_chip, [swap(give, "rep", 1)], [])

    def gather(hidden, behind):
        other = swap(hidden, "wid", 2)
        return [hidden, other, swap(hidden, "wid", 1), swap(join([other], behind), "wid", 1)]

    features = down_weight.shape[1]
    acc = down(where, gather(keep, [rest]), down_weight, None, [(1, 0, bounds[2])], (0, features), False)
    pieces = gather(rest, [acc])
    rest_segments = [(-1, half, bounds[2])] + [(0, start, width) for start, width in segments]
    out = down(where, pieces, down_weight, acc, rest_segments, (0, features), True)
    return lax.all_to_all(out, "hid", 0, 0).astype(f32).sum(0).astype(bf16)


def solution(mesh):
    n_rep, n_hid, n_wid = (mesh.shape[a] for a in ("rep", "hid", "wid"))

    def on_device(tokens, gate_weight, up_weight, down_weight):
        fits = (
            (n_rep, n_hid, n_wid) == (2, 4, 4)
            and gate_weight.shape[1] % (n_rep * TILE) == 0
            and tokens.shape[0] == ROWS
        )
        if not fits:
            return plain(tokens, gate_weight, up_weight, down_weight)
        return split_by_rep(tokens, gate_weight, up_weight, down_weight)

    return jax.shard_map(
        on_device,
        mesh=mesh,
        in_specs=(P(("rep", "hid"), "wid"), P("wid", "hid"), P("wid", "hid"), P("hid", "wid")),
        out_specs=P(("rep", "hid"), "wid"),
        check_vma=False,
    )
```

```python
import functools

import jax
import jax.numpy as jnp
from jax import lax
from jax.experimental import pallas as pl
from jax.experimental.pallas import tpu as pltpu
from jax.sharding import PartitionSpec as P

TILE = 256
CHUNKS = (6, 3, 4)
ROWS = 16
COST = pl.CostEstimate(flops=0, bytes_accessed=1024, transcendentals=0)


def plain(tokens, gate_weight, up_weight, down_weight):
    piece = lax.all_gather(tokens, "hid", axis=0, tiled=True)
    gate_rows = jnp.dot(piece, gate_weight, preferred_element_type=jnp.float32)
    up_rows = jnp.dot(piece, up_weight, preferred_element_type=jnp.float32)
    partial_terms = jnp.stack([gate_rows, up_rows], 0)
    summed = lax.psum(partial_terms.astype(jnp.bfloat16), "wid").astype(jnp.float32)
    hidden = (jax.nn.silu(summed[0]) * summed[1]).astype(jnp.bfloat16)
    return lax.psum_scatter(
        jnp.dot(hidden, down_weight, preferred_element_type=jnp.float32).astype(jnp.bfloat16),
        "hid",
        scatter_dimension=0,
        tiled=True,
    )


def pieces_of(width, most):
    first = width % most
    edges = ([0] if first else []) + list(range(first, width + 1, most))
    return list(zip(edges[:-1], edges[1:]))


def place(wid, d):
    step = wid ^ d
    return (step % 2) * 2 + step // 2


def spec(space):
    return pl.BlockSpec(memory_space=space)


def params(mib):
    return pltpu.CompilerParams(vmem_limit_bytes=mib * 2**20)


def column_copies(source_ref, out_ref, segments, sems):
    copies, cuts, at = [], [], 0
    for start, width in segments:
        for a, b in pieces_of(width, 2 * TILE):
            source = source_ref.at[:, pl.ds(pl.multiple_of(start + a, TILE), b - a)]
            copies.append(pltpu.make_async_copy(source, out_ref.at[:, at + a : at + b], sems.at[len(copies)]))
            cuts.append((at + a, at + b))
        at += width
    return copies, cuts


def fetch_kernel(first, where, gate_ref, up_ref, tokens_ref, gate_out, up_out, tokens_out, sems):
    copies = [pltpu.make_async_copy(tokens_ref, tokens_out, sems.at[2, 0])]
    for k, (source, out) in enumerate(((gate_ref, gate_out), (up_ref, up_out))):
        copies += column_copies(source, out, [(where[0] + first, out.shape[1])], sems.at[k])[0]
    for copy in copies:
        copy.start()
    for copy in copies:
        copy.wait()


def fetch(where, gate, up, tokens, first, width):
    depth = gate.shape[0]
    return pl.pallas_call(
        functools.partial(fetch_kernel, first),
        in_specs=[spec(pltpu.SMEM)] + [spec(pltpu.HBM)] * 3,
        out_specs=[spec(pltpu.VMEM)] * 3,
        out_shape=[pltpu.VMEM(x, jnp.bfloat16) for x in ((depth, width), (depth, width), tokens.shape)],
        scratch_shapes=[pltpu.SemaphoreType.DMA((3, len(pieces_of(width, 2 * TILE))))],
        compiler_params=params(1),
        cost_estimate=COST,
        name="fetch",
    )(where, gate, up, tokens)


def join_kernel(n, first, *refs):
    out_ref, at = refs[-1], 0
    for ref in refs[:n]:
        out_ref[at : at + ref.shape[0], :] = ref[:, first : first + out_ref.shape[1]]
        at += ref.shape[0]


def join(arrays, behind, first=0, width=None):
    rows, width = sum(a.shape[0] for a in arrays), width or arrays[0].shape[1]
    return pl.pallas_call(
        functools.partial(join_kernel, len(arrays), first),
        in_specs=[spec(pltpu.VMEM)] * len(arrays) + [spec(pl.ANY)] * len(behind),
        out_specs=spec(pltpu.VMEM),
        out_shape=jax.ShapeDtypeStruct((rows, width), arrays[0].dtype),
        compiler_params=params(1),
        cost_estimate=COST,
        name="join",
    )(*arrays, *behind)


def gate_up_kernel(n_arrays, n_pairs, segments, where, *refs):
    arrays, weights = refs[:n_arrays], refs[n_arrays : n_arrays + 2 * n_pairs]
    if segments:
        mine_ref, theirs_ref, x_ref, w_ref, sems = refs[-5:]
        copies = [column_copies(weights[k], w_ref.at[k], segments, sems.at[k]) for k in range(2)]
        cuts = copies[0][1]
        for i in range(len(cuts)):
            for k in range(2):
                copies[k][0][i].start()
    else:
        mine_ref, theirs_ref, x_ref = refs[-3:]
        step = weights[0].shape[1]
        cuts = [(p * step + a, p * step + b) for p in range(n_pairs) for a, b in pieces_of(step, 2 * TILE)]
    per = x_ref.shape[0] // (4 * ROWS)
    b = 0
    for array in arrays:
        for at in range(0, array.shape[0], ROWS):
            to = (place(where[1], b % 4) * per + b // 4) * ROWS
            x_ref[pl.ds(pl.multiple_of(to, ROWS), ROWS), :] = array[at : at + ROWS, :]
            b += 1
    half = x_ref.shape[0] // 2
    for i, (a, b) in enumerate(cuts):
        for k in range(2):
            if segments:
                copies[k][0][i].wait()
                weight = w_ref[k, :, a:b]
            else:
                p = a // step
                weight = weights[2 * p + k][:, a - p * step : b - p * step]
            part = jnp.dot(x_ref[...], weight, preferred_element_type=jnp.float32).astype(jnp.bfloat16)
            mine_ref[k, :, a:b] = part[:half]
            theirs_ref[k, :, a:b] = part[half:]


def gate_up(where, arrays, weights, segments, behind):
    depth = weights[0].shape[0]
    width = sum(w for _, w in segments) if segments else sum(w.shape[1] for w in weights[::2])
    total = sum(a.shape[0] for a in arrays)
    scratch = [pltpu.VMEM((total, depth), jnp.bfloat16)]
    if segments:
        n_cuts = sum(len(pieces_of(w, 2 * TILE)) for _, w in segments)
        scratch.append(pltpu.VMEM((2, depth, width), jnp.bfloat16))
        scratch.append(pltpu.SemaphoreType.DMA((2, n_cuts)))
    return pl.pallas_call(
        functools.partial(gate_up_kernel, len(arrays), len(weights) // 2, segments),
        in_specs=[spec(pltpu.SMEM)]
        + [spec(pltpu.VMEM)] * len(arrays)
        + [spec(pltpu.HBM if segments else pltpu.VMEM)] * len(weights)
        + [spec(pl.ANY)] * len(behind),
        out_specs=[spec(pltpu.VMEM)] * 2,
        scratch_shapes=scratch,
        out_shape=[jax.ShapeDtypeStruct((2, total // 2, width), jnp.bfloat16)] * 2,
        compiler_params=params(20 if segments else 4),
        cost_estimate=COST,
        name="gate_up",
    )(where, *arrays, *weights, *behind)


def pair_sum_kernel(mine_ref, got_ref, *refs):
    out_ref = refs[-1]
    rows = out_ref.shape[1]
    for k in range(2):
        total = mine_ref[k, rows:].astype(jnp.float32) + got_ref[k, rows:].astype(jnp.float32)
        out_ref[k] = total.astype(out_ref.dtype)


def pair_sum(mine, got, behind):
    _, rows, width = mine.shape
    return pl.pallas_call(
        pair_sum_kernel,
        in_specs=[spec(pltpu.VMEM)] * 2 + [spec(pl.ANY)] * len(behind),
        out_specs=spec(pltpu.VMEM),
        out_shape=jax.ShapeDtypeStruct((2, rows // 2, width), mine.dtype),
        compiler_params=params(2),
        cost_estimate=COST,
        name="pair_sum",
    )(mine, got, *behind)


def later_kernel(array_ref, *refs):
    refs[-1][...] = array_ref[...]


def later(array, behind):
    return pl.pallas_call(
        later_kernel,
        in_specs=[spec(pltpu.VMEM)] + [spec(pl.ANY)] * len(behind),
        out_specs=spec(pltpu.VMEM),
        out_shape=jax.ShapeDtypeStruct(array.shape, array.dtype),
        compiler_params=params(1),
        cost_estimate=COST,
        name="later",
    )(array, *behind)


def combine_kernel(n_left, n_sums, n_outs, *refs):
    lefts, refs, outs = refs[:n_left], refs[n_left:], refs[-n_outs:]
    first, total = 0, sum(refs[3 * i + 2].shape[2] for i in range(n_sums))
    for left in lefts:
        outs[0][:, first : first + left.shape[1]] = left[...]
        first += left.shape[1]
    for i in range(n_sums):
        mine_ref, got_ref, chip_ref = refs[3 * i : 3 * i + 3]
        _, rows, width = chip_ref.shape
        for a, b in pieces_of(width, TILE):
            gate, up = (
                mine_ref[k, :rows, a:b].astype(jnp.float32)
                + got_ref[k, :rows, a:b].astype(jnp.float32)
                + chip_ref[k, :, a:b].astype(jnp.float32)
                for k in range(2)
            )
            hidden = (gate / (1 + jnp.exp(-gate)) * up).astype(jnp.bfloat16)
            for j, out in enumerate(outs):
                at = out.shape[1] - total + a
                out[:, at : at + b - a] = hidden[j * ROWS : (j + 1) * ROWS]
        total -= width


def combine(sums, left, behind):
    n_outs = sums[0][2].shape[1] // ROWS
    width = sum(chip.shape[2] for _, _, chip in sums)
    widths = [width + sum(x.shape[1] for x in left)] + [width] * (n_outs - 1)
    args = [*left, *(x for triple in sums for x in triple)]
    return pl.pallas_call(
        functools.partial(combine_kernel, len(left), len(sums), n_outs),
        in_specs=[spec(pltpu.VMEM)] * len(args) + [spec(pl.ANY)] * len(behind),
        out_specs=[spec(pltpu.VMEM)] * n_outs,
        out_shape=[jax.ShapeDtypeStruct((ROWS, w), jnp.bfloat16) for w in widths],
        compiler_params=params(2),
        cost_estimate=COST,
        name="combine",
    )(*args, *behind)


def down_kernel(n_pieces, has_acc, last, segments, where, *refs):
    pieces, refs = refs[:n_pieces], refs[n_pieces:]
    down_ref, refs = refs[0], refs[1:]
    prev_ref, refs = (refs[0], refs[1:]) if has_acc else (None, refs)
    outs, (acc_ref, lhs_ref) = refs[:-2], refs[-2:]
    at = 0
    for piece in pieces:
        lhs_ref[at : at + piece.shape[0], :] = piece[...]
        at += piece.shape[0]
    for a, b in pieces_of(down_ref.shape[1], 2 * TILE):
        part = prev_ref[:, a:b] if has_acc else 0.0
        at = 0
        for sign, start, depth in segments:
            rows = pl.ds(pl.multiple_of(sign * where[0] + start, TILE) if sign else start, depth)
            part += jnp.dot(lhs_ref[:, at : at + depth], down_ref[rows, a:b], preferred_element_type=jnp.float32)
            at += depth
        acc_ref[:, a:b] = part
    if last:
        for d, out in enumerate(outs):
            source = pl.multiple_of(place(where[1], d) * ROWS, ROWS)
            out[...] = acc_ref[pl.ds(source, ROWS), :].astype(out.dtype)


def down(where, pieces, down_weight, prev, segments, last):
    width = down_weight.shape[1]
    total = 4 * ROWS
    args = [*pieces, down_weight] + ([] if prev is None else [prev])
    sums = jax.ShapeDtypeStruct((total, width), jnp.float32)
    scratch = [pltpu.VMEM((total, pieces[0].shape[1]), jnp.bfloat16)]
    if last:
        scratch = [pltpu.VMEM(sums.shape, sums.dtype)] + scratch
    return pl.pallas_call(
        functools.partial(down_kernel, len(pieces), prev is not None, last, segments),
        in_specs=[spec(pltpu.SMEM)] + [spec(pltpu.VMEM)] * len(args),
        out_specs=[spec(pltpu.VMEM)] * 4 if last else spec(pltpu.VMEM),
        scratch_shapes=scratch,
        out_shape=[jax.ShapeDtypeStruct((ROWS, width), jnp.bfloat16)] * 4 if last else sums,
        compiler_params=params(4),
        cost_estimate=COST,
        name="down",
    )(where, *args)


def split_by_rep(tokens, gate_weight, up_weight, down_weight):
    rep, wid = lax.axis_index("rep"), lax.axis_index("wid")
    f32, bf16 = jnp.float32, jnp.bfloat16
    half = gate_weight.shape[1] // 2
    where = jnp.stack([rep * half, wid]).astype(jnp.int32)

    def swap(x, axis, step):
        n = {"rep": 2, "hid": 4, "wid": 4}[axis]
        return lax.ppermute(x, axis, [(i, i ^ step) for i in range(n)])

    bounds = [sum(CHUNKS[:c]) * TILE for c in range(4)]
    both = [[(r * half + a, b - a) for r in range(2)] for a, b in zip(bounds[:-1], bounds[1:])]
    gate_weight, up_weight, hbm_tokens = (
        pltpu.with_memory_space_constraint(w, pltpu.HBM) for w in (gate_weight, up_weight, tokens)
    )
    down_weight = pltpu.with_memory_space_constraint(down_weight, pltpu.VMEM)

    far_own = swap(tokens, "rep", 1)
    by_hid = [swap(tokens, "hid", d) for d in (3, 2, 1)][::-1]
    *early, own = fetch(where, gate_weight, up_weight, hbm_tokens, 0, bounds[1])
    near = join(by_hid, [own, far_own])
    far = swap(near, "rep", 1)

    def reduce(mine, got):
        to_chip = pair_sum(mine, got, [])
        return to_chip, (mine, got, swap(to_chip, "wid", 2))

    weights = [gate_weight, up_weight]
    mine_1, theirs_1 = gate_up(where, [own, near], weights, both[1], [])
    mine_0, theirs_0 = gate_up(where, [own, near, far_own, far], early, [], [mine_1])
    to_chip_1, sum_1 = reduce(mine_1, swap(theirs_1, "wid", 1))
    to_chip_0, sum_0 = reduce(mine_0, swap(theirs_0, "wid", 1))
    mine_2, theirs_2 = gate_up(where, [own, near], weights, both[2], [to_chip_1, to_chip_0])
    theirs_2 = later(theirs_2, [sum_1[2], sum_0[2]])
    _, sum_2 = reduce(mine_2, swap(theirs_2, "wid", 1))

    (first,) = combine([sum_1], [], [])
    first, give = combine([sum_0], [first], [])
    second = swap(give, "rep", 1)
    (third,) = combine([sum_2], [], [])
    static = [[(0, *segment) for segment in segments] for segments in both]
    acc, behind = None, [second]
    for hidden, segments in (
        (first, static[1] + [(1, 0, bounds[1])]),
        (second, [(-1, half, bounds[1])]),
        (third, static[2]),
    ):
        other = swap(hidden, "wid", 2)
        pieces = [hidden, other, swap(hidden, "wid", 1), swap(join([other], behind), "wid", 1)]
        acc = down(where, pieces, down_weight, acc, segments, hidden is third)
        behind = [acc]

    mixed = acc[0].astype(f32)
    for d in (3, 2, 1):
        mixed = mixed + swap(acc[d], "hid", d).astype(f32)
    return mixed.astype(bf16)


def solution(mesh):
    n_rep, n_hid, n_wid = (mesh.shape[a] for a in ("rep", "hid", "wid"))

    def on_device(tokens, gate_weight, up_weight, down_weight):
        fits = (
            (n_rep, n_hid, n_wid) == (2, 4, 4)
            and gate_weight.shape[1] == n_rep * sum(CHUNKS) * TILE
            and tokens.shape[0] == ROWS
        )
        if not fits:
            return plain(tokens, gate_weight, up_weight, down_weight)
        return split_by_rep(tokens, gate_weight, up_weight, down_weight)

    return jax.shard_map(
        on_device,
        mesh=mesh,
        in_specs=(P(("rep", "hid"), "wid"), P("wid", "hid"), P("wid", "hid"), P("hid", "wid")),
        out_specs=P(("rep", "hid"), "wid"),
        check_vma=False,
    )
```

```python
import functools

import jax
import jax.numpy as jnp
from jax import lax
from jax.experimental import pallas as pl
from jax.experimental.pallas import tpu as pltpu
from jax.sharding import PartitionSpec as P

TILE = 256
LAST = 3
ROWS = 16
COST = pl.CostEstimate(flops=0, bytes_accessed=1024, transcendentals=0)


def plain(tokens, gate_weight, up_weight, down_weight):
    piece = lax.all_gather(tokens, "hid", axis=0, tiled=True)
    gate_rows = jnp.dot(piece, gate_weight, preferred_element_type=jnp.float32)
    up_rows = jnp.dot(piece, up_weight, preferred_element_type=jnp.float32)
    partial_terms = jnp.stack([gate_rows, up_rows], 0)
    summed = lax.psum(partial_terms.astype(jnp.bfloat16), "wid").astype(jnp.float32)
    hidden = (jax.nn.silu(summed[0]) * summed[1]).astype(jnp.bfloat16)
    return lax.psum_scatter(
        jnp.dot(hidden, down_weight, preferred_element_type=jnp.float32).astype(jnp.bfloat16),
        "hid",
        scatter_dimension=0,
        tiled=True,
    )


def pieces_of(width, most):
    first = width % most
    edges = ([0] if first else []) + list(range(first, width + 1, most))
    return list(zip(edges[:-1], edges[1:]))


def place(wid, d):
    step = wid ^ d
    return (step % 2) * 2 + step // 2


def spec(space):
    return pl.BlockSpec(memory_space=space)


def params(mib):
    return pltpu.CompilerParams(vmem_limit_bytes=mib * 2**20)


def column_copies(source_ref, out_ref, segments, sems):
    copies, cuts, at = [], [], 0
    for start, width in segments:
        for a, b in pieces_of(width, 2 * TILE):
            source = source_ref.at[:, pl.ds(pl.multiple_of(start + a, TILE), b - a)]
            copies.append(pltpu.make_async_copy(source, out_ref.at[:, at + a : at + b], sems.at[len(copies)]))
            cuts.append((at + a, at + b))
        at += width
    return copies, cuts


def fetch_kernel(first, where, gate_ref, up_ref, tokens_ref, gate_out, up_out, tokens_out, sems):
    copies = [pltpu.make_async_copy(tokens_ref, tokens_out, sems.at[2, 0])]
    for k, (source, out) in enumerate(((gate_ref, gate_out), (up_ref, up_out))):
        copies += column_copies(source, out, [(where[0] + first, out.shape[1])], sems.at[k])[0]
    for copy in copies:
        copy.start()
    for copy in copies:
        copy.wait()


def fetch(where, gate, up, tokens, first, width):
    depth = gate.shape[0]
    return pl.pallas_call(
        functools.partial(fetch_kernel, first),
        in_specs=[spec(pltpu.SMEM)] + [spec(pltpu.HBM)] * 3,
        out_specs=[spec(pltpu.VMEM)] * 3,
        out_shape=[pltpu.VMEM(x, jnp.bfloat16) for x in ((depth, width), (depth, width), tokens.shape)],
        scratch_shapes=[pltpu.SemaphoreType.DMA((3, len(pieces_of(width, 2 * TILE))))],
        compiler_params=params(1),
        cost_estimate=COST,
        name="fetch",
    )(where, gate, up, tokens)


def join_kernel(n, first, *refs):
    out_ref, at = refs[-1], 0
    for ref in refs[:n]:
        out_ref[at : at + ref.shape[0], :] = ref[:, first : first + out_ref.shape[1]]
        at += ref.shape[0]


def join(arrays, behind, first=0, width=None):
    rows, width = sum(a.shape[0] for a in arrays), width or arrays[0].shape[1]
    return pl.pallas_call(
        functools.partial(join_kernel, len(arrays), first),
        in_specs=[spec(pltpu.VMEM)] * len(arrays) + [spec(pl.ANY)] * len(behind),
        out_specs=spec(pltpu.VMEM),
        out_shape=jax.ShapeDtypeStruct((rows, width), arrays[0].dtype),
        compiler_params=params(1),
        cost_estimate=COST,
        name="join",
    )(*arrays, *behind)


def gate_up_kernel(n_arrays, n_pairs, segments, where, *refs):
    arrays, weights = refs[:n_arrays], refs[n_arrays : n_arrays + 2 * n_pairs]
    if segments:
        mine_ref, theirs_ref, x_ref, w_ref, sems = refs[-5:]
        copies = [column_copies(weights[k], w_ref.at[k], segments, sems.at[k]) for k in range(2)]
        cuts = copies[0][1]
        for i in range(len(cuts)):
            for k in range(2):
                copies[k][0][i].start()
    else:
        mine_ref, theirs_ref, x_ref = refs[-3:]
        step = weights[0].shape[1]
        cuts = [(p * step + a, p * step + b) for p in range(n_pairs) for a, b in pieces_of(step, 2 * TILE)]
    per = x_ref.shape[0] // (4 * ROWS)
    b = 0
    for array in arrays:
        for at in range(0, array.shape[0], ROWS):
            to = (place(where[1], b % 4) * per + b // 4) * ROWS
            x_ref[pl.ds(pl.multiple_of(to, ROWS), ROWS), :] = array[at : at + ROWS, :]
            b += 1
    half = x_ref.shape[0] // 2
    for i, (a, b) in enumerate(cuts):
        for k in range(2):
            if segments:
                copies[k][0][i].wait()
                weight = w_ref[k, :, a:b]
            else:
                p = a // step
                weight = weights[2 * p + k][:, a - p * step : b - p * step]
            part = jnp.dot(x_ref[...], weight, preferred_element_type=jnp.float32).astype(jnp.bfloat16)
            mine_ref[k, :, a:b] = part[:half]
            theirs_ref[k, :, a:b] = part[half:]


def gate_up(where, arrays, weights, segments, behind):
    depth = weights[0].shape[0]
    width = sum(w for _, w in segments) if segments else sum(w.shape[1] for w in weights[::2])
    total = sum(a.shape[0] for a in arrays)
    scratch = [pltpu.VMEM((total, depth), jnp.bfloat16)]
    if segments:
        n_cuts = sum(len(pieces_of(w, 2 * TILE)) for _, w in segments)
        scratch.append(pltpu.VMEM((2, depth, width), jnp.bfloat16))
        scratch.append(pltpu.SemaphoreType.DMA((2, n_cuts)))
    return pl.pallas_call(
        functools.partial(gate_up_kernel, len(arrays), len(weights) // 2, segments),
        in_specs=[spec(pltpu.SMEM)]
        + [spec(pltpu.VMEM)] * len(arrays)
        + [spec(pltpu.HBM if segments else pltpu.VMEM)] * len(weights)
        + [spec(pl.ANY)] * len(behind),
        out_specs=[spec(pltpu.VMEM)] * 2,
        scratch_shapes=scratch,
        out_shape=[jax.ShapeDtypeStruct((2, total // 2, width), jnp.bfloat16)] * 2,
        compiler_params=params(16 if segments else 4),
        cost_estimate=COST,
        name="gate_up",
    )(where, *arrays, *weights, *behind)


def pair_sum_kernel(n_outs, mine_ref, got_ref, *refs):
    outs = refs[-n_outs:]
    rows = mine_ref.shape[1] // 2
    for k in range(2):
        total = mine_ref[k, rows:].astype(jnp.float32) + got_ref[k, rows:].astype(jnp.float32)
        if n_outs == 1:
            outs[0][k] = total.astype(jnp.bfloat16)
        else:
            outs[k][...] = total.astype(jnp.bfloat16)


def pair_sum(mine, got, apart, behind):
    _, rows, width = mine.shape
    shapes = [(rows // 2, width)] * 2 if apart else [(2, rows // 2, width)]
    return pl.pallas_call(
        functools.partial(pair_sum_kernel, len(shapes)),
        in_specs=[spec(pltpu.VMEM)] * 2 + [spec(pl.ANY)] * len(behind),
        out_specs=[spec(pltpu.VMEM)] * len(shapes),
        out_shape=[jax.ShapeDtypeStruct(x, mine.dtype) for x in shapes],
        compiler_params=params(2),
        cost_estimate=COST,
        name="pair_sum",
    )(mine, got, *behind)


def later_kernel(array_ref, *refs):
    refs[-1][...] = array_ref[...]


def later(array, behind):
    return pl.pallas_call(
        later_kernel,
        in_specs=[spec(pltpu.VMEM)] + [spec(pl.ANY)] * len(behind),
        out_specs=spec(pltpu.VMEM),
        out_shape=jax.ShapeDtypeStruct(array.shape, array.dtype),
        compiler_params=params(1),
        cost_estimate=COST,
        name="later",
    )(array, *behind)


def add_kernel(left_ref, right_ref, out_ref):
    out_ref[...] = left_ref[...].astype(jnp.float32) + right_ref[...].astype(jnp.float32)


def add(left, right):
    return pl.pallas_call(
        add_kernel,
        in_specs=[spec(pltpu.VMEM)] * 2,
        out_specs=spec(pltpu.VMEM),
        out_shape=jax.ShapeDtypeStruct(left.shape, jnp.float32),
        compiler_params=params(1),
        cost_estimate=COST,
        name="add",
    )(left, right)


def combine_kernel(n_chips, n_left, n_outs, mine_ref, got_ref, *refs):
    chips, refs, outs = refs[:n_chips], refs[n_chips:], refs[-n_outs:]
    rows, first = mine_ref.shape[1] // 2, 0
    for left in refs[:n_left]:
        first = left.shape[1]
        outs[0][:, :first] = left[...]
    for a, b in pieces_of(mine_ref.shape[2], TILE):
        gate, up = (
            mine_ref[k, :rows, a:b].astype(jnp.float32)
            + got_ref[k, :rows, a:b].astype(jnp.float32)
            + (chips[k][:, a:b] if n_chips == 2 else chips[0][k, :, a:b]).astype(jnp.float32)
            for k in range(2)
        )
        hidden = (gate / (1 + jnp.exp(-gate)) * up).astype(jnp.bfloat16)
        for i, out in enumerate(outs):
            out[:, first + a : first + b] = hidden[i * ROWS : (i + 1) * ROWS]


def combine(mine, got, from_chips, left, behind):
    _, rows, width = mine.shape
    n_outs = rows // (2 * ROWS)
    width += sum(x.shape[1] for x in left)
    return pl.pallas_call(
        functools.partial(combine_kernel, len(from_chips), len(left), n_outs),
        in_specs=[spec(pltpu.VMEM)] * (2 + len(from_chips) + len(left)) + [spec(pl.ANY)] * len(behind),
        out_specs=[spec(pltpu.VMEM)] * n_outs,
        out_shape=[jax.ShapeDtypeStruct((ROWS, width), jnp.bfloat16)] * n_outs,
        compiler_params=params(2),
        cost_estimate=COST,
        name="combine",
    )(mine, got, *from_chips, *left, *behind)


def down_kernel(n_pieces, has_acc, last, segments, where, *refs):
    pieces, refs = refs[:n_pieces], refs[n_pieces:]
    down_ref, refs = refs[0], refs[1:]
    prev_ref, refs = (refs[0], refs[1:]) if has_acc else (None, refs)
    outs, (acc_ref, lhs_ref) = refs[:-2], refs[-2:]
    at = 0
    for piece in pieces:
        lhs_ref[at : at + piece.shape[0], :] = piece[...]
        at += piece.shape[0]
    for a, b in pieces_of(down_ref.shape[1], 2 * TILE):
        part = prev_ref[:, a:b] if has_acc else 0.0
        at = 0
        for sign, start, depth in segments:
            rows = pl.ds(pl.multiple_of(sign * where[0] + start, TILE) if sign else start, depth)
            part += jnp.dot(lhs_ref[:, at : at + depth], down_ref[rows, a:b], preferred_element_type=jnp.float32)
            at += depth
        acc_ref[:, a:b] = part
    if last:
        for d, out in enumerate(outs):
            source = pl.multiple_of(place(where[1], d) * ROWS, ROWS)
            out[...] = acc_ref[pl.ds(source, ROWS), :].astype(out.dtype)


def down(where, pieces, down_weight, prev, segments, last):
    width = down_weight.shape[1]
    total = 4 * ROWS
    args = [*pieces, down_weight] + ([] if prev is None else [prev])
    sums = jax.ShapeDtypeStruct((total, width), jnp.float32)
    scratch = [pltpu.VMEM((total, pieces[0].shape[1]), jnp.bfloat16)]
    if last:
        scratch = [pltpu.VMEM(sums.shape, sums.dtype)] + scratch
    return pl.pallas_call(
        functools.partial(down_kernel, len(pieces), prev is not None, last, segments),
        in_specs=[spec(pltpu.SMEM)] + [spec(pltpu.VMEM)] * len(args),
        out_specs=[spec(pltpu.VMEM)] * 4 if last else spec(pltpu.VMEM),
        scratch_shapes=scratch,
        out_shape=[jax.ShapeDtypeStruct((ROWS, width), jnp.bfloat16)] * 4 if last else sums,
        compiler_params=params(4),
        cost_estimate=COST,
        name="down",
    )(where, *args)


def split_by_rep(tokens, gate_weight, up_weight, down_weight):
    rep, wid = lax.axis_index("rep"), lax.axis_index("wid")
    f32, bf16 = jnp.float32, jnp.bfloat16
    half = gate_weight.shape[1] // 2
    where = jnp.stack([rep * half, wid]).astype(jnp.int32)

    def swap(x, axis, step):
        n = {"rep": 2, "hid": 4, "wid": 4}[axis]
        return lax.ppermute(x, axis, [(i, i ^ step) for i in range(n)])

    tiles = half // TILE
    bounds = [0, (tiles - LAST) // 2 * TILE, (tiles - LAST) * TILE, half]
    widths = [b - a for a, b in zip(bounds[:-1], bounds[1:])]
    gate_weight, up_weight, hbm_tokens = (
        pltpu.with_memory_space_constraint(w, pltpu.HBM) for w in (gate_weight, up_weight, tokens)
    )
    down_weight = pltpu.with_memory_space_constraint(down_weight, pltpu.VMEM)

    far_own = swap(tokens, "rep", 1)
    by_hid = [swap(tokens, "hid", d) for d in (3, 2, 1)][::-1]
    early = [fetch(where, gate_weight, up_weight, hbm_tokens, bounds[c], widths[c]) for c in range(2)]
    own = early[0][2]
    near = join(by_hid, [own, far_own])
    far = swap(near, "rep", 1)

    weights = [w for fetched in early for w in fetched[:2]]
    mine, theirs = gate_up(where, [own, near, far_own, far], weights, [], [])
    got = swap(theirs, "wid", 1)
    (to_chip,) = pair_sum(mine, got, False, [])
    from_chip = swap(to_chip, "wid", 2)
    segments = [(bounds[2], widths[2]), (half + bounds[2], widths[2])]
    last_mine, theirs = gate_up(where, [own, near], [gate_weight, up_weight], segments, [to_chip])
    last_got = swap(theirs, "wid", 1)

    keep, give = combine(mine, got, [from_chip], [], [])
    far_columns = swap(give, "rep", 1)
    last_from_chip = [swap(x, "wid", 2) for x in pair_sum(last_mine, last_got, True, [give])]
    (rest,) = combine(last_mine, last_got, last_from_chip, [far_columns], [])
    rest_segments = [(-1, half, bounds[2])] + [(0, start, width) for start, width in segments]
    acc, behind = None, [rest]
    for hidden, parts in ((keep, [(1, 0, bounds[2])]), (rest, rest_segments)):
        other = swap(hidden, "wid", 2)
        pieces = [hidden, other, swap(hidden, "wid", 1), swap(join([other], behind), "wid", 1)]
        acc = down(where, pieces, down_weight, acc, parts, hidden is rest)
        behind = [acc]

    via = (acc[2].astype(f32) + swap(acc[3], "hid", 1).astype(f32)).astype(bf16)
    mixed = add(acc[0], swap(via, "hid", 2))
    mixed = mixed + swap(later(acc[1], [via]), "hid", 1).astype(f32)
    return mixed.astype(bf16)


def solution(mesh):
    n_rep, n_hid, n_wid = (mesh.shape[a] for a in ("rep", "hid", "wid"))

    def on_device(tokens, gate_weight, up_weight, down_weight):
        fits = (
            (n_rep, n_hid, n_wid) == (2, 4, 4)
            and gate_weight.shape[1] % (n_rep * TILE) == 0
            and tokens.shape[0] == ROWS
        )
        if not fits:
            return plain(tokens, gate_weight, up_weight, down_weight)
        return split_by_rep(tokens, gate_weight, up_weight, down_weight)

    return jax.shard_map(
        on_device,
        mesh=mesh,
        in_specs=(P(("rep", "hid"), "wid"), P("wid", "hid"), P("wid", "hid"), P("hid", "wid")),
        out_specs=P(("rep", "hid"), "wid"),
        check_vma=False,
    )
```

```python
import functools

import jax
import jax.numpy as jnp
from jax import lax
from jax.experimental import pallas as pl
from jax.experimental.pallas import tpu as pltpu
from jax.sharding import PartitionSpec as P

TILE = 256
LAST = 3
ROWS = 16
COST = pl.CostEstimate(flops=0, bytes_accessed=1024, transcendentals=0)


def plain(tokens, gate_weight, up_weight, down_weight):
    piece = lax.all_gather(tokens, "hid", axis=0, tiled=True)
    gate_rows = jnp.dot(piece, gate_weight, preferred_element_type=jnp.float32)
    up_rows = jnp.dot(piece, up_weight, preferred_element_type=jnp.float32)
    partial_terms = jnp.stack([gate_rows, up_rows], 0)
    summed = lax.psum(partial_terms.astype(jnp.bfloat16), "wid").astype(jnp.float32)
    hidden = (jax.nn.silu(summed[0]) * summed[1]).astype(jnp.bfloat16)
    return lax.psum_scatter(
        jnp.dot(hidden, down_weight, preferred_element_type=jnp.float32).astype(jnp.bfloat16),
        "hid",
        scatter_dimension=0,
        tiled=True,
    )


def pieces_of(width, most):
    first = width % most
    edges = ([0] if first else []) + list(range(first, width + 1, most))
    return list(zip(edges[:-1], edges[1:]))


def place(wid, d):
    step = wid ^ d
    return (step % 2) * 2 + step // 2


def spec(space):
    return pl.BlockSpec(memory_space=space)


def params(mib):
    return pltpu.CompilerParams(vmem_limit_bytes=mib * 2**20)


def column_copies(source_ref, out_ref, segments, sems):
    copies, cuts, at = [], [], 0
    for start, width in segments:
        for a, b in pieces_of(width, 2 * TILE):
            source = source_ref.at[:, pl.ds(pl.multiple_of(start + a, TILE), b - a)]
            copies.append(pltpu.make_async_copy(source, out_ref.at[:, at + a : at + b], sems.at[len(copies)]))
            cuts.append((at + a, at + b))
        at += width
    return copies, cuts


def fetch_kernel(first, where, gate_ref, up_ref, tokens_ref, gate_out, up_out, tokens_out, sems):
    copies = [pltpu.make_async_copy(tokens_ref, tokens_out, sems.at[2, 0])]
    for k, (source, out) in enumerate(((gate_ref, gate_out), (up_ref, up_out))):
        copies += column_copies(source, out, [(where[0] + first, out.shape[1])], sems.at[k])[0]
    for copy in copies:
        copy.start()
    for copy in copies:
        copy.wait()


def fetch(where, gate, up, tokens, first, width):
    depth = gate.shape[0]
    return pl.pallas_call(
        functools.partial(fetch_kernel, first),
        in_specs=[spec(pltpu.SMEM)] + [spec(pltpu.HBM)] * 3,
        out_specs=[spec(pltpu.VMEM)] * 3,
        out_shape=[pltpu.VMEM(x, jnp.bfloat16) for x in ((depth, width), (depth, width), tokens.shape)],
        scratch_shapes=[pltpu.SemaphoreType.DMA((3, len(pieces_of(width, 2 * TILE))))],
        compiler_params=params(1),
        cost_estimate=COST,
        name="fetch",
    )(where, gate, up, tokens)


def join_kernel(n, first, *refs):
    out_ref, at = refs[-1], 0
    for ref in refs[:n]:
        out_ref[at : at + ref.shape[0], :] = ref[:, first : first + out_ref.shape[1]]
        at += ref.shape[0]


def join(arrays, behind, first=0, width=None):
    rows, width = sum(a.shape[0] for a in arrays), width or arrays[0].shape[1]
    return pl.pallas_call(
        functools.partial(join_kernel, len(arrays), first),
        in_specs=[spec(pltpu.VMEM)] * len(arrays) + [spec(pl.ANY)] * len(behind),
        out_specs=spec(pltpu.VMEM),
        out_shape=jax.ShapeDtypeStruct((rows, width), arrays[0].dtype),
        compiler_params=params(1),
        cost_estimate=COST,
        name="join",
    )(*arrays, *behind)


def gate_up_kernel(n_arrays, n_pairs, n_parts, segments, where, *refs):
    arrays, weights = refs[:n_arrays], refs[n_arrays : n_arrays + 2 * n_pairs]
    if segments:
        refs, (w_ref, sems) = refs[:-2], refs[-2:]
    mine_ref, theirs, x_ref = refs[-n_parts - 2], refs[-n_parts - 1 : -1], refs[-1]
    if segments:
        copies = [column_copies(weights[k], w_ref.at[k], segments, sems.at[k]) for k in range(2)]
        cuts = copies[0][1]
        for i in range(len(cuts)):
            for k in range(2):
                copies[k][0][i].start()
    else:
        step = weights[0].shape[1]
        cuts = [(p * step + a, p * step + b) for p in range(n_pairs) for a, b in pieces_of(step, 2 * TILE)]
    per = x_ref.shape[0] // (4 * ROWS)
    b = 0
    for array in arrays:
        for at in range(0, array.shape[0], ROWS):
            to = (place(where[1], b % 4) * per + b // 4) * ROWS
            x_ref[pl.ds(pl.multiple_of(to, ROWS), ROWS), :] = array[at : at + ROWS, :]
            b += 1
    half = x_ref.shape[0] // 2
    for i, (a, b) in enumerate(cuts):
        for k in range(2):
            if segments:
                copies[k][0][i].wait()
                weight = w_ref[k, :, a:b]
            else:
                p = a // step
                weight = weights[2 * p + k][:, a - p * step : b - p * step]
            part = jnp.dot(x_ref[...], weight, preferred_element_type=jnp.float32).astype(jnp.bfloat16)
            mine_ref[k, :, a:b] = part[:half]
            part_width = theirs[0].shape[2]
            i_part = a // part_width
            theirs[i_part][k, :, a - i_part * part_width : b - i_part * part_width] = part[half:]


def gate_up(where, arrays, weights, segments, n_parts, behind):
    depth = weights[0].shape[0]
    width = sum(w for _, w in segments) if segments else sum(w.shape[1] for w in weights[::2])
    total = sum(a.shape[0] for a in arrays)
    scratch = [pltpu.VMEM((total, depth), jnp.bfloat16)]
    if segments:
        n_cuts = sum(len(pieces_of(w, 2 * TILE)) for _, w in segments)
        scratch.append(pltpu.VMEM((2, depth, width), jnp.bfloat16))
        scratch.append(pltpu.SemaphoreType.DMA((2, n_cuts)))
    return pl.pallas_call(
        functools.partial(gate_up_kernel, len(arrays), len(weights) // 2, n_parts, segments),
        in_specs=[spec(pltpu.SMEM)]
        + [spec(pltpu.VMEM)] * len(arrays)
        + [spec(pltpu.HBM if segments else pltpu.VMEM)] * len(weights)
        + [spec(pl.ANY)] * len(behind),
        out_specs=[spec(pltpu.VMEM)] * (1 + n_parts),
        scratch_shapes=scratch,
        out_shape=[jax.ShapeDtypeStruct((2, total // 2, w), jnp.bfloat16) for w in [width] + [width // n_parts] * n_parts],
        compiler_params=params(16 if segments else 4),
        cost_estimate=COST,
        name="gate_up",
    )(where, *arrays, *weights, *behind)


def pair_sum_kernel(first, mine_ref, got_ref, out_ref):
    rows, width = out_ref.shape[1:]
    for k in range(2):
        mine = mine_ref[k, rows:, first : first + width].astype(jnp.float32)
        out_ref[k] = (mine + got_ref[k, rows:].astype(jnp.float32)).astype(out_ref.dtype)


def pair_sum(mine, got, first):
    _, rows, width = got.shape
    return pl.pallas_call(
        functools.partial(pair_sum_kernel, first),
        in_specs=[spec(pltpu.VMEM)] * 2,
        out_specs=spec(pltpu.VMEM),
        out_shape=jax.ShapeDtypeStruct((2, rows // 2, width), mine.dtype),
        compiler_params=params(2),
        cost_estimate=COST,
        name="pair_sum",
    )(mine, got)


def later_kernel(array_ref, *refs):
    refs[-1][...] = array_ref[...]


def later(array, behind):
    return pl.pallas_call(
        later_kernel,
        in_specs=[spec(pltpu.VMEM)] + [spec(pl.ANY)] * len(behind),
        out_specs=spec(pltpu.VMEM),
        out_shape=jax.ShapeDtypeStruct(array.shape, array.dtype),
        compiler_params=params(1),
        cost_estimate=COST,
        name="later",
    )(array, *behind)


def combine_kernel(n_left, n_parts, n_outs, mine_ref, *refs):
    lefts, refs, outs = refs[:n_left], refs[n_left:], refs[-n_outs:]
    first = 0
    for left in lefts:
        first = left.shape[1]
        outs[0][:, :first] = left[...]
    at = 0
    for got_ref, chip_ref in zip(refs[:n_parts], refs[n_parts : 2 * n_parts]):
        _, rows, width = chip_ref.shape
        for a, b in pieces_of(width, TILE):
            gate, up = (
                mine_ref[k, :rows, at + a : at + b].astype(jnp.float32)
                + got_ref[k, :rows, a:b].astype(jnp.float32)
                + chip_ref[k, :, a:b].astype(jnp.float32)
                for k in range(2)
            )
            hidden = (gate / (1 + jnp.exp(-gate)) * up).astype(jnp.bfloat16)
            for i, out in enumerate(outs):
                out[:, first + at + a : first + at + b] = hidden[i * ROWS : (i + 1) * ROWS]
        at += width


def combine(mine, gots, from_chips, left):
    _, rows, width = mine.shape
    n_outs = rows // (2 * ROWS)
    width += sum(x.shape[1] for x in left)
    args = [mine, *left, *gots, *from_chips]
    return pl.pallas_call(
        functools.partial(combine_kernel, len(left), len(gots), n_outs),
        in_specs=[spec(pltpu.VMEM)] * len(args),
        out_specs=[spec(pltpu.VMEM)] * n_outs,
        out_shape=[jax.ShapeDtypeStruct((ROWS, width), jnp.bfloat16)] * n_outs,
        compiler_params=params(2),
        cost_estimate=COST,
        name="combine",
    )(*args)


def down_kernel(n_pieces, has_acc, last, segments, where, *refs):
    pieces, refs = refs[:n_pieces], refs[n_pieces:]
    down_ref, refs = refs[0], refs[1:]
    prev_ref, refs = (refs[0], refs[1:]) if has_acc else (None, refs)
    outs, (acc_ref, lhs_ref) = refs[:-2], refs[-2:]
    at = 0
    for piece in pieces:
        lhs_ref[at : at + piece.shape[0], :] = piece[...]
        at += piece.shape[0]
    for a, b in pieces_of(down_ref.shape[1], 4 * TILE):
        part = prev_ref[:, a:b] if has_acc else 0.0
        at = 0
        for sign, start, depth in segments:
            rows = pl.ds(pl.multiple_of(sign * where[0] + start, TILE) if sign else start, depth)
            part += jnp.dot(lhs_ref[:, at : at + depth], down_ref[rows, a:b], preferred_element_type=jnp.float32)
            at += depth
        acc_ref[:, a:b] = part
    if last:
        for d, out in enumerate(outs):
            source = pl.multiple_of(place(where[1], d) * ROWS, ROWS)
            out[...] = acc_ref[pl.ds(source, ROWS), :].astype(out.dtype)


def down(where, pieces, down_weight, prev, segments, last):
    width = down_weight.shape[1]
    total = 4 * ROWS
    args = [*pieces, down_weight] + ([] if prev is None else [prev])
    sums = jax.ShapeDtypeStruct((total, width), jnp.float32)
    scratch = [pltpu.VMEM((total, pieces[0].shape[1]), jnp.bfloat16)]
    if last:
        scratch = [pltpu.VMEM(sums.shape, sums.dtype)] + scratch
    return pl.pallas_call(
        functools.partial(down_kernel, len(pieces), prev is not None, last, segments),
        in_specs=[spec(pltpu.SMEM)] + [spec(pltpu.VMEM)] * len(args),
        out_specs=[spec(pltpu.VMEM)] * 4 if last else spec(pltpu.VMEM),
        scratch_shapes=scratch,
        out_shape=[jax.ShapeDtypeStruct((ROWS, width), jnp.bfloat16)] * 4 if last else sums,
        compiler_params=params(4),
        cost_estimate=COST,
        name="down",
    )(where, *args)


def split_by_rep(tokens, gate_weight, up_weight, down_weight):
    rep, wid = lax.axis_index("rep"), lax.axis_index("wid")
    f32, bf16 = jnp.float32, jnp.bfloat16
    half = gate_weight.shape[1] // 2
    where = jnp.stack([rep * half, wid]).astype(jnp.int32)

    def swap(x, axis, step):
        n = {"rep": 2, "hid": 4, "wid": 4}[axis]
        return lax.ppermute(x, axis, [(i, i ^ step) for i in range(n)])

    tiles = half // TILE
    bounds = [0, (tiles - LAST) // 2 * TILE, (tiles - LAST) * TILE, half]
    widths = [b - a for a, b in zip(bounds[:-1], bounds[1:])]
    gate_weight, up_weight, hbm_tokens = (
        pltpu.with_memory_space_constraint(w, pltpu.HBM) for w in (gate_weight, up_weight, tokens)
    )
    down_weight = pltpu.with_memory_space_constraint(down_weight, pltpu.VMEM)

    far_own = swap(tokens, "rep", 1)
    by_hid = [swap(tokens, "hid", d) for d in (3, 2, 1)][::-1]
    early = [fetch(where, gate_weight, up_weight, hbm_tokens, bounds[c], widths[c]) for c in range(2)]
    own = early[0][2]
    near = join(by_hid, [own, far_own])
    far = swap(near, "rep", 1)

    weights = [w for fetched in early for w in fetched[:2]]
    mine, *theirs = gate_up(where, [own, near, far_own, far], weights, [], 2, [])
    gots = [swap(x, "wid", 1) for x in theirs]
    to_chips = [pair_sum(mine, got, first) for got, first in zip(gots, bounds)]
    from_chips = [swap(x, "wid", 2) for x in to_chips]
    segments = [(bounds[2], widths[2]), (half + bounds[2], widths[2])]
    last_mine, theirs = gate_up(where, [own, near], [gate_weight, up_weight], segments, 1, to_chips)
    last_got = swap(later(theirs, from_chips), "wid", 1)
    last_from_chip = swap(pair_sum(last_mine, last_got, 0), "wid", 2)

    keep, give = combine(mine, gots, from_chips, [])
    far_columns = swap(give, "rep", 1)
    (rest,) = combine(last_mine, [last_got], [last_from_chip], [far_columns])
    rest_segments = [(-1, half, bounds[2])] + [(0, start, width) for start, width in segments]

    other = swap(keep, "wid", 2)
    pieces = [keep, other, swap(join([keep, other], []), "wid", 1)]
    acc = down(where, pieces, down_weight, None, [(1, 0, bounds[2])], False)
    other = swap(rest, "wid", 2)
    pieces = [rest, other, swap(rest, "wid", 1), swap(join([other], [acc]), "wid", 1)]
    acc = down(where, pieces, down_weight, acc, rest_segments, True)

    mixed = acc[0].astype(f32)
    for d in (3, 2, 1):
        mixed = mixed + swap(acc[d], "hid", d).astype(f32)
    return mixed.astype(bf16)


def solution(mesh):
    n_rep, n_hid, n_wid = (mesh.shape[a] for a in ("rep", "hid", "wid"))

    def on_device(tokens, gate_weight, up_weight, down_weight):
        fits = (
            (n_rep, n_hid, n_wid) == (2, 4, 4)
            and gate_weight.shape[1] % (n_rep * TILE) == 0
            and tokens.shape[0] == ROWS
        )
        if not fits:
            return plain(tokens, gate_weight, up_weight, down_weight)
        return split_by_rep(tokens, gate_weight, up_weight, down_weight)

    return jax.shard_map(
        on_device,
        mesh=mesh,
        in_specs=(P(("rep", "hid"), "wid"), P("wid", "hid"), P("wid", "hid"), P("hid", "wid")),
        out_specs=P(("rep", "hid"), "wid"),
        check_vma=False,
    )
```

```python
import functools

import jax
import jax.numpy as jnp
from jax import lax
from jax.experimental import pallas as pl
from jax.experimental.pallas import tpu as pltpu
from jax.sharding import PartitionSpec as P

TILE = 256
LAST = 3
ROWS = 16
COST = pl.CostEstimate(flops=0, bytes_accessed=1024, transcendentals=0)


def plain(tokens, gate_weight, up_weight, down_weight):
    piece = lax.all_gather(tokens, "hid", axis=0, tiled=True)
    gate_rows = jnp.dot(piece, gate_weight, preferred_element_type=jnp.float32)
    up_rows = jnp.dot(piece, up_weight, preferred_element_type=jnp.float32)
    partial_terms = jnp.stack([gate_rows, up_rows], 0)
    summed = lax.psum(partial_terms.astype(jnp.bfloat16), "wid").astype(jnp.float32)
    hidden = (jax.nn.silu(summed[0]) * summed[1]).astype(jnp.bfloat16)
    return lax.psum_scatter(
        jnp.dot(hidden, down_weight, preferred_element_type=jnp.float32).astype(jnp.bfloat16),
        "hid",
        scatter_dimension=0,
        tiled=True,
    )


def pieces_of(width, most):
    first = width % most
    edges = ([0] if first else []) + list(range(first, width + 1, most))
    return list(zip(edges[:-1], edges[1:]))


def place(wid, d):
    step = wid ^ d
    return (step % 2) * 2 + step // 2


def spec(space):
    return pl.BlockSpec(memory_space=space)


def params(mib):
    return pltpu.CompilerParams(vmem_limit_bytes=mib * 2**20)


def column_copies(source_ref, out_ref, segments, sems):
    copies, cuts, at = [], [], 0
    for start, width in segments:
        for a, b in pieces_of(width, 2 * TILE):
            source = source_ref.at[:, pl.ds(pl.multiple_of(start + a, TILE), b - a)]
            copies.append(pltpu.make_async_copy(source, out_ref.at[:, at + a : at + b], sems.at[len(copies)]))
            cuts.append((at + a, at + b))
        at += width
    return copies, cuts


def fetch_kernel(first, where, gate_ref, up_ref, tokens_ref, gate_out, up_out, tokens_out, sems):
    copies = [pltpu.make_async_copy(tokens_ref, tokens_out, sems.at[2, 0])]
    for k, (source, out) in enumerate(((gate_ref, gate_out), (up_ref, up_out))):
        copies += column_copies(source, out, [(where[0] + first, out.shape[1])], sems.at[k])[0]
    for copy in copies:
        copy.start()
    for copy in copies:
        copy.wait()


def fetch(where, gate, up, tokens, first, width):
    depth = gate.shape[0]
    return pl.pallas_call(
        functools.partial(fetch_kernel, first),
        in_specs=[spec(pltpu.SMEM)] + [spec(pltpu.HBM)] * 3,
        out_specs=[spec(pltpu.VMEM)] * 3,
        out_shape=[pltpu.VMEM(x, jnp.bfloat16) for x in ((depth, width), (depth, width), tokens.shape)],
        scratch_shapes=[pltpu.SemaphoreType.DMA((3, len(pieces_of(width, 2 * TILE))))],
        compiler_params=params(1),
        cost_estimate=COST,
        name="fetch",
    )(where, gate, up, tokens)


def join_kernel(n, first, *refs):
    out_ref, at = refs[-1], 0
    for ref in refs[:n]:
        out_ref[at : at + ref.shape[0], :] = ref[:, first : first + out_ref.shape[1]]
        at += ref.shape[0]


def join(arrays, behind, first=0, width=None):
    rows, width = sum(a.shape[0] for a in arrays), width or arrays[0].shape[1]
    return pl.pallas_call(
        functools.partial(join_kernel, len(arrays), first),
        in_specs=[spec(pltpu.VMEM)] * len(arrays) + [spec(pl.ANY)] * len(behind),
        out_specs=spec(pltpu.VMEM),
        out_shape=jax.ShapeDtypeStruct((rows, width), arrays[0].dtype),
        compiler_params=params(1),
        cost_estimate=COST,
        name="join",
    )(*arrays, *behind)


def gate_up_kernel(n_arrays, n_pairs, n_parts, segments, where, *refs):
    arrays, weights = refs[:n_arrays], refs[n_arrays : n_arrays + 2 * n_pairs]
    if segments:
        refs, (w_ref, sems) = refs[:-2], refs[-2:]
    mine_ref, theirs, x_ref = refs[-n_parts - 2], refs[-n_parts - 1 : -1], refs[-1]
    if segments:
        copies = [column_copies(weights[k], w_ref.at[k], segments, sems.at[k]) for k in range(2)]
        cuts = copies[0][1]
        for i in range(len(cuts)):
            for k in range(2):
                copies[k][0][i].start()
    else:
        step = weights[0].shape[1]
        cuts = [(p * step + a, p * step + b) for p in range(n_pairs) for a, b in pieces_of(step, 2 * TILE)]
    per = x_ref.shape[0] // (4 * ROWS)
    b = 0
    for array in arrays:
        for at in range(0, array.shape[0], ROWS):
            to = (place(where[1], b % 4) * per + b // 4) * ROWS
            x_ref[pl.ds(pl.multiple_of(to, ROWS), ROWS), :] = array[at : at + ROWS, :]
            b += 1
    half = x_ref.shape[0] // 2
    for i, (a, b) in enumerate(cuts):
        for k in range(2):
            if segments:
                copies[k][0][i].wait()
                weight = w_ref[k, :, a:b]
            else:
                p = a // step
                weight = weights[2 * p + k][:, a - p * step : b - p * step]
            part = jnp.dot(x_ref[...], weight, preferred_element_type=jnp.float32).astype(jnp.bfloat16)
            mine_ref[k, :, a:b] = part[:half]
            part_width = theirs[0].shape[2]
            i_part = a // part_width
            theirs[i_part][k, :, a - i_part * part_width : b - i_part * part_width] = part[half:]


def gate_up(where, arrays, weights, segments, n_parts, behind):
    depth = weights[0].shape[0]
    width = sum(w for _, w in segments) if segments else sum(w.shape[1] for w in weights[::2])
    total = sum(a.shape[0] for a in arrays)
    scratch = [pltpu.VMEM((total, depth), jnp.bfloat16)]
    if segments:
        n_cuts = sum(len(pieces_of(w, 2 * TILE)) for _, w in segments)
        scratch.append(pltpu.VMEM((2, depth, width), jnp.bfloat16))
        scratch.append(pltpu.SemaphoreType.DMA((2, n_cuts)))
    return pl.pallas_call(
        functools.partial(gate_up_kernel, len(arrays), len(weights) // 2, n_parts, segments),
        in_specs=[spec(pltpu.SMEM)]
        + [spec(pltpu.VMEM)] * len(arrays)
        + [spec(pltpu.HBM if segments else pltpu.VMEM)] * len(weights)
        + [spec(pl.ANY)] * len(behind),
        out_specs=[spec(pltpu.VMEM)] * (1 + n_parts),
        scratch_shapes=scratch,
        out_shape=[jax.ShapeDtypeStruct((2, total // 2, w), jnp.bfloat16) for w in [width] + [width // n_parts] * n_parts],
        compiler_params=params(16 if segments else 4),
        cost_estimate=COST,
        name="gate_up",
    )(where, *arrays, *weights, *behind)


def pair_sum_kernel(first, mine_ref, got_ref, out_ref):
    rows, width = out_ref.shape[1:]
    for k in range(2):
        mine = mine_ref[k, rows:, first : first + width].astype(jnp.float32)
        out_ref[k] = (mine + got_ref[k, rows:].astype(jnp.float32)).astype(out_ref.dtype)


def pair_sum(mine, got, first):
    _, rows, width = got.shape
    return pl.pallas_call(
        functools.partial(pair_sum_kernel, first),
        in_specs=[spec(pltpu.VMEM)] * 2,
        out_specs=spec(pltpu.VMEM),
        out_shape=jax.ShapeDtypeStruct((2, rows // 2, width), mine.dtype),
        compiler_params=params(2),
        cost_estimate=COST,
        name="pair_sum",
    )(mine, got)


def later_kernel(array_ref, *refs):
    refs[-1][...] = array_ref[...]


def later(array, behind):
    return pl.pallas_call(
        later_kernel,
        in_specs=[spec(pltpu.VMEM)] + [spec(pl.ANY)] * len(behind),
        out_specs=spec(pltpu.VMEM),
        out_shape=jax.ShapeDtypeStruct(array.shape, array.dtype),
        compiler_params=params(1),
        cost_estimate=COST,
        name="later",
    )(array, *behind)


def combine_kernel(n_left, n_parts, n_outs, mine_ref, *refs):
    lefts, refs, outs = refs[:n_left], refs[n_left:], refs[-n_outs:]
    first = 0
    for left in lefts:
        first = left.shape[1]
        outs[0][:, :first] = left[...]
    at = 0
    for got_ref, chip_ref in zip(refs[:n_parts], refs[n_parts : 2 * n_parts]):
        _, rows, width = chip_ref.shape
        for a, b in pieces_of(width, TILE):
            gate, up = (
                mine_ref[k, :rows, at + a : at + b].astype(jnp.float32)
                + got_ref[k, :rows, a:b].astype(jnp.float32)
                + chip_ref[k, :, a:b].astype(jnp.float32)
                for k in range(2)
            )
            hidden = (gate / (1 + jnp.exp(-gate)) * up).astype(jnp.bfloat16)
            for i, out in enumerate(outs):
                out[:, first + at + a : first + at + b] = hidden[i * ROWS : (i + 1) * ROWS]
        at += width


def combine(mine, gots, from_chips, left):
    _, rows, width = mine.shape
    n_outs = rows // (2 * ROWS)
    width += sum(x.shape[1] for x in left)
    args = [mine, *left, *gots, *from_chips]
    return pl.pallas_call(
        functools.partial(combine_kernel, len(left), len(gots), n_outs),
        in_specs=[spec(pltpu.VMEM)] * len(args),
        out_specs=[spec(pltpu.VMEM)] * n_outs,
        out_shape=[jax.ShapeDtypeStruct((ROWS, width), jnp.bfloat16)] * n_outs,
        compiler_params=params(2),
        cost_estimate=COST,
        name="combine",
    )(*args)


def down_kernel(n_pieces, has_acc, last, segments, where, *refs):
    pieces, refs = refs[:n_pieces], refs[n_pieces:]
    down_ref, refs = refs[0], refs[1:]
    prev_ref, refs = (refs[0], refs[1:]) if has_acc else (None, refs)
    outs, (acc_ref, lhs_ref) = refs[:-2], refs[-2:]
    at = 0
    for piece in pieces:
        lhs_ref[at : at + piece.shape[0], :] = piece[...]
        at += piece.shape[0]

    @pl.loop(0, down_ref.shape[1] // (2 * TILE))
    def _(i):
        columns = pl.ds(pl.multiple_of(i * 2 * TILE, 2 * TILE), 2 * TILE)
        part = prev_ref[:, columns] if has_acc else 0.0
        at = 0
        for sign, start, depth in segments:
            rows = pl.ds(pl.multiple_of(sign * where[0] + start, TILE) if sign else start, depth)
            part += jnp.dot(lhs_ref[:, at : at + depth], down_ref[rows, columns], preferred_element_type=jnp.float32)
            at += depth
        acc_ref[:, columns] = part

    if last:
        for d, out in enumerate(outs):
            source = pl.multiple_of(place(where[1], d) * ROWS, ROWS)
            out[...] = acc_ref[pl.ds(source, ROWS), :].astype(out.dtype)


def down(where, pieces, down_weight, prev, segments, last):
    width = down_weight.shape[1]
    total = 4 * ROWS
    args = [*pieces, down_weight] + ([] if prev is None else [prev])
    sums = jax.ShapeDtypeStruct((total, width), jnp.float32)
    scratch = [pltpu.VMEM((total, pieces[0].shape[1]), jnp.bfloat16)]
    if last:
        scratch = [pltpu.VMEM(sums.shape, sums.dtype)] + scratch
    return pl.pallas_call(
        functools.partial(down_kernel, len(pieces), prev is not None, last, segments),
        in_specs=[spec(pltpu.SMEM)] + [spec(pltpu.VMEM)] * len(args),
        out_specs=[spec(pltpu.VMEM)] * 4 if last else spec(pltpu.VMEM),
        scratch_shapes=scratch,
        out_shape=[jax.ShapeDtypeStruct((ROWS, width), jnp.bfloat16)] * 4 if last else sums,
        compiler_params=params(4),
        cost_estimate=COST,
        name="down",
    )(where, *args)


def split_by_rep(tokens, gate_weight, up_weight, down_weight):
    rep, wid = lax.axis_index("rep"), lax.axis_index("wid")
    f32, bf16 = jnp.float32, jnp.bfloat16
    half = gate_weight.shape[1] // 2
    where = jnp.stack([rep * half, wid]).astype(jnp.int32)

    def swap(x, axis, step):
        n = {"rep": 2, "hid": 4, "wid": 4}[axis]
        return lax.ppermute(x, axis, [(i, i ^ step) for i in range(n)])

    tiles = half // TILE
    bounds = [0, (tiles - LAST) // 2 * TILE, (tiles - LAST) * TILE, half]
    widths = [b - a for a, b in zip(bounds[:-1], bounds[1:])]
    gate_weight, up_weight, hbm_tokens = (
        pltpu.with_memory_space_constraint(w, pltpu.HBM) for w in (gate_weight, up_weight, tokens)
    )
    down_weight = pltpu.with_memory_space_constraint(down_weight, pltpu.VMEM)

    far_own = swap(tokens, "rep", 1)
    by_hid = [swap(tokens, "hid", d) for d in (3, 2, 1)][::-1]
    early = [fetch(where, gate_weight, up_weight, hbm_tokens, bounds[c], widths[c]) for c in range(2)]
    own = early[0][2]
    near = join(by_hid, [own, far_own])
    far = swap(near, "rep", 1)

    weights = [w for fetched in early for w in fetched[:2]]
    mine, *theirs = gate_up(where, [own, near, far_own, far], weights, [], 2, [])
    gots = [swap(x, "wid", 1) for x in theirs]
    to_chips = [pair_sum(mine, got, first) for got, first in zip(gots, bounds)]
    from_chips = [swap(x, "wid", 2) for x in to_chips]
    segments = [(bounds[2], widths[2]), (half + bounds[2], widths[2])]
    last_mine, theirs = gate_up(where, [own, near], [gate_weight, up_weight], segments, 1, to_chips)
    last_got = swap(later(theirs, from_chips), "wid", 1)
    last_from_chip = swap(pair_sum(last_mine, last_got, 0), "wid", 2)

    keep, give = combine(mine, gots, from_chips, [])
    far_columns = swap(give, "rep", 1)
    (rest,) = combine(last_mine, [last_got], [last_from_chip], [far_columns])
    rest_segments = [(-1, half, bounds[2])] + [(0, start, width) for start, width in segments]

    other = swap(keep, "wid", 2)
    pieces = [keep, other, swap(join([keep, other], []), "wid", 1)]
    acc = down(where, pieces, down_weight, None, [(1, 0, bounds[2])], False)
    other = swap(rest, "wid", 2)
    pieces = [rest, other, swap(rest, "wid", 1), swap(join([other], [acc]), "wid", 1)]
    acc = down(where, pieces, down_weight, acc, rest_segments, True)

    mixed = acc[0].astype(f32)
    for d in (1, 2, 3):
        mixed = mixed + swap(acc[d], "hid", d).astype(f32)
    return mixed.astype(bf16)


def solution(mesh):
    n_rep, n_hid, n_wid = (mesh.shape[a] for a in ("rep", "hid", "wid"))

    def on_device(tokens, gate_weight, up_weight, down_weight):
        fits = (
            (n_rep, n_hid, n_wid) == (2, 4, 4)
            and gate_weight.shape[1] % (n_rep * TILE) == 0
            and tokens.shape[0] == ROWS
        )
        if not fits:
            return plain(tokens, gate_weight, up_weight, down_weight)
        return split_by_rep(tokens, gate_weight, up_weight, down_weight)

    return jax.shard_map(
        on_device,
        mesh=mesh,
        in_specs=(P(("rep", "hid"), "wid"), P("wid", "hid"), P("wid", "hid"), P("hid", "wid")),
        out_specs=P(("rep", "hid"), "wid"),
        check_vma=False,
    )
```

```python
import functools

import jax
import jax.numpy as jnp
from jax import lax
from jax.experimental import pallas as pl
from jax.experimental.pallas import tpu as pltpu
from jax.sharding import PartitionSpec as P

TILE = 256
LAST = 3
ROWS = 16
COST = pl.CostEstimate(flops=0, bytes_accessed=1024, transcendentals=0)


def plain(tokens, gate_weight, up_weight, down_weight):
    piece = lax.all_gather(tokens, "hid", axis=0, tiled=True)
    gate_rows = jnp.dot(piece, gate_weight, preferred_element_type=jnp.float32)
    up_rows = jnp.dot(piece, up_weight, preferred_element_type=jnp.float32)
    partial_terms = jnp.stack([gate_rows, up_rows], 0)
    summed = lax.psum(partial_terms.astype(jnp.bfloat16), "wid").astype(jnp.float32)
    hidden = (jax.nn.silu(summed[0]) * summed[1]).astype(jnp.bfloat16)
    return lax.psum_scatter(
        jnp.dot(hidden, down_weight, preferred_element_type=jnp.float32).astype(jnp.bfloat16),
        "hid",
        scatter_dimension=0,
        tiled=True,
    )


def pieces_of(width, most):
    first = width % most
    edges = ([0] if first else []) + list(range(first, width + 1, most))
    return list(zip(edges[:-1], edges[1:]))


def place(wid, d):
    step = wid ^ d
    return (step % 2) * 2 + step // 2


def spec(space):
    return pl.BlockSpec(memory_space=space)


def params(mib):
    return pltpu.CompilerParams(vmem_limit_bytes=mib * 2**20)


def column_copies(source_ref, out_ref, segments, sems):
    copies, cuts, at = [], [], 0
    for start, width in segments:
        for a, b in pieces_of(width, 2 * TILE):
            source = source_ref.at[:, pl.ds(pl.multiple_of(start + a, TILE), b - a)]
            copies.append(pltpu.make_async_copy(source, out_ref.at[:, at + a : at + b], sems.at[len(copies)]))
            cuts.append((at + a, at + b))
        at += width
    return copies, cuts


def fetch_kernel(first, where, gate_ref, up_ref, tokens_ref, gate_out, up_out, tokens_out, sems):
    copies = [pltpu.make_async_copy(tokens_ref, tokens_out, sems.at[2, 0])]
    for k, (source, out) in enumerate(((gate_ref, gate_out), (up_ref, up_out))):
        copies += column_copies(source, out, [(where[0] + first, out.shape[1])], sems.at[k])[0]
    for copy in copies:
        copy.start()
    for copy in copies:
        copy.wait()


def fetch(where, gate, up, tokens, first, width):
    depth = gate.shape[0]
    return pl.pallas_call(
        functools.partial(fetch_kernel, first),
        in_specs=[spec(pltpu.SMEM)] + [spec(pltpu.HBM)] * 3,
        out_specs=[spec(pltpu.VMEM)] * 3,
        out_shape=[pltpu.VMEM(x, jnp.bfloat16) for x in ((depth, width), (depth, width), tokens.shape)],
        scratch_shapes=[pltpu.SemaphoreType.DMA((3, len(pieces_of(width, 2 * TILE))))],
        compiler_params=params(1),
        cost_estimate=COST,
        name="fetch",
    )(where, gate, up, tokens)


def join_kernel(n, first, *refs):
    out_ref, at = refs[-1], 0
    for ref in refs[:n]:
        out_ref[at : at + ref.shape[0], :] = ref[:, first : first + out_ref.shape[1]]
        at += ref.shape[0]


def join(arrays, behind, first=0, width=None):
    rows, width = sum(a.shape[0] for a in arrays), width or arrays[0].shape[1]
    return pl.pallas_call(
        functools.partial(join_kernel, len(arrays), first),
        in_specs=[spec(pltpu.VMEM)] * len(arrays) + [spec(pl.ANY)] * len(behind),
        out_specs=spec(pltpu.VMEM),
        out_shape=jax.ShapeDtypeStruct((rows, width), arrays[0].dtype),
        compiler_params=params(1),
        cost_estimate=COST,
        name="join",
    )(*arrays, *behind)


def gate_up_kernel(n_arrays, n_pairs, n_parts, segments, where, *refs):
    arrays, weights = refs[:n_arrays], refs[n_arrays : n_arrays + 2 * n_pairs]
    if segments:
        refs, (w_ref, sems) = refs[:-2], refs[-2:]
    mine_ref, theirs, x_ref = refs[-n_parts - 2], refs[-n_parts - 1 : -1], refs[-1]
    if segments:
        copies = [column_copies(weights[k], w_ref.at[k], segments, sems.at[k]) for k in range(2)]
        cuts = copies[0][1]
        for i in range(len(cuts)):
            for k in range(2):
                copies[k][0][i].start()
    else:
        step = weights[0].shape[1]
        cuts = [(p * step + a, p * step + b) for p in range(n_pairs) for a, b in pieces_of(step, 2 * TILE)]
    per = x_ref.shape[0] // (4 * ROWS)
    b = 0
    for array in arrays:
        for at in range(0, array.shape[0], ROWS):
            to = (place(where[1], b % 4) * per + b // 4) * ROWS
            x_ref[pl.ds(pl.multiple_of(to, ROWS), ROWS), :] = array[at : at + ROWS, :]
            b += 1
    half = x_ref.shape[0] // 2
    for i, (a, b) in enumerate(cuts):
        for k in range(2):
            if segments:
                copies[k][0][i].wait()
                weight = w_ref[k, :, a:b]
            else:
                p = a // step
                weight = weights[2 * p + k][:, a - p * step : b - p * step]
            part = jnp.dot(x_ref[...], weight, preferred_element_type=jnp.float32).astype(jnp.bfloat16)
            mine_ref[k, :, a:b] = part[:half]
            part_width = theirs[0].shape[2]
            i_part = a // part_width
            theirs[i_part][k, :, a - i_part * part_width : b - i_part * part_width] = part[half:]


def gate_up(where, arrays, weights, segments, n_parts, behind):
    depth = weights[0].shape[0]
    width = sum(w for _, w in segments) if segments else sum(w.shape[1] for w in weights[::2])
    total = sum(a.shape[0] for a in arrays)
    scratch = [pltpu.VMEM((total, depth), jnp.bfloat16)]
    if segments:
        n_cuts = sum(len(pieces_of(w, 2 * TILE)) for _, w in segments)
        scratch.append(pltpu.VMEM((2, depth, width), jnp.bfloat16))
        scratch.append(pltpu.SemaphoreType.DMA((2, n_cuts)))
    return pl.pallas_call(
        functools.partial(gate_up_kernel, len(arrays), len(weights) // 2, n_parts, segments),
        in_specs=[spec(pltpu.SMEM)]
        + [spec(pltpu.VMEM)] * len(arrays)
        + [spec(pltpu.HBM if segments else pltpu.VMEM)] * len(weights)
        + [spec(pl.ANY)] * len(behind),
        out_specs=[spec(pltpu.VMEM)] * (1 + n_parts),
        scratch_shapes=scratch,
        out_shape=[jax.ShapeDtypeStruct((2, total // 2, w), jnp.bfloat16) for w in [width] + [width // n_parts] * n_parts],
        compiler_params=params(16 if segments else 4),
        cost_estimate=COST,
        name="gate_up",
    )(where, *arrays, *weights, *behind)


def pair_sum_kernel(first, mine_ref, got_ref, out_ref):
    rows, width = out_ref.shape[1:]
    for k in range(2):
        mine = mine_ref[k, rows:, first : first + width].astype(jnp.float32)
        out_ref[k] = (mine + got_ref[k, rows:].astype(jnp.float32)).astype(out_ref.dtype)


def pair_sum(mine, got, first):
    _, rows, width = got.shape
    return pl.pallas_call(
        functools.partial(pair_sum_kernel, first),
        in_specs=[spec(pltpu.VMEM)] * 2,
        out_specs=spec(pltpu.VMEM),
        out_shape=jax.ShapeDtypeStruct((2, rows // 2, width), mine.dtype),
        compiler_params=params(2),
        cost_estimate=COST,
        name="pair_sum",
    )(mine, got)


def later_kernel(array_ref, *refs):
    refs[-1][...] = array_ref[...]


def later(array, behind):
    return pl.pallas_call(
        later_kernel,
        in_specs=[spec(pltpu.VMEM)] + [spec(pl.ANY)] * len(behind),
        out_specs=spec(pltpu.VMEM),
        out_shape=jax.ShapeDtypeStruct(array.shape, array.dtype),
        compiler_params=params(1),
        cost_estimate=COST,
        name="later",
    )(array, *behind)


def combine_kernel(n_left, n_parts, n_outs, mine_ref, *refs):
    lefts, refs, outs = refs[:n_left], refs[n_left:], refs[-n_outs:]
    first = 0
    for left in lefts:
        first = left.shape[1]
        outs[0][:, :first] = left[...]
    at = 0
    for got_ref, chip_ref in zip(refs[:n_parts], refs[n_parts : 2 * n_parts]):
        _, rows, width = chip_ref.shape
        for a, b in pieces_of(width, TILE):
            gate, up = (
                mine_ref[k, :rows, at + a : at + b].astype(jnp.float32)
                + got_ref[k, :rows, a:b].astype(jnp.float32)
                + chip_ref[k, :, a:b].astype(jnp.float32)
                for k in range(2)
            )
            hidden = (gate / (1 + jnp.exp(-gate)) * up).astype(jnp.bfloat16)
            for i, out in enumerate(outs):
                out[:, first + at + a : first + at + b] = hidden[i * ROWS : (i + 1) * ROWS]
        at += width


def combine(mine, gots, from_chips, left):
    _, rows, width = mine.shape
    n_outs = rows // (2 * ROWS)
    width += sum(x.shape[1] for x in left)
    args = [mine, *left, *gots, *from_chips]
    return pl.pallas_call(
        functools.partial(combine_kernel, len(left), len(gots), n_outs),
        in_specs=[spec(pltpu.VMEM)] * len(args),
        out_specs=[spec(pltpu.VMEM)] * n_outs,
        out_shape=[jax.ShapeDtypeStruct((ROWS, width), jnp.bfloat16)] * n_outs,
        compiler_params=params(2),
        cost_estimate=COST,
        name="combine",
    )(*args)


def down_kernel(n_pieces, has_acc, last, segments, where, *refs):
    pieces, refs = refs[:n_pieces], refs[n_pieces:]
    down_ref, refs = refs[0], refs[1:]
    prev_ref, refs = (refs[0], refs[1:]) if has_acc else (None, refs)
    outs, (acc_ref, lhs_ref) = refs[:-2], refs[-2:]
    at = 0
    for piece in pieces:
        lhs_ref[at : at + piece.shape[0], :] = piece[...]
        at += piece.shape[0]
    lhs_ref[at:, :] = jnp.zeros_like(lhs_ref[at:, :])
    total = at
    for a, b in pieces_of(down_ref.shape[1], 2 * TILE):
        part = prev_ref[:, a:b] if has_acc else 0.0
        at = 0
        for sign, start, depth in segments:
            rows = pl.ds(pl.multiple_of(sign * where[0] + start, TILE) if sign else start, depth)
            product = jnp.dot(lhs_ref[:, at : at + depth], down_ref[rows, a:b], preferred_element_type=jnp.float32)
            part += product[:total]
            at += depth
        acc_ref[:, a:b] = part
    if last:
        for d, out in enumerate(outs):
            source = pl.multiple_of(place(where[1], d) * ROWS, ROWS)
            out[...] = acc_ref[pl.ds(source, ROWS), :].astype(out.dtype)


def down(where, pieces, down_weight, prev, segments, last):
    width = down_weight.shape[1]
    total = 4 * ROWS
    args = [*pieces, down_weight] + ([] if prev is None else [prev])
    sums = jax.ShapeDtypeStruct((total, width), jnp.float32)
    scratch = [pltpu.VMEM((max(total, 128), pieces[0].shape[1]), jnp.bfloat16)]
    if last:
        scratch = [pltpu.VMEM(sums.shape, sums.dtype)] + scratch
    return pl.pallas_call(
        functools.partial(down_kernel, len(pieces), prev is not None, last, segments),
        in_specs=[spec(pltpu.SMEM)] + [spec(pltpu.VMEM)] * len(args),
        out_specs=[spec(pltpu.VMEM)] * 4 if last else spec(pltpu.VMEM),
        scratch_shapes=scratch,
        out_shape=[jax.ShapeDtypeStruct((ROWS, width), jnp.bfloat16)] * 4 if last else sums,
        compiler_params=params(4),
        cost_estimate=COST,
        name="down",
    )(where, *args)


def split_by_rep(tokens, gate_weight, up_weight, down_weight):
    rep, wid = lax.axis_index("rep"), lax.axis_index("wid")
    f32, bf16 = jnp.float32, jnp.bfloat16
    half = gate_weight.shape[1] // 2
    where = jnp.stack([rep * half, wid]).astype(jnp.int32)

    def swap(x, axis, step):
        n = {"rep": 2, "hid": 4, "wid": 4}[axis]
        return lax.ppermute(x, axis, [(i, i ^ step) for i in range(n)])

    tiles = half // TILE
    bounds = [0, (tiles - LAST) // 2 * TILE, (tiles - LAST) * TILE, half]
    widths = [b - a for a, b in zip(bounds[:-1], bounds[1:])]
    gate_weight, up_weight, hbm_tokens = (
        pltpu.with_memory_space_constraint(w, pltpu.HBM) for w in (gate_weight, up_weight, tokens)
    )
    down_weight = pltpu.with_memory_space_constraint(down_weight, pltpu.VMEM)

    far_own = swap(tokens, "rep", 1)
    by_hid = [swap(tokens, "hid", d) for d in (3, 2, 1)][::-1]
    early = [fetch(where, gate_weight, up_weight, hbm_tokens, bounds[c], widths[c]) for c in range(2)]
    own = early[0][2]
    near = join(by_hid, [own, far_own])
    far = swap(near, "rep", 1)

    weights = [w for fetched in early for w in fetched[:2]]
    mine, *theirs = gate_up(where, [own, near, far_own, far], weights, [], 2, [])
    gots = [swap(x, "wid", 1) for x in theirs]
    to_chips = [pair_sum(mine, got, first) for got, first in zip(gots, bounds)]
    from_chips = [swap(x, "wid", 2) for x in to_chips]
    segments = [(bounds[2], widths[2]), (half + bounds[2], widths[2])]
    last_mine, theirs = gate_up(where, [own, near], [gate_weight, up_weight], segments, 1, to_chips)
    last_got = swap(later(theirs, from_chips), "wid", 1)
    last_from_chip = swap(pair_sum(last_mine, last_got, 0), "wid", 2)

    keep, give = combine(mine, gots, from_chips, [])
    far_columns = swap(give, "rep", 1)
    (rest,) = combine(last_mine, [last_got], [last_from_chip], [far_columns])
    rest_segments = [(-1, half, bounds[2])] + [(0, start, width) for start, width in segments]

    other = swap(keep, "wid", 2)
    pieces = [keep, other, swap(join([keep, other], []), "wid", 1)]
    acc = down(where, pieces, down_weight, None, [(1, 0, bounds[2])], False)
    other = swap(rest, "wid", 2)
    pieces = [rest, other, swap(rest, "wid", 1), swap(join([other], [acc]), "wid", 1)]
    acc = down(where, pieces, down_weight, acc, rest_segments, True)

    mixed = acc[0].astype(f32)
    for d in (3, 2, 1):
        mixed = mixed + swap(acc[d], "hid", d).astype(f32)
    return mixed.astype(bf16)


def solution(mesh):
    n_rep, n_hid, n_wid = (mesh.shape[a] for a in ("rep", "hid", "wid"))

    def on_device(tokens, gate_weight, up_weight, down_weight):
        fits = (
            (n_rep, n_hid, n_wid) == (2, 4, 4)
            and gate_weight.shape[1] % (n_rep * TILE) == 0
            and tokens.shape[0] == ROWS
        )
        if not fits:
            return plain(tokens, gate_weight, up_weight, down_weight)
        return split_by_rep(tokens, gate_weight, up_weight, down_weight)

    return jax.shard_map(
        on_device,
        mesh=mesh,
        in_specs=(P(("rep", "hid"), "wid"), P("wid", "hid"), P("wid", "hid"), P("hid", "wid")),
        out_specs=P(("rep", "hid"), "wid"),
        check_vma=False,
    )
```

```python
import functools

import jax
import jax.numpy as jnp
from jax import lax
from jax.experimental import pallas as pl
from jax.experimental.pallas import tpu as pltpu
from jax.sharding import PartitionSpec as P

TILE = 256
LAST = 3
ROWS = 16
COST = pl.CostEstimate(flops=0, bytes_accessed=1024, transcendentals=0)


def plain(tokens, gate_weight, up_weight, down_weight):
    piece = lax.all_gather(tokens, "hid", axis=0, tiled=True)
    gate_rows = jnp.dot(piece, gate_weight, preferred_element_type=jnp.float32)
    up_rows = jnp.dot(piece, up_weight, preferred_element_type=jnp.float32)
    partial_terms = jnp.stack([gate_rows, up_rows], 0)
    summed = lax.psum(partial_terms.astype(jnp.bfloat16), "wid").astype(jnp.float32)
    hidden = (jax.nn.silu(summed[0]) * summed[1]).astype(jnp.bfloat16)
    return lax.psum_scatter(
        jnp.dot(hidden, down_weight, preferred_element_type=jnp.float32).astype(jnp.bfloat16),
        "hid",
        scatter_dimension=0,
        tiled=True,
    )


def pieces_of(width, most):
    first = width % most
    edges = ([0] if first else []) + list(range(first, width + 1, most))
    return list(zip(edges[:-1], edges[1:]))


def place(wid, d):
    step = wid ^ d
    return (step % 2) * 2 + step // 2


def spec(space):
    return pl.BlockSpec(memory_space=space)


def params(mib):
    return pltpu.CompilerParams(vmem_limit_bytes=mib * 2**20)


def column_copies(source_ref, out_ref, segments, sems):
    copies, cuts, at = [], [], 0
    for start, width in segments:
        for a, b in pieces_of(width, 2 * TILE):
            source = source_ref.at[:, pl.ds(pl.multiple_of(start + a, TILE), b - a)]
            copies.append(pltpu.make_async_copy(source, out_ref.at[:, at + a : at + b], sems.at[len(copies)]))
            cuts.append((at + a, at + b))
        at += width
    return copies, cuts


def fetch_kernel(first, where, gate_ref, up_ref, tokens_ref, gate_out, up_out, tokens_out, sems):
    copies = [pltpu.make_async_copy(tokens_ref, tokens_out, sems.at[2, 0])]
    for k, (source, out) in enumerate(((gate_ref, gate_out), (up_ref, up_out))):
        copies += column_copies(source, out, [(where[0] + first, out.shape[1])], sems.at[k])[0]
    for copy in copies:
        copy.start()
    for copy in copies:
        copy.wait()


def fetch(where, gate, up, tokens, first, width):
    depth = gate.shape[0]
    return pl.pallas_call(
        functools.partial(fetch_kernel, first),
        in_specs=[spec(pltpu.SMEM)] + [spec(pltpu.HBM)] * 3,
        out_specs=[spec(pltpu.VMEM)] * 3,
        out_shape=[pltpu.VMEM(x, jnp.bfloat16) for x in ((depth, width), (depth, width), tokens.shape)],
        scratch_shapes=[pltpu.SemaphoreType.DMA((3, len(pieces_of(width, 2 * TILE))))],
        compiler_params=params(1),
        cost_estimate=COST,
        name="fetch",
    )(where, gate, up, tokens)


def join_kernel(n, first, *refs):
    out_ref, at = refs[-1], 0
    for ref in refs[:n]:
        out_ref[at : at + ref.shape[0], :] = ref[:, first : first + out_ref.shape[1]]
        at += ref.shape[0]


def join(arrays, behind, first=0, width=None):
    rows, width = sum(a.shape[0] for a in arrays), width or arrays[0].shape[1]
    return pl.pallas_call(
        functools.partial(join_kernel, len(arrays), first),
        in_specs=[spec(pltpu.VMEM)] * len(arrays) + [spec(pl.ANY)] * len(behind),
        out_specs=spec(pltpu.VMEM),
        out_shape=jax.ShapeDtypeStruct((rows, width), arrays[0].dtype),
        compiler_params=params(1),
        cost_estimate=COST,
        name="join",
    )(*arrays, *behind)


def gate_up_kernel(n_arrays, n_pairs, n_parts, segments, where, *refs):
    arrays, weights = refs[:n_arrays], refs[n_arrays : n_arrays + 2 * n_pairs]
    if segments:
        refs, (w_ref, sems) = refs[:-2], refs[-2:]
    mine_ref, theirs, x_ref = refs[-n_parts - 2], refs[-n_parts - 1 : -1], refs[-1]
    if segments:
        copies = [column_copies(weights[k], w_ref.at[k], segments, sems.at[k]) for k in range(2)]
        cuts = copies[0][1]
        for i in range(len(cuts)):
            for k in range(2):
                copies[k][0][i].start()
    else:
        step = weights[0].shape[1]
        cuts = [(p * step + a, p * step + b) for p in range(n_pairs) for a, b in pieces_of(step, 2 * TILE)]
    per = x_ref.shape[0] // (4 * ROWS)
    b = 0
    for array in arrays:
        for at in range(0, array.shape[0], ROWS):
            to = (place(where[1], b % 4) * per + b // 4) * ROWS
            x_ref[pl.ds(pl.multiple_of(to, ROWS), ROWS), :] = array[at : at + ROWS, :]
            b += 1
    half = x_ref.shape[0] // 2
    for i, (a, b) in enumerate(cuts):
        for k in range(2):
            if segments:
                copies[k][0][i].wait()
                weight = w_ref[k, :, a:b]
            else:
                p = a // step
                weight = weights[2 * p + k][:, a - p * step : b - p * step]
            part = jnp.dot(x_ref[...], weight, preferred_element_type=jnp.float32).astype(jnp.bfloat16)
            mine_ref[k, :, a:b] = part[:half]
            part_width = theirs[0].shape[2]
            i_part = a // part_width
            theirs[i_part][k, :, a - i_part * part_width : b - i_part * part_width] = part[half:]


def gate_up(where, arrays, weights, segments, n_parts, behind):
    depth = weights[0].shape[0]
    width = sum(w for _, w in segments) if segments else sum(w.shape[1] for w in weights[::2])
    total = sum(a.shape[0] for a in arrays)
    scratch = [pltpu.VMEM((total, depth), jnp.bfloat16)]
    if segments:
        n_cuts = sum(len(pieces_of(w, 2 * TILE)) for _, w in segments)
        scratch.append(pltpu.VMEM((2, depth, width), jnp.bfloat16))
        scratch.append(pltpu.SemaphoreType.DMA((2, n_cuts)))
    return pl.pallas_call(
        functools.partial(gate_up_kernel, len(arrays), len(weights) // 2, n_parts, segments),
        in_specs=[spec(pltpu.SMEM)]
        + [spec(pltpu.VMEM)] * len(arrays)
        + [spec(pltpu.HBM if segments else pltpu.VMEM)] * len(weights)
        + [spec(pl.ANY)] * len(behind),
        out_specs=[spec(pltpu.VMEM)] * (1 + n_parts),
        scratch_shapes=scratch,
        out_shape=[jax.ShapeDtypeStruct((2, total // 2, w), jnp.bfloat16) for w in [width] + [width // n_parts] * n_parts],
        compiler_params=params(16 if segments else 4),
        cost_estimate=COST,
        name="gate_up",
    )(where, *arrays, *weights, *behind)


def pair_sum_kernel(first, mine_ref, got_ref, out_ref):
    rows, width = out_ref.shape[1:]
    for k in range(2):
        mine = mine_ref[k, rows:, first : first + width].astype(jnp.float32)
        out_ref[k] = (mine + got_ref[k, rows:].astype(jnp.float32)).astype(out_ref.dtype)


def pair_sum(mine, got, first):
    _, rows, width = got.shape
    return pl.pallas_call(
        functools.partial(pair_sum_kernel, first),
        in_specs=[spec(pltpu.VMEM)] * 2,
        out_specs=spec(pltpu.VMEM),
        out_shape=jax.ShapeDtypeStruct((2, rows // 2, width), mine.dtype),
        compiler_params=params(2),
        cost_estimate=COST,
        name="pair_sum",
    )(mine, got)


def later_kernel(array_ref, *refs):
    refs[-1][...] = array_ref[...]


def later(array, behind):
    return pl.pallas_call(
        later_kernel,
        in_specs=[spec(pltpu.VMEM)] + [spec(pl.ANY)] * len(behind),
        out_specs=spec(pltpu.VMEM),
        out_shape=jax.ShapeDtypeStruct(array.shape, array.dtype),
        compiler_params=params(1),
        cost_estimate=COST,
        name="later",
    )(array, *behind)


def combine_kernel(n_left, n_parts, n_outs, mine_ref, *refs):
    lefts, refs, outs = refs[:n_left], refs[n_left:], refs[-n_outs:]
    first = 0
    for left in lefts:
        first = left.shape[1]
        outs[0][:, :first] = left[...]
    at = 0
    for got_ref, chip_ref in zip(refs[:n_parts], refs[n_parts : 2 * n_parts]):
        _, rows, width = chip_ref.shape
        for a, b in pieces_of(width, TILE):
            gate, up = (
                mine_ref[k, :rows, at + a : at + b].astype(jnp.float32)
                + got_ref[k, :rows, a:b].astype(jnp.float32)
                + chip_ref[k, :, a:b].astype(jnp.float32)
                for k in range(2)
            )
            hidden = (gate / (1 + jnp.exp(-gate)) * up).astype(jnp.bfloat16)
            for i, out in enumerate(outs):
                out[:, first + at + a : first + at + b] = hidden[i * ROWS : (i + 1) * ROWS]
        at += width


def combine(mine, gots, from_chips, left):
    _, rows, width = mine.shape
    n_outs = rows // (2 * ROWS)
    width += sum(x.shape[1] for x in left)
    args = [mine, *left, *gots, *from_chips]
    return pl.pallas_call(
        functools.partial(combine_kernel, len(left), len(gots), n_outs),
        in_specs=[spec(pltpu.VMEM)] * len(args),
        out_specs=[spec(pltpu.VMEM)] * n_outs,
        out_shape=[jax.ShapeDtypeStruct((ROWS, width), jnp.bfloat16)] * n_outs,
        compiler_params=params(2),
        cost_estimate=COST,
        name="combine",
    )(*args)


def down_kernel(n_pieces, has_acc, last, segments, where, *refs):
    pieces, refs = refs[:n_pieces], refs[n_pieces:]
    down_ref, refs = refs[0], refs[1:]
    prev_ref, refs = (refs[0], refs[1:]) if has_acc else (None, refs)
    outs, (acc_ref, lhs_ref) = refs[:-2], refs[-2:]
    at = 0
    for piece in pieces:
        lhs_ref[at : at + piece.shape[0], :] = piece[...]
        at += piece.shape[0]
    lhs_ref[at:, :] = jnp.zeros_like(lhs_ref[at:, :])
    total = at
    for a, b in pieces_of(down_ref.shape[1], 2 * TILE):
        part = prev_ref[:, a:b] if has_acc else 0.0
        at = 0
        for sign, start, depth in segments:
            rows = pl.ds(pl.multiple_of(sign * where[0] + start, TILE) if sign else start, depth)
            product = jnp.dot(lhs_ref[:, at : at + depth], down_ref[rows, a:b], preferred_element_type=jnp.float32)
            part += product[:total]
            at += depth
        acc_ref[:, a:b] = part
    if last:
        for d, out in enumerate(outs):
            source = pl.multiple_of(place(where[1], d) * ROWS, ROWS)
            out[...] = acc_ref[pl.ds(source, ROWS), :].astype(out.dtype)


def down(where, pieces, down_weight, prev, segments, last):
    width = down_weight.shape[1]
    total = 4 * ROWS
    args = [*pieces, down_weight] + ([] if prev is None else [prev])
    sums = jax.ShapeDtypeStruct((total, width), jnp.float32)
    scratch = [pltpu.VMEM((max(total, 128), pieces[0].shape[1]), jnp.bfloat16)]
    if last:
        scratch = [pltpu.VMEM(sums.shape, sums.dtype)] + scratch
    return pl.pallas_call(
        functools.partial(down_kernel, len(pieces), prev is not None, last, segments),
        in_specs=[spec(pltpu.SMEM)] + [spec(pltpu.VMEM)] * len(args),
        out_specs=[spec(pltpu.VMEM)] * 4 if last else spec(pltpu.VMEM),
        scratch_shapes=scratch,
        out_shape=[jax.ShapeDtypeStruct((ROWS, width), jnp.bfloat16)] * 4 if last else sums,
        compiler_params=params(4),
        cost_estimate=COST,
        name="down",
    )(where, *args)


def split_by_rep(tokens, gate_weight, up_weight, down_weight):
    rep, wid = lax.axis_index("rep"), lax.axis_index("wid")
    f32, bf16 = jnp.float32, jnp.bfloat16
    half = gate_weight.shape[1] // 2
    where = jnp.stack([rep * half, wid]).astype(jnp.int32)

    def swap(x, axis, step):
        n = {"rep": 2, "hid": 4, "wid": 4}[axis]
        return lax.ppermute(x, axis, [(i, i ^ step) for i in range(n)])

    tiles = half // TILE
    bounds = [0, (tiles - LAST) // 2 * TILE, (tiles - LAST) * TILE, half]
    widths = [b - a for a, b in zip(bounds[:-1], bounds[1:])]
    gate_weight, up_weight, hbm_tokens = (
        pltpu.with_memory_space_constraint(w, pltpu.HBM) for w in (gate_weight, up_weight, tokens)
    )
    down_weight = pltpu.with_memory_space_constraint(down_weight, pltpu.VMEM)

    far_own = swap(tokens, "rep", 1)
    by_hid = [swap(tokens, "hid", d) for d in (3, 2, 1)][::-1]
    early = [fetch(where, gate_weight, up_weight, hbm_tokens, bounds[c], widths[c]) for c in range(2)]
    own = early[0][2]
    near = join(by_hid, [own, far_own])
    far = swap(near, "rep", 1)

    weights = [w for fetched in early for w in fetched[:2]]
    mine, *theirs = gate_up(where, [own, near, far_own, far], weights, [], 2, [])
    gots = [swap(x, "wid", 1) for x in theirs]
    to_chips = [pair_sum(mine, got, first) for got, first in zip(gots, bounds)]
    from_chips = [swap(x, "wid", 2) for x in to_chips]
    segments = [(bounds[2], widths[2]), (half + bounds[2], widths[2])]
    last_mine, theirs = gate_up(where, [own, near], [gate_weight, up_weight], segments, 1, to_chips)
    last_got = swap(later(theirs, from_chips), "wid", 1)
    last_from_chip = swap(pair_sum(last_mine, last_got, 0), "wid", 2)

    keep, give = combine(mine, gots, from_chips, [])
    far_columns = swap(give, "rep", 1)
    (rest,) = combine(last_mine, [last_got], [last_from_chip], [])
    static = [(0, start, width) for start, width in segments]
    acc, behind = None, [far_columns]
    for hidden, parts in ((keep, [(1, 0, bounds[2])]), (far_columns, [(-1, half, bounds[2])]), (rest, static)):
        other = swap(hidden, "wid", 2)
        pieces = [hidden, other, swap(hidden, "wid", 1), swap(join([other], behind), "wid", 1)]
        acc = down(where, pieces, down_weight, acc, parts, hidden is rest)
        behind = [acc] if hidden is keep else []

    mixed = acc[0].astype(f32)
    for d in (3, 2, 1):
        mixed = mixed + swap(acc[d], "hid", d).astype(f32)
    return mixed.astype(bf16)


def solution(mesh):
    n_rep, n_hid, n_wid = (mesh.shape[a] for a in ("rep", "hid", "wid"))

    def on_device(tokens, gate_weight, up_weight, down_weight):
        fits = (
            (n_rep, n_hid, n_wid) == (2, 4, 4)
            and gate_weight.shape[1] % (n_rep * TILE) == 0
            and tokens.shape[0] == ROWS
        )
        if not fits:
            return plain(tokens, gate_weight, up_weight, down_weight)
        return split_by_rep(tokens, gate_weight, up_weight, down_weight)

    return jax.shard_map(
        on_device,
        mesh=mesh,
        in_specs=(P(("rep", "hid"), "wid"), P("wid", "hid"), P("wid", "hid"), P("hid", "wid")),
        out_specs=P(("rep", "hid"), "wid"),
        check_vma=False,
    )
```

```python
import functools

import jax
import jax.numpy as jnp
from jax import lax
from jax.experimental import pallas as pl
from jax.experimental.pallas import tpu as pltpu
from jax.sharding import PartitionSpec as P

TILE = 256
LAST = 3
ROWS = 16
COST = pl.CostEstimate(flops=0, bytes_accessed=1024, transcendentals=0)


def plain(tokens, gate_weight, up_weight, down_weight):
    piece = lax.all_gather(tokens, "hid", axis=0, tiled=True)
    gate_rows = jnp.dot(piece, gate_weight, preferred_element_type=jnp.float32)
    up_rows = jnp.dot(piece, up_weight, preferred_element_type=jnp.float32)
    partial_terms = jnp.stack([gate_rows, up_rows], 0)
    summed = lax.psum(partial_terms.astype(jnp.bfloat16), "wid").astype(jnp.float32)
    hidden = (jax.nn.silu(summed[0]) * summed[1]).astype(jnp.bfloat16)
    return lax.psum_scatter(
        jnp.dot(hidden, down_weight, preferred_element_type=jnp.float32).astype(jnp.bfloat16),
        "hid",
        scatter_dimension=0,
        tiled=True,
    )


def pieces_of(width, most):
    first = width % most
    edges = ([0] if first else []) + list(range(first, width + 1, most))
    return list(zip(edges[:-1], edges[1:]))


def place(wid, d):
    step = wid ^ d
    return (step % 2) * 2 + step // 2


def spec(space):
    return pl.BlockSpec(memory_space=space)


def params(mib):
    return pltpu.CompilerParams(vmem_limit_bytes=mib * 2**20)


def column_copies(source_ref, out_ref, segments, sems):
    copies, cuts, at = [], [], 0
    for start, width in segments:
        for a, b in pieces_of(width, 2 * TILE):
            source = source_ref.at[:, pl.ds(pl.multiple_of(start + a, TILE), b - a)]
            copies.append(pltpu.make_async_copy(source, out_ref.at[:, at + a : at + b], sems.at[len(copies)]))
            cuts.append((at + a, at + b))
        at += width
    return copies, cuts


def fetch_kernel(first, where, gate_ref, up_ref, tokens_ref, gate_out, up_out, tokens_out, sems):
    copies = [pltpu.make_async_copy(tokens_ref, tokens_out, sems.at[2, 0])]
    for k, (source, out) in enumerate(((gate_ref, gate_out), (up_ref, up_out))):
        copies += column_copies(source, out, [(where[0] + first, out.shape[1])], sems.at[k])[0]
    for copy in copies:
        copy.start()
    for copy in copies:
        copy.wait()


def fetch(where, gate, up, tokens, first, width):
    depth = gate.shape[0]
    return pl.pallas_call(
        functools.partial(fetch_kernel, first),
        in_specs=[spec(pltpu.SMEM)] + [spec(pltpu.HBM)] * 3,
        out_specs=[spec(pltpu.VMEM)] * 3,
        out_shape=[pltpu.VMEM(x, jnp.bfloat16) for x in ((depth, width), (depth, width), tokens.shape)],
        scratch_shapes=[pltpu.SemaphoreType.DMA((3, len(pieces_of(width, 2 * TILE))))],
        compiler_params=params(1),
        cost_estimate=COST,
        name="fetch",
    )(where, gate, up, tokens)


def join_kernel(n, first, *refs):
    out_ref, at = refs[-1], 0
    for ref in refs[:n]:
        out_ref[at : at + ref.shape[0], :] = ref[:, first : first + out_ref.shape[1]]
        at += ref.shape[0]


def join(arrays, behind, first=0, width=None):
    rows, width = sum(a.shape[0] for a in arrays), width or arrays[0].shape[1]
    return pl.pallas_call(
        functools.partial(join_kernel, len(arrays), first),
        in_specs=[spec(pltpu.VMEM)] * len(arrays) + [spec(pl.ANY)] * len(behind),
        out_specs=spec(pltpu.VMEM),
        out_shape=jax.ShapeDtypeStruct((rows, width), arrays[0].dtype),
        compiler_params=params(1),
        cost_estimate=COST,
        name="join",
    )(*arrays, *behind)


def gate_up_kernel(n_arrays, n_pairs, segments, where, *refs):
    arrays, weights = refs[:n_arrays], refs[n_arrays : n_arrays + 2 * n_pairs]
    if segments:
        mine_ref, theirs_ref, x_ref, w_ref, sems = refs[-5:]
        copies = [column_copies(weights[k], w_ref.at[k], segments, sems.at[k]) for k in range(2)]
        cuts = copies[0][1]
        for i in range(len(cuts)):
            for k in range(2):
                copies[k][0][i].start()
    else:
        mine_ref, theirs_ref, x_ref = refs[-3:]
        step = weights[0].shape[1]
        cuts = [(p * step + a, p * step + b) for p in range(n_pairs) for a, b in pieces_of(step, 2 * TILE)]
    per = x_ref.shape[0] // (4 * ROWS)
    b = 0
    for array in arrays:
        for at in range(0, array.shape[0], ROWS):
            to = (place(where[1], b % 4) * per + b // 4) * ROWS
            x_ref[pl.ds(pl.multiple_of(to, ROWS), ROWS), :] = array[at : at + ROWS, :]
            b += 1
    half = x_ref.shape[0] // 2
    for i, (a, b) in enumerate(cuts):
        for k in range(2):
            if segments:
                copies[k][0][i].wait()
                weight = w_ref[k, :, a:b]
            else:
                p = a // step
                weight = weights[2 * p + k][:, a - p * step : b - p * step]
            part = jnp.dot(x_ref[...], weight, preferred_element_type=jnp.float32).astype(jnp.bfloat16)
            mine_ref[k, :, a:b] = part[:half]
            theirs_ref[k, :, a:b] = part[half:]


def gate_up(where, arrays, weights, segments, behind):
    depth = weights[0].shape[0]
    width = sum(w for _, w in segments) if segments else sum(w.shape[1] for w in weights[::2])
    total = sum(a.shape[0] for a in arrays)
    scratch = [pltpu.VMEM((total, depth), jnp.bfloat16)]
    if segments:
        n_cuts = sum(len(pieces_of(w, 2 * TILE)) for _, w in segments)
        scratch.append(pltpu.VMEM((2, depth, width), jnp.bfloat16))
        scratch.append(pltpu.SemaphoreType.DMA((2, n_cuts)))
    return pl.pallas_call(
        functools.partial(gate_up_kernel, len(arrays), len(weights) // 2, segments),
        in_specs=[spec(pltpu.SMEM)]
        + [spec(pltpu.VMEM)] * len(arrays)
        + [spec(pltpu.HBM if segments else pltpu.VMEM)] * len(weights)
        + [spec(pl.ANY)] * len(behind),
        out_specs=[spec(pltpu.VMEM)] * 2,
        scratch_shapes=scratch,
        out_shape=[jax.ShapeDtypeStruct((2, total // 2, width), jnp.bfloat16)] * 2,
        compiler_params=params(16 if segments else 4),
        cost_estimate=COST,
        name="gate_up",
    )(where, *arrays, *weights, *behind)


def pair_sum_kernel(mine_ref, got_ref, *refs):
    out_ref = refs[-1]
    rows = out_ref.shape[1]
    for k in range(2):
        total = mine_ref[k, rows:].astype(jnp.float32) + got_ref[k, rows:].astype(jnp.float32)
        out_ref[k] = total.astype(out_ref.dtype)


def pair_sum(mine, got, behind):
    _, rows, width = mine.shape
    return pl.pallas_call(
        pair_sum_kernel,
        in_specs=[spec(pltpu.VMEM)] * 2 + [spec(pl.ANY)] * len(behind),
        out_specs=spec(pltpu.VMEM),
        out_shape=jax.ShapeDtypeStruct((2, rows // 2, width), mine.dtype),
        compiler_params=params(2),
        cost_estimate=COST,
        name="pair_sum",
    )(mine, got, *behind)


def combine_kernel(n_left, n_outs, mine_ref, got_ref, chip_ref, *refs):
    outs = refs[-n_outs:]
    rows, first = chip_ref.shape[1], 0
    for left in refs[:n_left]:
        first = left.shape[1]
        outs[0][:, :first] = left[...]
    for a, b in pieces_of(chip_ref.shape[2], TILE):
        gate, up = (
            mine_ref[k, :rows, a:b].astype(jnp.float32)
            + got_ref[k, :rows, a:b].astype(jnp.float32)
            + chip_ref[k, :, a:b].astype(jnp.float32)
            for k in range(2)
        )
        hidden = (gate / (1 + jnp.exp(-gate)) * up).astype(jnp.bfloat16)
        for i, out in enumerate(outs):
            out[:, first + a : first + b] = hidden[i * ROWS : (i + 1) * ROWS]


def combine(mine, got, from_chip, left, behind):
    _, rows, width = from_chip.shape
    n_outs = rows // ROWS
    width += sum(x.shape[1] for x in left)
    return pl.pallas_call(
        functools.partial(combine_kernel, len(left), n_outs),
        in_specs=[spec(pltpu.VMEM)] * (3 + len(left)) + [spec(pl.ANY)] * len(behind),
        out_specs=[spec(pltpu.VMEM)] * n_outs,
        out_shape=[jax.ShapeDtypeStruct((ROWS, width), jnp.bfloat16)] * n_outs,
        compiler_params=params(2),
        cost_estimate=COST,
        name="combine",
    )(mine, got, from_chip, *left, *behind)


def down_kernel(n_pieces, has_acc, last, segments, where, *refs):
    pieces, refs = refs[:n_pieces], refs[n_pieces:]
    down_ref, refs = refs[0], refs[1:]
    prev_ref, refs = (refs[0], refs[1:]) if has_acc else (None, refs)
    outs, (acc_ref, lhs_ref) = refs[:-2], refs[-2:]
    at = 0
    for piece in pieces:
        lhs_ref[at : at + piece.shape[0], :] = piece[...]
        at += piece.shape[0]
    lhs_ref[at:, :] = jnp.zeros_like(lhs_ref[at:, :])
    total = at
    for a, b in pieces_of(acc_ref.shape[1], 2 * TILE):
        part = prev_ref[:, a:b] if has_acc else 0.0
        at = 0
        for sign, start, depth in segments:
            rows = pl.ds(pl.multiple_of(sign * where[0] + start, TILE) if sign else start, depth)
            product = jnp.dot(lhs_ref[:, at : at + depth], down_ref[rows, a:b], preferred_element_type=jnp.float32)
            part += product[:total]
            at += depth
        acc_ref[:, a:b] = part
    if last:
        for d, out in enumerate(outs):
            source = pl.multiple_of(place(where[1], d) * ROWS, ROWS)
            out[...] = acc_ref[pl.ds(source, ROWS), :].astype(out.dtype)


def down(where, pieces, down_weight, prev, segments, last):
    width = down_weight.shape[1]
    total = 4 * ROWS
    args = [*pieces, down_weight] + ([] if prev is None else [prev])
    sums = jax.ShapeDtypeStruct((total, width), jnp.float32)
    scratch = [pltpu.VMEM((max(total, 128), pieces[0].shape[1]), jnp.bfloat16)]
    if last:
        scratch = [pltpu.VMEM(sums.shape, sums.dtype)] + scratch
    return pl.pallas_call(
        functools.partial(down_kernel, len(pieces), prev is not None, last, segments),
        in_specs=[spec(pltpu.SMEM)] + [spec(pltpu.VMEM)] * len(args),
        out_specs=[spec(pltpu.VMEM)] * 4 if last else spec(pltpu.VMEM),
        scratch_shapes=scratch,
        out_shape=[jax.ShapeDtypeStruct((ROWS, width), jnp.bfloat16)] * 4 if last else sums,
        compiler_params=params(4),
        cost_estimate=COST,
        name="down",
    )(where, *args)


def split_by_rep(tokens, gate_weight, up_weight, down_weight):
    rep, wid = lax.axis_index("rep"), lax.axis_index("wid")
    f32, bf16 = jnp.float32, jnp.bfloat16
    half = gate_weight.shape[1] // 2
    where = jnp.stack([rep * half, wid]).astype(jnp.int32)

    def swap(x, axis, step):
        n = {"rep": 2, "hid": 4, "wid": 4}[axis]
        return lax.ppermute(x, axis, [(i, i ^ step) for i in range(n)])

    tiles = half // TILE
    bounds = [0, (tiles - LAST) // 2 * TILE, (tiles - LAST) * TILE, half]
    widths = [b - a for a, b in zip(bounds[:-1], bounds[1:])]
    gate_weight, up_weight, hbm_tokens = (
        pltpu.with_memory_space_constraint(w, pltpu.HBM) for w in (gate_weight, up_weight, tokens)
    )
    down_weight = pltpu.with_memory_space_constraint(down_weight, pltpu.VMEM)

    far_own = swap(tokens, "rep", 1)
    by_hid = [swap(tokens, "hid", d) for d in (3, 2, 1)][::-1]
    early = [fetch(where, gate_weight, up_weight, hbm_tokens, bounds[c], widths[c]) for c in range(2)]
    own = early[0][2]
    near = join(by_hid, [own, far_own])
    far = swap(near, "rep", 1)

    weights = [w for fetched in early for w in fetched[:2]]
    mine, theirs = gate_up(where, [own, near, far_own, far], weights, [], [])
    got = swap(theirs, "wid", 1)
    to_chip = pair_sum(mine, got, [])
    from_chip = swap(to_chip, "wid", 2)
    segments = [(bounds[2], widths[2]), (half + bounds[2], widths[2])]
    last_mine, theirs = gate_up(where, [own, near], [gate_weight, up_weight], segments, [to_chip])
    last_got = swap(theirs, "wid", 1)
    keep, give = combine(mine, got, from_chip, [], [])
    last_to_chip = pair_sum(last_mine, last_got, [give])
    last_from_chip = swap(last_to_chip, "wid", 2)
    (rest,) = combine(last_mine, last_got, last_from_chip, [swap(give, "rep", 1)], [])

    def gather(hidden, behind):
        other = swap(hidden, "wid", 2)
        return [hidden, other, swap(hidden, "wid", 1), swap(join([other], behind), "wid", 1)]

    acc = down(where, gather(keep, [rest]), down_weight, None, [(1, 0, bounds[2])], False)
    rest_segments = [(-1, half, bounds[2])] + [(0, start, width) for start, width in segments]
    acc = down(where, gather(rest, [acc]), down_weight, acc, rest_segments, True)

    mixed = acc[0].astype(f32)
    for d in (3, 2, 1):
        mixed = mixed + swap(acc[d], "hid", d).astype(f32)
    return mixed.astype(bf16)


def solution(mesh):
    n_rep, n_hid, n_wid = (mesh.shape[a] for a in ("rep", "hid", "wid"))

    def on_device(tokens, gate_weight, up_weight, down_weight):
        fits = (
            (n_rep, n_hid, n_wid) == (2, 4, 4)
            and gate_weight.shape[1] % (n_rep * TILE) == 0
            and tokens.shape[0] == ROWS
        )
        if not fits:
            return plain(tokens, gate_weight, up_weight, down_weight)
        return split_by_rep(tokens, gate_weight, up_weight, down_weight)

    return jax.shard_map(
        on_device,
        mesh=mesh,
        in_specs=(P(("rep", "hid"), "wid"), P("wid", "hid"), P("wid", "hid"), P("hid", "wid")),
        out_specs=P(("rep", "hid"), "wid"),
        check_vma=False,
    )
```

```python
import functools

import jax
import jax.numpy as jnp
from jax import lax
from jax.experimental import pallas as pl
from jax.experimental.pallas import tpu as pltpu
from jax.sharding import PartitionSpec as P

TILE = 256
CHUNKS = (4, 4, 2, 3)
ROWS = 16
COST = pl.CostEstimate(flops=0, bytes_accessed=1024, transcendentals=0)


def plain(tokens, gate_weight, up_weight, down_weight):
    piece = lax.all_gather(tokens, "hid", axis=0, tiled=True)
    gate_rows = jnp.dot(piece, gate_weight, preferred_element_type=jnp.float32)
    up_rows = jnp.dot(piece, up_weight, preferred_element_type=jnp.float32)
    partial_terms = jnp.stack([gate_rows, up_rows], 0)
    summed = lax.psum(partial_terms.astype(jnp.bfloat16), "wid").astype(jnp.float32)
    hidden = (jax.nn.silu(summed[0]) * summed[1]).astype(jnp.bfloat16)
    return lax.psum_scatter(
        jnp.dot(hidden, down_weight, preferred_element_type=jnp.float32).astype(jnp.bfloat16),
        "hid",
        scatter_dimension=0,
        tiled=True,
    )


def pieces_of(width, most):
    first = width % most
    edges = ([0] if first else []) + list(range(first, width + 1, most))
    return list(zip(edges[:-1], edges[1:]))


def place(wid, d):
    step = wid ^ d
    return (step % 2) * 2 + step // 2


def spec(space):
    return pl.BlockSpec(memory_space=space)


def params(mib):
    return pltpu.CompilerParams(vmem_limit_bytes=mib * 2**20)


def column_copies(source_ref, out_ref, segments, sems):
    copies, cuts, at = [], [], 0
    for start, width in segments:
        for a, b in pieces_of(width, 2 * TILE):
            source = source_ref.at[:, pl.ds(pl.multiple_of(start + a, TILE), b - a)]
            copies.append(pltpu.make_async_copy(source, out_ref.at[:, at + a : at + b], sems.at[len(copies)]))
            cuts.append((at + a, at + b))
        at += width
    return copies, cuts


def fetch_kernel(first, where, gate_ref, up_ref, tokens_ref, gate_out, up_out, tokens_out, sems):
    copies = [pltpu.make_async_copy(tokens_ref, tokens_out, sems.at[2, 0])]
    for k, (source, out) in enumerate(((gate_ref, gate_out), (up_ref, up_out))):
        copies += column_copies(source, out, [(where[0] + first, out.shape[1])], sems.at[k])[0]
    for copy in copies:
        copy.start()
    for copy in copies:
        copy.wait()


def fetch(where, gate, up, tokens, first, width):
    depth = gate.shape[0]
    return pl.pallas_call(
        functools.partial(fetch_kernel, first),
        in_specs=[spec(pltpu.SMEM)] + [spec(pltpu.HBM)] * 3,
        out_specs=[spec(pltpu.VMEM)] * 3,
        out_shape=[pltpu.VMEM(x, jnp.bfloat16) for x in ((depth, width), (depth, width), tokens.shape)],
        scratch_shapes=[pltpu.SemaphoreType.DMA((3, len(pieces_of(width, 2 * TILE))))],
        compiler_params=params(1),
        cost_estimate=COST,
        name="fetch",
    )(where, gate, up, tokens)


def join_kernel(n, first, *refs):
    out_ref, at = refs[-1], 0
    for ref in refs[:n]:
        out_ref[at : at + ref.shape[0], :] = ref[:, first : first + out_ref.shape[1]]
        at += ref.shape[0]


def join(arrays, behind, first=0, width=None):
    rows, width = sum(a.shape[0] for a in arrays), width or arrays[0].shape[1]
    return pl.pallas_call(
        functools.partial(join_kernel, len(arrays), first),
        in_specs=[spec(pltpu.VMEM)] * len(arrays) + [spec(pl.ANY)] * len(behind),
        out_specs=spec(pltpu.VMEM),
        out_shape=jax.ShapeDtypeStruct((rows, width), arrays[0].dtype),
        compiler_params=params(1),
        cost_estimate=COST,
        name="join",
    )(*arrays, *behind)


def gate_up_kernel(n_arrays, n_weights, segments, where, *refs):
    arrays, weights = refs[:n_arrays], refs[n_arrays : n_arrays + n_weights]
    pieces, at = [], 0
    if segments:
        mine_ref, theirs_ref, x_ref, w_ref, sems = refs[-5:]
        *weights, gate_ref, up_ref = weights
    else:
        mine_ref, theirs_ref, x_ref = refs[-3:]
    for gate, up in zip(weights[::2], weights[1::2]):
        pieces += [(at, a, b, (gate, up), None) for a, b in pieces_of(gate.shape[1], 2 * TILE)]
        at += gate.shape[1]
    if segments:
        starts = [(sign * where[0] + start if sign else start, width) for sign, start, width in segments]
        copies = [column_copies(ref, w_ref.at[k], starts, sems.at[k]) for k, ref in enumerate((gate_ref, up_ref))]
        cuts = copies[0][1]
        for i in range(len(cuts)):
            for k in range(2):
                copies[k][0][i].start()
        pieces += [(at, a, b, (w_ref.at[0], w_ref.at[1]), i) for i, (a, b) in enumerate(cuts)]
    per = x_ref.shape[0] // (4 * ROWS)
    b = 0
    for array in arrays:
        for at in range(0, array.shape[0], ROWS):
            to = (place(where[1], b % 4) * per + b // 4) * ROWS
            x_ref[pl.ds(pl.multiple_of(to, ROWS), ROWS), :] = array[at : at + ROWS, :]
            b += 1
    half = x_ref.shape[0] // 2
    for at, a, b, refs, i in pieces:
        for k in range(2):
            if i is not None:
                copies[k][0][i].wait()
            part = jnp.dot(x_ref[...], refs[k][:, a:b], preferred_element_type=jnp.float32).astype(jnp.bfloat16)
            mine_ref[k, :, at + a : at + b] = part[:half]
            theirs_ref[k, :, at + a : at + b] = part[half:]


def gate_up(where, arrays, weights, segments, behind):
    depth = weights[0].shape[0]
    near = weights[:-2] if segments else weights
    streamed = sum(width for _, _, width in segments)
    width = sum(w.shape[1] for w in near[::2]) + streamed
    total = sum(a.shape[0] for a in arrays)
    scratch = [pltpu.VMEM((total, depth), jnp.bfloat16)]
    if segments:
        n_cuts = sum(len(pieces_of(w, 2 * TILE)) for _, _, w in segments)
        scratch.append(pltpu.VMEM((2, depth, streamed), jnp.bfloat16))
        scratch.append(pltpu.SemaphoreType.DMA((2, n_cuts)))
    return pl.pallas_call(
        functools.partial(gate_up_kernel, len(arrays), len(weights), segments),
        in_specs=[spec(pltpu.SMEM)]
        + [spec(pltpu.VMEM)] * (len(arrays) + len(near))
        + [spec(pltpu.HBM)] * (len(weights) - len(near))
        + [spec(pl.ANY)] * len(behind),
        out_specs=[spec(pltpu.VMEM)] * 2,
        scratch_shapes=scratch,
        out_shape=[jax.ShapeDtypeStruct((2, total // 2, width), jnp.bfloat16)] * 2,
        compiler_params=params(4 + 4 * depth * streamed // 2**20),
        cost_estimate=COST,
        name="gate_up",
    )(where, *arrays, *weights, *behind)


def pair_sum_kernel(mine_ref, got_ref, *refs):
    out_ref = refs[-1]
    rows = out_ref.shape[1]
    for k in range(2):
        total = mine_ref[k, rows:].astype(jnp.float32) + got_ref[k, rows:].astype(jnp.float32)
        out_ref[k] = total.astype(out_ref.dtype)


def pair_sum(mine, got, behind):
    _, rows, width = mine.shape
    return pl.pallas_call(
        pair_sum_kernel,
        in_specs=[spec(pltpu.VMEM)] * 2 + [spec(pl.ANY)] * len(behind),
        out_specs=spec(pltpu.VMEM),
        out_shape=jax.ShapeDtypeStruct((2, rows // 2, width), mine.dtype),
        compiler_params=params(2),
        cost_estimate=COST,
        name="pair_sum",
    )(mine, got, *behind)


def combine_kernel(n_left, n_outs, mine_ref, got_ref, chip_ref, *refs):
    outs = refs[-n_outs:]
    rows, first = chip_ref.shape[1], 0
    for left in refs[:n_left]:
        first = left.shape[1]
        outs[0][:, :first] = left[...]
    for a, b in pieces_of(chip_ref.shape[2], TILE):
        gate, up = (
            mine_ref[k, :rows, a:b].astype(jnp.float32)
            + got_ref[k, :rows, a:b].astype(jnp.float32)
            + chip_ref[k, :, a:b].astype(jnp.float32)
            for k in range(2)
        )
        hidden = (gate / (1 + jnp.exp(-gate)) * up).astype(jnp.bfloat16)
        for i, out in enumerate(outs):
            out[:, first + a : first + b] = hidden[i * ROWS : (i + 1) * ROWS]


def combine(mine, got, from_chip, left, behind):
    _, rows, width = from_chip.shape
    n_outs = rows // ROWS
    width += sum(x.shape[1] for x in left)
    return pl.pallas_call(
        functools.partial(combine_kernel, len(left), n_outs),
        in_specs=[spec(pltpu.VMEM)] * (3 + len(left)) + [spec(pl.ANY)] * len(behind),
        out_specs=[spec(pltpu.VMEM)] * n_outs,
        out_shape=[jax.ShapeDtypeStruct((ROWS, width), jnp.bfloat16)] * n_outs,
        compiler_params=params(2),
        cost_estimate=COST,
        name="combine",
    )(mine, got, from_chip, *left, *behind)


def down_kernel(n_pieces, has_acc, last, segments, where, *refs):
    pieces, refs = refs[:n_pieces], refs[n_pieces:]
    down_ref, refs = refs[0], refs[1:]
    prev_ref, refs = (refs[0], refs[1:]) if has_acc else (None, refs)
    outs, (acc_ref, lhs_ref) = refs[:-2], refs[-2:]
    at = 0
    for piece in pieces:
        lhs_ref[at : at + piece.shape[0], :] = piece[...]
        at += piece.shape[0]
    lhs_ref[at:, :] = jnp.zeros_like(lhs_ref[at:, :])
    total = at
    for a, b in pieces_of(acc_ref.shape[1], 2 * TILE):
        part = prev_ref[:, a:b] if has_acc else 0.0
        at = 0
        for sign, start, depth in segments:
            rows = pl.ds(pl.multiple_of(sign * where[0] + start, TILE) if sign else start, depth)
            product = jnp.dot(lhs_ref[:, at : at + depth], down_ref[rows, a:b], preferred_element_type=jnp.float32)
            part += product[:total]
            at += depth
        acc_ref[:, a:b] = part
    if last:
        for d, out in enumerate(outs):
            source = pl.multiple_of(place(where[1], d) * ROWS, ROWS)
            out[...] = acc_ref[pl.ds(source, ROWS), :].astype(out.dtype)


def down(where, pieces, down_weight, prev, segments, last):
    width = down_weight.shape[1]
    total = 4 * ROWS
    args = [*pieces, down_weight] + ([] if prev is None else [prev])
    sums = jax.ShapeDtypeStruct((total, width), jnp.float32)
    scratch = [pltpu.VMEM((max(total, 128), pieces[0].shape[1]), jnp.bfloat16)]
    if last:
        scratch = [pltpu.VMEM(sums.shape, sums.dtype)] + scratch
    return pl.pallas_call(
        functools.partial(down_kernel, len(pieces), prev is not None, last, segments),
        in_specs=[spec(pltpu.SMEM)] + [spec(pltpu.VMEM)] * len(args),
        out_specs=[spec(pltpu.VMEM)] * 4 if last else spec(pltpu.VMEM),
        scratch_shapes=scratch,
        out_shape=[jax.ShapeDtypeStruct((ROWS, width), jnp.bfloat16)] * 4 if last else sums,
        compiler_params=params(4),
        cost_estimate=COST,
        name="down",
    )(where, *args)


def split_by_rep(tokens, gate_weight, up_weight, down_weight):
    rep, wid = lax.axis_index("rep"), lax.axis_index("wid")
    f32, bf16 = jnp.float32, jnp.bfloat16
    half = gate_weight.shape[1] // 2
    where = jnp.stack([rep * half, wid]).astype(jnp.int32)

    def swap(x, axis, step):
        n = {"rep": 2, "hid": 4, "wid": 4}[axis]
        return lax.ppermute(x, axis, [(i, i ^ step) for i in range(n)])

    bounds = [sum(CHUNKS[:c]) * TILE for c in range(5)]
    widths = [n * TILE for n in CHUNKS]
    split = bounds[3]
    gate_weight, up_weight, hbm_tokens = (
        pltpu.with_memory_space_constraint(w, pltpu.HBM) for w in (gate_weight, up_weight, tokens)
    )
    down_weight = pltpu.with_memory_space_constraint(down_weight, pltpu.VMEM)

    by_hid = {d: swap(tokens, "hid", d) for d in (1, 3, 2)}
    far_own, far_1 = swap(tokens, "rep", 1), swap(by_hid[1], "rep", 1)
    early = [fetch(where, gate_weight, up_weight, hbm_tokens, bounds[c], widths[c]) for c in range(2)]
    own = early[0][2]
    near = join([by_hid[2], by_hid[3]], [own, far_own, far_1])
    far = swap(near, "rep", 1)

    weights = [w for fetched in early for w in fetched[:2]] + [gate_weight, up_weight]
    arrays = [own, by_hid[1], near, far_own, far_1, far]
    mine, theirs = gate_up(where, arrays, weights, [(1, bounds[2], widths[2])], [])
    got = swap(theirs, "wid", 1)
    to_chip = pair_sum(mine, got, [])
    from_chip = swap(to_chip, "wid", 2)
    segments = [(0, split, widths[3]), (0, half + split, widths[3])]
    last_mine, theirs = gate_up(where, arrays[:3], [gate_weight, up_weight], segments, [to_chip])
    last_got = swap(theirs, "wid", 1)
    keep, give = combine(mine, got, from_chip, [], [])
    last_to_chip = pair_sum(last_mine, last_got, [give])
    last_from_chip = swap(last_to_chip, "wid", 2)
    (rest,) = combine(last_mine, last_got, last_from_chip, [swap(give, "rep", 1)], [])

    def gather(hidden, behind):
        other = swap(hidden, "wid", 2)
        return [hidden, other, swap(hidden, "wid", 1), swap(join([other], behind), "wid", 1)]

    acc = down(where, gather(keep, [rest]), down_weight, None, [(1, 0, split)], False)
    acc = down(where, gather(rest, [acc]), down_weight, acc, [(-1, half, split)] + segments, True)

    mixed = acc[0].astype(f32)
    for d in (3, 2, 1):
        mixed = mixed + swap(acc[d], "hid", d).astype(f32)
    return mixed.astype(bf16)


def solution(mesh):
    n_rep, n_hid, n_wid = (mesh.shape[a] for a in ("rep", "hid", "wid"))

    def on_device(tokens, gate_weight, up_weight, down_weight):
        fits = (
            (n_rep, n_hid, n_wid) == (2, 4, 4)
            and gate_weight.shape[1] == n_rep * sum(CHUNKS) * TILE
            and tokens.shape[0] == ROWS
        )
        if not fits:
            return plain(tokens, gate_weight, up_weight, down_weight)
        return split_by_rep(tokens, gate_weight, up_weight, down_weight)

    return jax.shard_map(
        on_device,
        mesh=mesh,
        in_specs=(P(("rep", "hid"), "wid"), P("wid", "hid"), P("wid", "hid"), P("hid", "wid")),
        out_specs=P(("rep", "hid"), "wid"),
        check_vma=False,
    )
```

```python
import functools

import jax
import jax.numpy as jnp
from jax import lax
from jax.experimental import pallas as pl
from jax.experimental.pallas import tpu as pltpu
from jax.sharding import PartitionSpec as P

TILE = 256
LAST = 3
ROWS = 16
COST = pl.CostEstimate(flops=0, bytes_accessed=1024, transcendentals=0)


def plain(tokens, gate_weight, up_weight, down_weight):
    piece = lax.all_gather(tokens, "hid", axis=0, tiled=True)
    gate_rows = jnp.dot(piece, gate_weight, preferred_element_type=jnp.float32)
    up_rows = jnp.dot(piece, up_weight, preferred_element_type=jnp.float32)
    partial_terms = jnp.stack([gate_rows, up_rows], 0)
    summed = lax.psum(partial_terms.astype(jnp.bfloat16), "wid").astype(jnp.float32)
    hidden = (jax.nn.silu(summed[0]) * summed[1]).astype(jnp.bfloat16)
    return lax.psum_scatter(
        jnp.dot(hidden, down_weight, preferred_element_type=jnp.float32).astype(jnp.bfloat16),
        "hid",
        scatter_dimension=0,
        tiled=True,
    )


def pieces_of(width, most):
    first = width % most
    edges = ([0] if first else []) + list(range(first, width + 1, most))
    return list(zip(edges[:-1], edges[1:]))


def place(wid, d):
    step = wid ^ d
    return (step % 2) * 2 + step // 2


def here(half):
    return lax.axis_index("rep") * half, lax.axis_index("wid")


def spec(space):
    return pl.BlockSpec(memory_space=space)


def params(mib):
    return pltpu.CompilerParams(vmem_limit_bytes=mib * 2**20)


def column_copies(source_ref, out_ref, segments, sems):
    copies, cuts, at = [], [], 0
    for start, width in segments:
        for a, b in pieces_of(width, 2 * TILE):
            source = source_ref.at[:, pl.ds(pl.multiple_of(start + a, TILE), b - a)]
            copies.append(pltpu.make_async_copy(source, out_ref.at[:, at + a : at + b], sems.at[len(copies)]))
            cuts.append((at + a, at + b))
        at += width
    return copies, cuts


def fetch_kernel(first, gate_ref, up_ref, tokens_ref, gate_out, up_out, tokens_out, sems):
    where = here(gate_ref.shape[1] // 2)
    copies = [pltpu.make_async_copy(tokens_ref, tokens_out, sems.at[2, 0])]
    for k, (source, out) in enumerate(((gate_ref, gate_out), (up_ref, up_out))):
        copies += column_copies(source, out, [(where[0] + first, out.shape[1])], sems.at[k])[0]
    for copy in copies:
        copy.start()
    for copy in copies:
        copy.wait()


def fetch(gate, up, tokens, first, width):
    depth = gate.shape[0]
    return pl.pallas_call(
        functools.partial(fetch_kernel, first),
        in_specs=[spec(pltpu.HBM)] * 3,
        out_specs=[spec(pltpu.VMEM)] * 3,
        out_shape=[pltpu.VMEM(x, jnp.bfloat16) for x in ((depth, width), (depth, width), tokens.shape)],
        scratch_shapes=[pltpu.SemaphoreType.DMA((3, len(pieces_of(width, 2 * TILE))))],
        compiler_params=params(1),
        cost_estimate=COST,
        name="fetch",
    )(gate, up, tokens)


def join_kernel(n, first, *refs):
    out_ref, at = refs[-1], 0
    for ref in refs[:n]:
        out_ref[at : at + ref.shape[0], :] = ref[:, first : first + out_ref.shape[1]]
        at += ref.shape[0]


def join(arrays, behind, first=0, width=None):
    rows, width = sum(a.shape[0] for a in arrays), width or arrays[0].shape[1]
    return pl.pallas_call(
        functools.partial(join_kernel, len(arrays), first),
        in_specs=[spec(pltpu.VMEM)] * len(arrays) + [spec(pl.ANY)] * len(behind),
        out_specs=spec(pltpu.VMEM),
        out_shape=jax.ShapeDtypeStruct((rows, width), arrays[0].dtype),
        compiler_params=params(1),
        cost_estimate=COST,
        name="join",
    )(*arrays, *behind)


def gate_up_kernel(n_arrays, n_pairs, segments, *refs):
    where = here(0)
    arrays, weights = refs[:n_arrays], refs[n_arrays : n_arrays + 2 * n_pairs]
    if segments:
        mine_ref, theirs_ref, x_ref, w_ref, sems = refs[-5:]
        copies = [column_copies(weights[k], w_ref.at[k], segments, sems.at[k]) for k in range(2)]
        cuts = copies[0][1]
        for i in range(len(cuts)):
            for k in range(2):
                copies[k][0][i].start()
    else:
        mine_ref, theirs_ref, x_ref = refs[-3:]
        step = weights[0].shape[1]
        cuts = [(p * step + a, p * step + b) for p in range(n_pairs) for a, b in pieces_of(step, 2 * TILE)]
    per = x_ref.shape[0] // (4 * ROWS)
    b = 0
    for array in arrays:
        for at in range(0, array.shape[0], ROWS):
            to = (place(where[1], b % 4) * per + b // 4) * ROWS
            x_ref[pl.ds(pl.multiple_of(to, ROWS), ROWS), :] = array[at : at + ROWS, :]
            b += 1
    half = x_ref.shape[0] // 2
    for i, (a, b) in enumerate(cuts):
        for k in range(2):
            if segments:
                copies[k][0][i].wait()
                weight = w_ref[k, :, a:b]
            else:
                p = a // step
                weight = weights[2 * p + k][:, a - p * step : b - p * step]
            part = jnp.dot(x_ref[...], weight, preferred_element_type=jnp.float32).astype(jnp.bfloat16)
            mine_ref[k, :, a:b] = part[:half]
            theirs_ref[k, :, a:b] = part[half:]


def gate_up(arrays, weights, segments, behind):
    depth = weights[0].shape[0]
    width = sum(w for _, w in segments) if segments else sum(w.shape[1] for w in weights[::2])
    total = sum(a.shape[0] for a in arrays)
    scratch = [pltpu.VMEM((total, depth), jnp.bfloat16)]
    if segments:
        n_cuts = sum(len(pieces_of(w, 2 * TILE)) for _, w in segments)
        scratch.append(pltpu.VMEM((2, depth, width), jnp.bfloat16))
        scratch.append(pltpu.SemaphoreType.DMA((2, n_cuts)))
    return pl.pallas_call(
        functools.partial(gate_up_kernel, len(arrays), len(weights) // 2, segments),
        in_specs=[spec(pltpu.VMEM)] * len(arrays)
        + [spec(pltpu.HBM if segments else pltpu.VMEM)] * len(weights)
        + [spec(pl.ANY)] * len(behind),
        out_specs=[spec(pltpu.VMEM)] * 2,
        scratch_shapes=scratch,
        out_shape=[jax.ShapeDtypeStruct((2, total // 2, width), jnp.bfloat16)] * 2,
        compiler_params=params(16 if segments else 4),
        cost_estimate=COST,
        name="gate_up",
    )(*arrays, *weights, *behind)


def pair_sum_kernel(mine_ref, got_ref, *refs):
    out_ref = refs[-1]
    rows = out_ref.shape[1]
    for k in range(2):
        total = mine_ref[k, rows:].astype(jnp.float32) + got_ref[k, rows:].astype(jnp.float32)
        out_ref[k] = total.astype(out_ref.dtype)


def pair_sum(mine, got, behind):
    _, rows, width = mine.shape
    return pl.pallas_call(
        pair_sum_kernel,
        in_specs=[spec(pltpu.VMEM)] * 2 + [spec(pl.ANY)] * len(behind),
        out_specs=spec(pltpu.VMEM),
        out_shape=jax.ShapeDtypeStruct((2, rows // 2, width), mine.dtype),
        compiler_params=params(2),
        cost_estimate=COST,
        name="pair_sum",
    )(mine, got, *behind)


def combine_kernel(n_left, n_outs, mine_ref, got_ref, chip_ref, *refs):
    outs = refs[-n_outs:]
    rows, first = chip_ref.shape[1], 0
    for left in refs[:n_left]:
        first = left.shape[1]
        outs[0][:, :first] = left[...]
    for a, b in pieces_of(chip_ref.shape[2], TILE):
        gate, up = (
            mine_ref[k, :rows, a:b].astype(jnp.float32)
            + got_ref[k, :rows, a:b].astype(jnp.float32)
            + chip_ref[k, :, a:b].astype(jnp.float32)
            for k in range(2)
        )
        hidden = (gate / (1 + jnp.exp(-gate)) * up).astype(jnp.bfloat16)
        for i, out in enumerate(outs):
            out[:, first + a : first + b] = hidden[i * ROWS : (i + 1) * ROWS]


def combine(mine, got, from_chip, left, behind):
    _, rows, width = from_chip.shape
    n_outs = rows // ROWS
    width += sum(x.shape[1] for x in left)
    return pl.pallas_call(
        functools.partial(combine_kernel, len(left), n_outs),
        in_specs=[spec(pltpu.VMEM)] * (3 + len(left)) + [spec(pl.ANY)] * len(behind),
        out_specs=[spec(pltpu.VMEM)] * n_outs,
        out_shape=[jax.ShapeDtypeStruct((ROWS, width), jnp.bfloat16)] * n_outs,
        compiler_params=params(2),
        cost_estimate=COST,
        name="combine",
    )(mine, got, from_chip, *left, *behind)


def down_kernel(n_pieces, has_acc, last, segments, *refs):
    pieces, refs = refs[:n_pieces], refs[n_pieces:]
    down_ref, refs = refs[0], refs[1:]
    where = here(down_ref.shape[0] // 2)
    prev_ref, refs = (refs[0], refs[1:]) if has_acc else (None, refs)
    outs, (acc_ref, lhs_ref) = refs[:-2], refs[-2:]
    at = 0
    for piece in pieces:
        lhs_ref[at : at + piece.shape[0], :] = piece[...]
        at += piece.shape[0]
    lhs_ref[at:, :] = jnp.zeros_like(lhs_ref[at:, :])
    total = at
    for a, b in pieces_of(acc_ref.shape[1], 2 * TILE):
        part = prev_ref[:, a:b] if has_acc else 0.0
        at = 0
        for sign, start, depth in segments:
            rows = pl.ds(pl.multiple_of(sign * where[0] + start, TILE) if sign else start, depth)
            product = jnp.dot(lhs_ref[:, at : at + depth], down_ref[rows, a:b], preferred_element_type=jnp.float32)
            part += product[:total]
            at += depth
        acc_ref[:, a:b] = part
    if last:
        for d, out in enumerate(outs):
            source = pl.multiple_of(place(where[1], d) * ROWS, ROWS)
            out[...] = acc_ref[pl.ds(source, ROWS), :].astype(out.dtype)


def down(pieces, down_weight, prev, segments, last):
    width = down_weight.shape[1]
    total = 4 * ROWS
    args = [*pieces, down_weight] + ([] if prev is None else [prev])
    sums = jax.ShapeDtypeStruct((total, width), jnp.float32)
    scratch = [pltpu.VMEM((max(total, 128), pieces[0].shape[1]), jnp.bfloat16)]
    if last:
        scratch = [pltpu.VMEM(sums.shape, sums.dtype)] + scratch
    return pl.pallas_call(
        functools.partial(down_kernel, len(pieces), prev is not None, last, segments),
        in_specs=[spec(pltpu.VMEM)] * len(args),
        out_specs=[spec(pltpu.VMEM)] * 4 if last else spec(pltpu.VMEM),
        scratch_shapes=scratch,
        out_shape=[jax.ShapeDtypeStruct((ROWS, width), jnp.bfloat16)] * 4 if last else sums,
        compiler_params=params(4),
        cost_estimate=COST,
        name="down",
    )(*args)


def split_by_rep(tokens, gate_weight, up_weight, down_weight):
    f32, bf16 = jnp.float32, jnp.bfloat16
    half = gate_weight.shape[1] // 2

    def swap(x, axis, step):
        n = {"rep": 2, "hid": 4, "wid": 4}[axis]
        return lax.ppermute(x, axis, [(i, i ^ step) for i in range(n)])

    tiles = half // TILE
    bounds = [0, (tiles - LAST) // 2 * TILE, (tiles - LAST) * TILE, half]
    widths = [b - a for a, b in zip(bounds[:-1], bounds[1:])]
    gate_weight, up_weight, hbm_tokens = (
        pltpu.with_memory_space_constraint(w, pltpu.HBM) for w in (gate_weight, up_weight, tokens)
    )
    down_weight = pltpu.with_memory_space_constraint(down_weight, pltpu.VMEM)

    far_own = swap(tokens, "rep", 1)
    by_hid = [swap(tokens, "hid", d) for d in (3, 2, 1)][::-1]
    early = [fetch(gate_weight, up_weight, hbm_tokens, bounds[c], widths[c]) for c in range(2)]
    own = early[0][2]
    near = join(by_hid, [own, far_own])
    far = swap(near, "rep", 1)

    weights = [w for fetched in early for w in fetched[:2]]
    mine, theirs = gate_up([own, near, far_own, far], weights, [], [])
    got = swap(theirs, "wid", 1)
    to_chip = pair_sum(mine, got, [])
    from_chip = swap(to_chip, "wid", 2)
    segments = [(bounds[2], widths[2]), (half + bounds[2], widths[2])]
    last_mine, theirs = gate_up([own, near], [gate_weight, up_weight], segments, [to_chip])
    last_got = swap(theirs, "wid", 1)
    keep, give = combine(mine, got, from_chip, [], [])
    last_to_chip = pair_sum(last_mine, last_got, [give])
    last_from_chip = swap(last_to_chip, "wid", 2)
    (rest,) = combine(last_mine, last_got, last_from_chip, [swap(give, "rep", 1)], [])

    def gather(hidden, behind):
        other = swap(hidden, "wid", 2)
        return [hidden, other, swap(hidden, "wid", 1), swap(join([other], behind), "wid", 1)]

    acc = down(gather(keep, [rest]), down_weight, None, [(1, 0, bounds[2])], False)
    rest_segments = [(-1, half, bounds[2])] + [(0, start, width) for start, width in segments]
    acc = down(gather(rest, [acc]), down_weight, acc, rest_segments, True)

    mixed = acc[0].astype(f32)
    for d in (3, 2, 1):
        mixed = mixed + swap(acc[d], "hid", d).astype(f32)
    return mixed.astype(bf16)


def solution(mesh):
    n_rep, n_hid, n_wid = (mesh.shape[a] for a in ("rep", "hid", "wid"))

    def on_device(tokens, gate_weight, up_weight, down_weight):
        fits = (
            (n_rep, n_hid, n_wid) == (2, 4, 4)
            and gate_weight.shape[1] % (n_rep * TILE) == 0
            and tokens.shape[0] == ROWS
        )
        if not fits:
            return plain(tokens, gate_weight, up_weight, down_weight)
        return split_by_rep(tokens, gate_weight, up_weight, down_weight)

    return jax.shard_map(
        on_device,
        mesh=mesh,
        in_specs=(P(("rep", "hid"), "wid"), P("wid", "hid"), P("wid", "hid"), P("hid", "wid")),
        out_specs=P(("rep", "hid"), "wid"),
        check_vma=False,
    )
```

```python
import functools

import jax
import jax.numpy as jnp
from jax import lax
from jax.experimental import pallas as pl
from jax.experimental.pallas import tpu as pltpu
from jax.sharding import PartitionSpec as P

TILE = 256
LAST = 4
ROWS = 16
COST = pl.CostEstimate(flops=0, bytes_accessed=1024, transcendentals=0)


def plain(tokens, gate_weight, up_weight, down_weight):
    piece = lax.all_gather(tokens, "hid", axis=0, tiled=True)
    gate_rows = jnp.dot(piece, gate_weight, preferred_element_type=jnp.float32)
    up_rows = jnp.dot(piece, up_weight, preferred_element_type=jnp.float32)
    partial_terms = jnp.stack([gate_rows, up_rows], 0)
    summed = lax.psum(partial_terms.astype(jnp.bfloat16), "wid").astype(jnp.float32)
    hidden = (jax.nn.silu(summed[0]) * summed[1]).astype(jnp.bfloat16)
    return lax.psum_scatter(
        jnp.dot(hidden, down_weight, preferred_element_type=jnp.float32).astype(jnp.bfloat16),
        "hid",
        scatter_dimension=0,
        tiled=True,
    )


def pieces_of(width, most):
    first = width % most
    edges = ([0] if first else []) + list(range(first, width + 1, most))
    return list(zip(edges[:-1], edges[1:]))


def place(wid, d):
    step = wid ^ d
    return (step % 2) * 2 + step // 2


def here(half):
    return lax.axis_index("rep") * half, lax.axis_index("wid")


def spec(space):
    return pl.BlockSpec(memory_space=space)


def params(mib):
    return pltpu.CompilerParams(vmem_limit_bytes=mib * 2**20)


def column_copies(source_ref, out_ref, segments, sems):
    copies, cuts, at = [], [], 0
    for start, width in segments:
        for a, b in pieces_of(width, 2 * TILE):
            source = source_ref.at[:, pl.ds(pl.multiple_of(start + a, TILE), b - a)]
            copies.append(pltpu.make_async_copy(source, out_ref.at[:, at + a : at + b], sems.at[len(copies)]))
            cuts.append((at + a, at + b))
        at += width
    return copies, cuts


def fetch_kernel(first, gate_ref, up_ref, tokens_ref, gate_out, up_out, tokens_out, sems):
    where = here(gate_ref.shape[1] // 2)
    copies = [pltpu.make_async_copy(tokens_ref, tokens_out, sems.at[2, 0])]
    for k, (source, out) in enumerate(((gate_ref, gate_out), (up_ref, up_out))):
        copies += column_copies(source, out, [(where[0] + first, out.shape[1])], sems.at[k])[0]
    for copy in copies:
        copy.start()
    for copy in copies:
        copy.wait()


def fetch(gate, up, tokens, first, width):
    depth = gate.shape[0]
    return pl.pallas_call(
        functools.partial(fetch_kernel, first),
        in_specs=[spec(pltpu.HBM)] * 3,
        out_specs=[spec(pltpu.VMEM)] * 3,
        out_shape=[pltpu.VMEM(x, jnp.bfloat16) for x in ((depth, width), (depth, width), tokens.shape)],
        scratch_shapes=[pltpu.SemaphoreType.DMA((3, len(pieces_of(width, 2 * TILE))))],
        compiler_params=params(1),
        cost_estimate=COST,
        name="fetch",
    )(gate, up, tokens)


def join_kernel(n, first, *refs):
    out_ref, at = refs[-1], 0
    for ref in refs[:n]:
        out_ref[at : at + ref.shape[0], :] = ref[:, first : first + out_ref.shape[1]]
        at += ref.shape[0]


def join(arrays, behind, first=0, width=None):
    rows, width = sum(a.shape[0] for a in arrays), width or arrays[0].shape[1]
    return pl.pallas_call(
        functools.partial(join_kernel, len(arrays), first),
        in_specs=[spec(pltpu.VMEM)] * len(arrays) + [spec(pl.ANY)] * len(behind),
        out_specs=spec(pltpu.VMEM),
        out_shape=jax.ShapeDtypeStruct((rows, width), arrays[0].dtype),
        compiler_params=params(1),
        cost_estimate=COST,
        name="join",
    )(*arrays, *behind)


def gate_up_kernel(n_arrays, n_pairs, segments, *refs):
    where = here(0)
    arrays, weights = refs[:n_arrays], refs[n_arrays : n_arrays + 2 * n_pairs]
    if segments:
        mine_ref, theirs_ref, x_ref, w_ref, sems = refs[-5:]
        copies = [column_copies(weights[k], w_ref.at[k], segments, sems.at[k]) for k in range(2)]
        cuts = copies[0][1]
        for i in range(len(cuts)):
            for k in range(2):
                copies[k][0][i].start()
    else:
        mine_ref, theirs_ref, x_ref = refs[-3:]
        cuts, at, pair_of = [], 0, {}
        for p in range(n_pairs):
            width = weights[2 * p].shape[1]
            for a, b in pieces_of(width, 2 * TILE):
                pair_of[at + a] = p, a, b
                cuts.append((at + a, at + b))
            at += width
    per = x_ref.shape[0] // (4 * ROWS)
    b = 0
    for array in arrays:
        for at in range(0, array.shape[0], ROWS):
            to = (place(where[1], b % 4) * per + b // 4) * ROWS
            x_ref[pl.ds(pl.multiple_of(to, ROWS), ROWS), :] = array[at : at + ROWS, :]
            b += 1
    half = x_ref.shape[0] // 2
    for i, (a, b) in enumerate(cuts):
        for k in range(2):
            if segments:
                copies[k][0][i].wait()
                weight = w_ref[k, :, a:b]
            else:
                p, first, end = pair_of[a]
                weight = weights[2 * p + k][:, first:end]
            part = jnp.dot(x_ref[...], weight, preferred_element_type=jnp.float32).astype(jnp.bfloat16)
            mine_ref[k, :, a:b] = part[:half]
            theirs_ref[k, :, a:b] = part[half:]


def gate_up(arrays, weights, segments, behind):
    depth = weights[0].shape[0]
    width = sum(w for _, w in segments) if segments else sum(w.shape[1] for w in weights[::2])
    total = sum(a.shape[0] for a in arrays)
    scratch = [pltpu.VMEM((total, depth), jnp.bfloat16)]
    if segments:
        n_cuts = sum(len(pieces_of(w, 2 * TILE)) for _, w in segments)
        scratch.append(pltpu.VMEM((2, depth, width), jnp.bfloat16))
        scratch.append(pltpu.SemaphoreType.DMA((2, n_cuts)))
    return pl.pallas_call(
        functools.partial(gate_up_kernel, len(arrays), len(weights) // 2, segments),
        in_specs=[spec(pltpu.VMEM)] * len(arrays)
        + [spec(pltpu.HBM if segments else pltpu.VMEM)] * len(weights)
        + [spec(pl.ANY)] * len(behind),
        out_specs=[spec(pltpu.VMEM)] * 2,
        scratch_shapes=scratch,
        out_shape=[jax.ShapeDtypeStruct((2, total // 2, width), jnp.bfloat16)] * 2,
        compiler_params=params(18 if segments else 4),
        cost_estimate=COST,
        name="gate_up",
    )(*arrays, *weights, *behind)


def pair_sum_kernel(mine_ref, got_ref, *refs):
    out_ref = refs[-1]
    rows = out_ref.shape[1]
    for k in range(2):
        total = mine_ref[k, rows:].astype(jnp.float32) + got_ref[k, rows:].astype(jnp.float32)
        out_ref[k] = total.astype(out_ref.dtype)


def pair_sum(mine, got, behind):
    _, rows, width = mine.shape
    return pl.pallas_call(
        pair_sum_kernel,
        in_specs=[spec(pltpu.VMEM)] * 2 + [spec(pl.ANY)] * len(behind),
        out_specs=spec(pltpu.VMEM),
        out_shape=jax.ShapeDtypeStruct((2, rows // 2, width), mine.dtype),
        compiler_params=params(2),
        cost_estimate=COST,
        name="pair_sum",
    )(mine, got, *behind)


def combine_kernel(n_left, n_outs, mine_ref, got_ref, chip_ref, *refs):
    outs = refs[-n_outs:]
    rows, first = chip_ref.shape[1], 0
    for left in refs[:n_left]:
        first = left.shape[1]
        outs[0][:, :first] = left[...]
    for a, b in pieces_of(chip_ref.shape[2], TILE):
        gate, up = (
            mine_ref[k, :rows, a:b].astype(jnp.float32)
            + got_ref[k, :rows, a:b].astype(jnp.float32)
            + chip_ref[k, :, a:b].astype(jnp.float32)
            for k in range(2)
        )
        hidden = (gate / (1 + jnp.exp(-gate)) * up).astype(jnp.bfloat16)
        for i, out in enumerate(outs):
            out[:, first + a : first + b] = hidden[i * ROWS : (i + 1) * ROWS]


def combine(mine, got, from_chip, left, behind):
    _, rows, width = from_chip.shape
    n_outs = rows // ROWS
    width += sum(x.shape[1] for x in left)
    return pl.pallas_call(
        functools.partial(combine_kernel, len(left), n_outs),
        in_specs=[spec(pltpu.VMEM)] * (3 + len(left)) + [spec(pl.ANY)] * len(behind),
        out_specs=[spec(pltpu.VMEM)] * n_outs,
        out_shape=[jax.ShapeDtypeStruct((ROWS, width), jnp.bfloat16)] * n_outs,
        compiler_params=params(2),
        cost_estimate=COST,
        name="combine",
    )(mine, got, from_chip, *left, *behind)


def down_kernel(n_pieces, has_acc, last, segments, *refs):
    pieces, refs = refs[:n_pieces], refs[n_pieces:]
    down_ref, refs = refs[0], refs[1:]
    where = here(down_ref.shape[0] // 2)
    prev_ref, refs = (refs[0], refs[1:]) if has_acc else (None, refs)
    outs, (acc_ref, lhs_ref) = refs[:-2], refs[-2:]
    at = 0
    for piece in pieces:
        lhs_ref[at : at + piece.shape[0], :] = piece[...]
        at += piece.shape[0]
    lhs_ref[at:, :] = jnp.zeros_like(lhs_ref[at:, :])
    total = at
    for a, b in pieces_of(acc_ref.shape[1], 2 * TILE):
        part = prev_ref[:, a:b] if has_acc else 0.0
        at = 0
        for sign, start, depth in segments:
            rows = pl.ds(pl.multiple_of(sign * where[0] + start, TILE) if sign else start, depth)
            product = jnp.dot(lhs_ref[:, at : at + depth], down_ref[rows, a:b], preferred_element_type=jnp.float32)
            part += product[:total]
            at += depth
        acc_ref[:, a:b] = part
    if last:
        for d, out in enumerate(outs):
            source = pl.multiple_of(place(where[1], d) * ROWS, ROWS)
            out[...] = acc_ref[pl.ds(source, ROWS), :].astype(out.dtype)


def down(pieces, down_weight, prev, segments, last):
    width = down_weight.shape[1]
    total = 4 * ROWS
    args = [*pieces, down_weight] + ([] if prev is None else [prev])
    sums = jax.ShapeDtypeStruct((total, width), jnp.float32)
    scratch = [pltpu.VMEM((max(total, 128), pieces[0].shape[1]), jnp.bfloat16)]
    if last:
        scratch = [pltpu.VMEM(sums.shape, sums.dtype)] + scratch
    return pl.pallas_call(
        functools.partial(down_kernel, len(pieces), prev is not None, last, segments),
        in_specs=[spec(pltpu.VMEM)] * len(args),
        out_specs=[spec(pltpu.VMEM)] * 4 if last else spec(pltpu.VMEM),
        scratch_shapes=scratch,
        out_shape=[jax.ShapeDtypeStruct((ROWS, width), jnp.bfloat16)] * 4 if last else sums,
        compiler_params=params(4),
        cost_estimate=COST,
        name="down",
    )(*args)


def split_by_rep(tokens, gate_weight, up_weight, down_weight):
    f32, bf16 = jnp.float32, jnp.bfloat16
    half = gate_weight.shape[1] // 2

    def swap(x, axis, step):
        n = {"rep": 2, "hid": 4, "wid": 4}[axis]
        return lax.ppermute(x, axis, [(i, i ^ step) for i in range(n)])

    tiles = half // TILE
    bounds = [0, (tiles - LAST + 1) // 2 * TILE, (tiles - LAST) * TILE, half]
    widths = [b - a for a, b in zip(bounds[:-1], bounds[1:])]
    gate_weight, up_weight, hbm_tokens = (
        pltpu.with_memory_space_constraint(w, pltpu.HBM) for w in (gate_weight, up_weight, tokens)
    )
    down_weight = pltpu.with_memory_space_constraint(down_weight, pltpu.VMEM)

    by_hid = {d: swap(tokens, "hid", d) for d in (1, 3, 2)}
    far_own, far_1 = swap(tokens, "rep", 1), swap(by_hid[1], "rep", 1)
    early = [fetch(gate_weight, up_weight, hbm_tokens, bounds[c], widths[c]) for c in range(2)]
    own = early[0][2]
    near = join([by_hid[2], by_hid[3]], [own, far_own, far_1])
    far = swap(near, "rep", 1)
    arrays = [own, by_hid[1], near, far_own, far_1, far]

    weights = [w for fetched in early for w in fetched[:2]]
    mine, theirs = gate_up(arrays, weights, [], [])
    got = swap(theirs, "wid", 1)
    to_chip = pair_sum(mine, got, [])
    from_chip = swap(to_chip, "wid", 2)
    segments = [(bounds[2], widths[2]), (half + bounds[2], widths[2])]
    last_mine, theirs = gate_up(arrays[:3], [gate_weight, up_weight], segments, [to_chip])
    last_got = swap(theirs, "wid", 1)
    keep, give = combine(mine, got, from_chip, [], [])
    last_to_chip = pair_sum(last_mine, last_got, [give])
    last_from_chip = swap(last_to_chip, "wid", 2)
    (rest,) = combine(last_mine, last_got, last_from_chip, [swap(give, "rep", 1)], [])

    def gather(hidden, behind):
        other = swap(hidden, "wid", 2)
        return [hidden, other, swap(hidden, "wid", 1), swap(join([other], behind), "wid", 1)]

    acc = down(gather(keep, [rest]), down_weight, None, [(1, 0, bounds[2])], False)
    rest_segments = [(-1, half, bounds[2])] + [(0, start, width) for start, width in segments]
    acc = down(gather(rest, [acc]), down_weight, acc, rest_segments, True)

    mixed = acc[0].astype(f32)
    for d in (3, 2, 1):
        mixed = mixed + swap(acc[d], "hid", d).astype(f32)
    return mixed.astype(bf16)


def solution(mesh):
    n_rep, n_hid, n_wid = (mesh.shape[a] for a in ("rep", "hid", "wid"))

    def on_device(tokens, gate_weight, up_weight, down_weight):
        fits = (
            (n_rep, n_hid, n_wid) == (2, 4, 4)
            and gate_weight.shape[1] % (n_rep * TILE) == 0
            and tokens.shape[0] == ROWS
        )
        if not fits:
            return plain(tokens, gate_weight, up_weight, down_weight)
        return split_by_rep(tokens, gate_weight, up_weight, down_weight)

    return jax.shard_map(
        on_device,
        mesh=mesh,
        in_specs=(P(("rep", "hid"), "wid"), P("wid", "hid"), P("wid", "hid"), P("hid", "wid")),
        out_specs=P(("rep", "hid"), "wid"),
        check_vma=False,
    )
```

```python
import functools

import jax
import jax.numpy as jnp
from jax import lax
from jax.experimental import pallas as pl
from jax.experimental.pallas import tpu as pltpu
from jax.sharding import PartitionSpec as P

TILE = 256
LAST = 3
ROWS = 16
COST = pl.CostEstimate(flops=0, bytes_accessed=1024, transcendentals=0)


def plain(tokens, gate_weight, up_weight, down_weight):
    piece = lax.all_gather(tokens, "hid", axis=0, tiled=True)
    gate_rows = jnp.dot(piece, gate_weight, preferred_element_type=jnp.float32)
    up_rows = jnp.dot(piece, up_weight, preferred_element_type=jnp.float32)
    partial_terms = jnp.stack([gate_rows, up_rows], 0)
    summed = lax.psum(partial_terms.astype(jnp.bfloat16), "wid").astype(jnp.float32)
    hidden = (jax.nn.silu(summed[0]) * summed[1]).astype(jnp.bfloat16)
    return lax.psum_scatter(
        jnp.dot(hidden, down_weight, preferred_element_type=jnp.float32).astype(jnp.bfloat16),
        "hid",
        scatter_dimension=0,
        tiled=True,
    )


def pieces_of(width, most):
    first = width % most
    edges = ([0] if first else []) + list(range(first, width + 1, most))
    return list(zip(edges[:-1], edges[1:]))


def place(wid, d):
    step = wid ^ d
    return (step % 2) * 2 + step // 2


def here(half):
    return lax.axis_index("rep") * half, lax.axis_index("wid")


def spec(space):
    return pl.BlockSpec(memory_space=space)


def params(mib):
    return pltpu.CompilerParams(vmem_limit_bytes=mib * 2**20)


def column_copies(source_ref, out_ref, segments, sems):
    copies, cuts, at = [], [], 0
    for start, width in segments:
        for a, b in pieces_of(width, 2 * TILE):
            source = source_ref.at[:, pl.ds(pl.multiple_of(start + a, TILE), b - a)]
            copies.append(pltpu.make_async_copy(source, out_ref.at[:, at + a : at + b], sems.at[len(copies)]))
            cuts.append((at + a, at + b))
        at += width
    return copies, cuts


def fetch_kernel(first, gate_ref, up_ref, tokens_ref, gate_out, up_out, tokens_out, sems):
    where = here(gate_ref.shape[1] // 2)
    copies = [pltpu.make_async_copy(tokens_ref, tokens_out, sems.at[2, 0])]
    for k, (source, out) in enumerate(((gate_ref, gate_out), (up_ref, up_out))):
        copies += column_copies(source, out, [(where[0] + first, out.shape[1])], sems.at[k])[0]
    for copy in copies:
        copy.start()
    for copy in copies:
        copy.wait()


def fetch(gate, up, tokens, first, width):
    depth = gate.shape[0]
    return pl.pallas_call(
        functools.partial(fetch_kernel, first),
        in_specs=[spec(pltpu.HBM)] * 3,
        out_specs=[spec(pltpu.VMEM)] * 3,
        out_shape=[pltpu.VMEM(x, jnp.bfloat16) for x in ((depth, width), (depth, width), tokens.shape)],
        scratch_shapes=[pltpu.SemaphoreType.DMA((3, len(pieces_of(width, 2 * TILE))))],
        compiler_params=params(1),
        cost_estimate=COST,
        name="fetch",
    )(gate, up, tokens)


def join_kernel(n, first, *refs):
    out_ref, at = refs[-1], 0
    for ref in refs[:n]:
        out_ref[at : at + ref.shape[0], :] = ref[:, first : first + out_ref.shape[1]]
        at += ref.shape[0]


def join(arrays, behind, first=0, width=None):
    rows, width = sum(a.shape[0] for a in arrays), width or arrays[0].shape[1]
    return pl.pallas_call(
        functools.partial(join_kernel, len(arrays), first),
        in_specs=[spec(pltpu.VMEM)] * len(arrays) + [spec(pl.ANY)] * len(behind),
        out_specs=spec(pltpu.VMEM),
        out_shape=jax.ShapeDtypeStruct((rows, width), arrays[0].dtype),
        compiler_params=params(1),
        cost_estimate=COST,
        name="join",
    )(*arrays, *behind)


def gate_up_kernel(n_arrays, n_pairs, segments, *refs):
    where = here(0)
    arrays, weights = refs[:n_arrays], refs[n_arrays : n_arrays + 2 * n_pairs]
    if segments:
        mine_ref, theirs_ref, x_ref, w_ref, sems = refs[-5:]
        copies = [column_copies(weights[k], w_ref.at[k], segments, sems.at[k]) for k in range(2)]
        cuts = copies[0][1]
        for i in range(len(cuts)):
            for k in range(2):
                copies[k][0][i].start()
    else:
        mine_ref, theirs_ref, x_ref = refs[-3:]
        step = weights[0].shape[1]
        cuts = [(p * step + a, p * step + b) for p in range(n_pairs) for a, b in pieces_of(step, 2 * TILE)]
    per = x_ref.shape[0] // (4 * ROWS)
    b = 0
    for array in arrays:
        for at in range(0, array.shape[0], ROWS):
            to = (place(where[1], b % 4) * per + b // 4) * ROWS
            x_ref[pl.ds(pl.multiple_of(to, ROWS), ROWS), :] = array[at : at + ROWS, :]
            b += 1
    half = x_ref.shape[0] // 2
    for i, (a, b) in enumerate(cuts):
        for k in range(2):
            if segments:
                copies[k][0][i].wait()
                weight = w_ref[k, :, a:b]
            else:
                p = a // step
                weight = weights[2 * p + k][:, a - p * step : b - p * step]
            part = jnp.dot(x_ref[...], weight, preferred_element_type=jnp.float32).astype(jnp.bfloat16)
            mine_ref[k, :, a:b] = part[:half]
            theirs_ref[k, :, a:b] = part[half:]


def gate_up(arrays, weights, segments, behind):
    depth = weights[0].shape[0]
    width = sum(w for _, w in segments) if segments else sum(w.shape[1] for w in weights[::2])
    total = sum(a.shape[0] for a in arrays)
    scratch = [pltpu.VMEM((total, depth), jnp.bfloat16)]
    if segments:
        n_cuts = sum(len(pieces_of(w, 2 * TILE)) for _, w in segments)
        scratch.append(pltpu.VMEM((2, depth, width), jnp.bfloat16))
        scratch.append(pltpu.SemaphoreType.DMA((2, n_cuts)))
    return pl.pallas_call(
        functools.partial(gate_up_kernel, len(arrays), len(weights) // 2, segments),
        in_specs=[spec(pltpu.VMEM)] * len(arrays)
        + [spec(pltpu.HBM if segments else pltpu.VMEM)] * len(weights)
        + [spec(pl.ANY)] * len(behind),
        out_specs=[spec(pltpu.VMEM)] * 2,
        scratch_shapes=scratch,
        out_shape=[jax.ShapeDtypeStruct((2, total // 2, width), jnp.bfloat16)] * 2,
        compiler_params=params(16 if segments else 4),
        cost_estimate=COST,
        name="gate_up",
    )(*arrays, *weights, *behind)


def pair_sum_kernel(mine_ref, got_ref, *refs):
    out_ref = refs[-1]
    rows = out_ref.shape[1]
    for k in range(2):
        total = mine_ref[k, rows:].astype(jnp.float32) + got_ref[k, rows:].astype(jnp.float32)
        out_ref[k] = total.astype(out_ref.dtype)


def pair_sum(mine, got, behind):
    _, rows, width = mine.shape
    return pl.pallas_call(
        pair_sum_kernel,
        in_specs=[spec(pltpu.VMEM)] * 2 + [spec(pl.ANY)] * len(behind),
        out_specs=spec(pltpu.VMEM),
        out_shape=jax.ShapeDtypeStruct((2, rows // 2, width), mine.dtype),
        compiler_params=params(2),
        cost_estimate=COST,
        name="pair_sum",
    )(mine, got, *behind)


def combine_kernel(n_left, n_outs, mine_ref, got_ref, chip_ref, *refs):
    outs = refs[-n_outs:]
    rows, first = chip_ref.shape[1], 0
    for left in refs[:n_left]:
        first = left.shape[1]
        outs[0][:, :first] = left[...]
    for a, b in pieces_of(chip_ref.shape[2], TILE):
        gate, up = (
            mine_ref[k, :rows, a:b].astype(jnp.float32)
            + got_ref[k, :rows, a:b].astype(jnp.float32)
            + chip_ref[k, :, a:b].astype(jnp.float32)
            for k in range(2)
        )
        hidden = (gate / (1 + jnp.exp(-gate)) * up).astype(jnp.bfloat16)
        for i, out in enumerate(outs):
            out[:, first + a : first + b] = hidden[i * ROWS : (i + 1) * ROWS]


def combine(mine, got, from_chip, left, behind):
    _, rows, width = from_chip.shape
    n_outs = rows // ROWS
    width += sum(x.shape[1] for x in left)
    return pl.pallas_call(
        functools.partial(combine_kernel, len(left), n_outs),
        in_specs=[spec(pltpu.VMEM)] * (3 + len(left)) + [spec(pl.ANY)] * len(behind),
        out_specs=[spec(pltpu.VMEM)] * n_outs,
        out_shape=[jax.ShapeDtypeStruct((ROWS, width), jnp.bfloat16)] * n_outs,
        compiler_params=params(2),
        cost_estimate=COST,
        name="combine",
    )(mine, got, from_chip, *left, *behind)


def down_kernel(n_pieces, n_behind, has_acc, last, segments, *refs):
    pieces, refs = refs[:n_pieces], refs[n_pieces:]
    down_ref, refs = refs[0], refs[1:]
    where = here(down_ref.shape[0] // 2)
    prev_ref, refs = (refs[0], refs[1:]) if has_acc else (None, refs)
    refs = refs[n_behind:]
    outs, (acc_ref, lhs_ref) = refs[:-2], refs[-2:]
    at = 0
    for piece in pieces:
        lhs_ref[at : at + piece.shape[0], :] = piece[...]
        at += piece.shape[0]
    lhs_ref[at:, :] = jnp.zeros_like(lhs_ref[at:, :])
    total = at
    for a, b in pieces_of(acc_ref.shape[1], 2 * TILE):
        part = prev_ref[:, a:b] if has_acc else 0.0
        at = 0
        for sign, start, depth in segments:
            rows = pl.ds(pl.multiple_of(sign * where[0] + start, TILE) if sign else start, depth)
            product = jnp.dot(lhs_ref[:, at : at + depth], down_ref[rows, a:b], preferred_element_type=jnp.float32)
            part += product[:total]
            at += depth
        acc_ref[:, a:b] = part
    if last:
        for d, out in enumerate(outs):
            source = pl.multiple_of(place(where[1], d) * ROWS, ROWS)
            out[...] = acc_ref[pl.ds(source, ROWS), :].astype(out.dtype)


def down(pieces, down_weight, prev, segments, last, behind):
    width = down_weight.shape[1]
    total = 4 * ROWS
    args = [*pieces, down_weight] + ([] if prev is None else [prev])
    sums = jax.ShapeDtypeStruct((total, width), jnp.float32)
    scratch = [pltpu.VMEM((max(total, 128), pieces[0].shape[1]), jnp.bfloat16)]
    if last:
        scratch = [pltpu.VMEM(sums.shape, sums.dtype)] + scratch
    return pl.pallas_call(
        functools.partial(down_kernel, len(pieces), len(behind), prev is not None, last, segments),
        in_specs=[spec(pltpu.VMEM)] * len(args) + [spec(pl.ANY)] * len(behind),
        out_specs=[spec(pltpu.VMEM)] * 4 if last else spec(pltpu.VMEM),
        scratch_shapes=scratch,
        out_shape=[jax.ShapeDtypeStruct((ROWS, width), jnp.bfloat16)] * 4 if last else sums,
        compiler_params=params(4),
        cost_estimate=COST,
        name="down",
    )(*args, *behind)


def split_by_rep(tokens, gate_weight, up_weight, down_weight):
    f32, bf16 = jnp.float32, jnp.bfloat16
    half = gate_weight.shape[1] // 2

    def swap(x, axis, step):
        n = {"rep": 2, "hid": 4, "wid": 4}[axis]
        return lax.ppermute(x, axis, [(i, i ^ step) for i in range(n)])

    tiles = half // TILE
    bounds = [0, (tiles - LAST) // 2 * TILE, (tiles - LAST) * TILE, half]
    widths = [b - a for a, b in zip(bounds[:-1], bounds[1:])]
    gate_weight, up_weight, hbm_tokens = (
        pltpu.with_memory_space_constraint(w, pltpu.HBM) for w in (gate_weight, up_weight, tokens)
    )
    down_weight = pltpu.with_memory_space_constraint(down_weight, pltpu.VMEM)

    far_own = swap(tokens, "rep", 1)
    by_hid = [swap(tokens, "hid", d) for d in (3, 2, 1)][::-1]
    early = [fetch(gate_weight, up_weight, hbm_tokens, bounds[c], widths[c]) for c in range(2)]
    own = early[0][2]
    near = join(by_hid, [own, far_own])
    far = swap(near, "rep", 1)

    weights = [w for fetched in early for w in fetched[:2]]
    mine, theirs = gate_up([own, near, far_own, far], weights, [], [])
    got = swap(theirs, "wid", 1)
    to_chip = pair_sum(mine, got, [])
    from_chip = swap(to_chip, "wid", 2)
    segments = [(bounds[2], widths[2]), (half + bounds[2], widths[2])]
    last_mine, theirs = gate_up([own, near], [gate_weight, up_weight], segments, [to_chip])
    last_got = swap(theirs, "wid", 1)
    keep, give = combine(mine, got, from_chip, [], [])
    far_columns = swap(give, "rep", 1)
    last_to_chip = pair_sum(last_mine, last_got, [give])
    last_from_chip = swap(last_to_chip, "wid", 2)
    (rest,) = combine(last_mine, last_got, last_from_chip, [], [])

    def gather(hidden, behind):
        other = swap(hidden, "wid", 2)
        held = join([other], behind)
        return (hidden, other, swap(hidden, "wid", 1), swap(held, "wid", 1)), [held]

    first, _ = gather(keep, [rest])
    second, held = gather(far_columns, [])
    acc = down(first, down_weight, None, [(1, 0, bounds[2])], False, held)
    third, held = gather(rest, [acc])
    acc = down(second, down_weight, acc, [(-1, half, bounds[2])], False, held)
    acc = down(third, down_weight, acc, [(0, start, width) for start, width in segments], True, [])

    mixed = acc[0].astype(f32)
    for d in (3, 2, 1):
        mixed = mixed + swap(acc[d], "hid", d).astype(f32)
    return mixed.astype(bf16)


def solution(mesh):
    n_rep, n_hid, n_wid = (mesh.shape[a] for a in ("rep", "hid", "wid"))

    def on_device(tokens, gate_weight, up_weight, down_weight):
        fits = (
            (n_rep, n_hid, n_wid) == (2, 4, 4)
            and gate_weight.shape[1] % (n_rep * TILE) == 0
            and tokens.shape[0] == ROWS
        )
        if not fits:
            return plain(tokens, gate_weight, up_weight, down_weight)
        return split_by_rep(tokens, gate_weight, up_weight, down_weight)

    return jax.shard_map(
        on_device,
        mesh=mesh,
        in_specs=(P(("rep", "hid"), "wid"), P("wid", "hid"), P("wid", "hid"), P("hid", "wid")),
        out_specs=P(("rep", "hid"), "wid"),
        check_vma=False,
    )
```

```python
import functools

import jax
import jax.numpy as jnp
from jax import lax
from jax.experimental import pallas as pl
from jax.experimental.pallas import tpu as pltpu
from jax.sharding import PartitionSpec as P

TILE = 256
LAST = 3
ROWS = 16
COST = pl.CostEstimate(flops=0, bytes_accessed=1024, transcendentals=0)


def plain(tokens, gate_weight, up_weight, down_weight):
    piece = lax.all_gather(tokens, "hid", axis=0, tiled=True)
    gate_rows = jnp.dot(piece, gate_weight, preferred_element_type=jnp.float32)
    up_rows = jnp.dot(piece, up_weight, preferred_element_type=jnp.float32)
    partial_terms = jnp.stack([gate_rows, up_rows], 0)
    summed = lax.psum(partial_terms.astype(jnp.bfloat16), "wid").astype(jnp.float32)
    hidden = (jax.nn.silu(summed[0]) * summed[1]).astype(jnp.bfloat16)
    return lax.psum_scatter(
        jnp.dot(hidden, down_weight, preferred_element_type=jnp.float32).astype(jnp.bfloat16),
        "hid",
        scatter_dimension=0,
        tiled=True,
    )


def pieces_of(width, most):
    first = width % most
    edges = ([0] if first else []) + list(range(first, width + 1, most))
    return list(zip(edges[:-1], edges[1:]))


def place(wid, d):
    step = wid ^ d
    return (step % 2) * 2 + step // 2


def here(half):
    return lax.axis_index("rep") * half, lax.axis_index("wid")


def spec(space):
    return pl.BlockSpec(memory_space=space)


def params(mib):
    return pltpu.CompilerParams(vmem_limit_bytes=mib * 2**20)


def column_copies(source_ref, out_ref, segments, sems):
    copies, cuts, at = [], [], 0
    for start, width in segments:
        for a, b in pieces_of(width, 2 * TILE):
            source = source_ref.at[:, pl.ds(pl.multiple_of(start + a, TILE), b - a)]
            copies.append(pltpu.make_async_copy(source, out_ref.at[:, at + a : at + b], sems.at[len(copies)]))
            cuts.append((at + a, at + b))
        at += width
    return copies, cuts


def fetch_kernel(first, gate_ref, up_ref, tokens_ref, gate_out, up_out, tokens_out, sems):
    where = here(gate_ref.shape[1] // 2)
    copies = [pltpu.make_async_copy(tokens_ref, tokens_out, sems.at[2, 0])]
    for k, (source, out) in enumerate(((gate_ref, gate_out), (up_ref, up_out))):
        copies += column_copies(source, out, [(where[0] + first, out.shape[1])], sems.at[k])[0]
    for copy in copies:
        copy.start()
    for copy in copies:
        copy.wait()


def fetch(gate, up, tokens, first, width):
    depth = gate.shape[0]
    return pl.pallas_call(
        functools.partial(fetch_kernel, first),
        in_specs=[spec(pltpu.HBM)] * 3,
        out_specs=[spec(pltpu.VMEM)] * 3,
        out_shape=[pltpu.VMEM(x, jnp.bfloat16) for x in ((depth, width), (depth, width), tokens.shape)],
        scratch_shapes=[pltpu.SemaphoreType.DMA((3, len(pieces_of(width, 2 * TILE))))],
        compiler_params=params(1),
        cost_estimate=COST,
        name="fetch",
    )(gate, up, tokens)


def join_kernel(n, first, *refs):
    out_ref, at = refs[-1], 0
    for ref in refs[:n]:
        out_ref[at : at + ref.shape[0], :] = ref[:, first : first + out_ref.shape[1]]
        at += ref.shape[0]


def join(arrays, behind, first=0, width=None):
    rows, width = sum(a.shape[0] for a in arrays), width or arrays[0].shape[1]
    return pl.pallas_call(
        functools.partial(join_kernel, len(arrays), first),
        in_specs=[spec(pltpu.VMEM)] * len(arrays) + [spec(pl.ANY)] * len(behind),
        out_specs=spec(pltpu.VMEM),
        out_shape=jax.ShapeDtypeStruct((rows, width), arrays[0].dtype),
        compiler_params=params(1),
        cost_estimate=COST,
        name="join",
    )(*arrays, *behind)


def gate_up_kernel(n_arrays, n_pairs, segments, *refs):
    where = here(0)
    arrays, weights = refs[:n_arrays], refs[n_arrays : n_arrays + 2 * n_pairs]
    if segments:
        mine_ref, theirs_ref, x_ref, w_ref, sems = refs[-5:]
        copies = [column_copies(weights[k], w_ref.at[k], segments, sems.at[k]) for k in range(2)]
        cuts = copies[0][1]
        for i in range(len(cuts)):
            for k in range(2):
                copies[k][0][i].start()
    else:
        mine_ref, theirs_ref, x_ref = refs[-3:]
        step = weights[0].shape[1]
        cuts = [(p * step + a, p * step + b) for p in range(n_pairs) for a, b in pieces_of(step, 2 * TILE)]
    per = x_ref.shape[0] // (4 * ROWS)
    b = 0
    for array in arrays:
        for at in range(0, array.shape[0], ROWS):
            to = (place(where[1], b % 4) * per + b // 4) * ROWS
            x_ref[pl.ds(pl.multiple_of(to, ROWS), ROWS), :] = array[at : at + ROWS, :]
            b += 1
    half = x_ref.shape[0] // 2
    for i, (a, b) in enumerate(cuts):
        for k in range(2):
            if segments:
                copies[k][0][i].wait()
                weight = w_ref[k, :, a:b]
            else:
                p = a // step
                weight = weights[2 * p + k][:, a - p * step : b - p * step]
            part = jnp.dot(x_ref[...], weight, preferred_element_type=jnp.float32).astype(jnp.bfloat16)
            mine_ref[k, :, a:b] = part[:half]
            theirs_ref[k, :, a:b] = part[half:]


def gate_up(arrays, weights, segments, behind):
    depth = weights[0].shape[0]
    width = sum(w for _, w in segments) if segments else sum(w.shape[1] for w in weights[::2])
    total = sum(a.shape[0] for a in arrays)
    scratch = [pltpu.VMEM((total, depth), jnp.bfloat16)]
    if segments:
        n_cuts = sum(len(pieces_of(w, 2 * TILE)) for _, w in segments)
        scratch.append(pltpu.VMEM((2, depth, width), jnp.bfloat16))
        scratch.append(pltpu.SemaphoreType.DMA((2, n_cuts)))
    return pl.pallas_call(
        functools.partial(gate_up_kernel, len(arrays), len(weights) // 2, segments),
        in_specs=[spec(pltpu.VMEM)] * len(arrays)
        + [spec(pltpu.HBM if segments else pltpu.VMEM)] * len(weights)
        + [spec(pl.ANY)] * len(behind),
        out_specs=[spec(pltpu.VMEM)] * 2,
        scratch_shapes=scratch,
        out_shape=[jax.ShapeDtypeStruct((2, total // 2, width), jnp.bfloat16)] * 2,
        compiler_params=params(16 if segments else 4),
        cost_estimate=COST,
        name="gate_up",
    )(*arrays, *weights, *behind)


def pair_sum_kernel(mine_ref, got_ref, *refs):
    out_ref = refs[-1]
    rows = out_ref.shape[1]
    for k in range(2):
        total = mine_ref[k, rows:].astype(jnp.float32) + got_ref[k, rows:].astype(jnp.float32)
        out_ref[k] = total.astype(out_ref.dtype)


def pair_sum(mine, got, behind):
    _, rows, width = mine.shape
    return pl.pallas_call(
        pair_sum_kernel,
        in_specs=[spec(pltpu.VMEM)] * 2 + [spec(pl.ANY)] * len(behind),
        out_specs=spec(pltpu.VMEM),
        out_shape=jax.ShapeDtypeStruct((2, rows // 2, width), mine.dtype),
        compiler_params=params(2),
        cost_estimate=COST,
        name="pair_sum",
    )(mine, got, *behind)


def later_kernel(array_ref, *refs):
    refs[-1][...] = array_ref[...]


def later(array, behind):
    return pl.pallas_call(
        later_kernel,
        in_specs=[spec(pltpu.VMEM)] + [spec(pl.ANY)] * len(behind),
        out_specs=spec(pltpu.VMEM),
        out_shape=jax.ShapeDtypeStruct(array.shape, array.dtype),
        compiler_params=params(1),
        cost_estimate=COST,
        name="later",
    )(array, *behind)


def combine_kernel(n_left, n_outs, mine_ref, got_ref, chip_ref, *refs):
    outs = refs[-n_outs:]
    rows, first = chip_ref.shape[1], 0
    for left in refs[:n_left]:
        first = left.shape[1]
        outs[0][:, :first] = left[...]
    for a, b in pieces_of(chip_ref.shape[2], TILE):
        gate, up = (
            mine_ref[k, :rows, a:b].astype(jnp.float32)
            + got_ref[k, :rows, a:b].astype(jnp.float32)
            + chip_ref[k, :, a:b].astype(jnp.float32)
            for k in range(2)
        )
        hidden = (gate / (1 + jnp.exp(-gate)) * up).astype(jnp.bfloat16)
        for i, out in enumerate(outs):
            out[:, first + a : first + b] = hidden[i * ROWS : (i + 1) * ROWS]


def combine(mine, got, from_chip, left, behind):
    _, rows, width = from_chip.shape
    n_outs = rows // ROWS
    width += sum(x.shape[1] for x in left)
    return pl.pallas_call(
        functools.partial(combine_kernel, len(left), n_outs),
        in_specs=[spec(pltpu.VMEM)] * (3 + len(left)) + [spec(pl.ANY)] * len(behind),
        out_specs=[spec(pltpu.VMEM)] * n_outs,
        out_shape=[jax.ShapeDtypeStruct((ROWS, width), jnp.bfloat16)] * n_outs,
        compiler_params=params(2),
        cost_estimate=COST,
        name="combine",
    )(mine, got, from_chip, *left, *behind)


def down_kernel(n_pieces, n_behind, has_acc, last, segments, *refs):
    pieces, refs = refs[:n_pieces], refs[n_pieces:]
    down_ref, refs = refs[0], refs[1:]
    where = here(down_ref.shape[0] // 2)
    prev_ref, refs = (refs[0], refs[1:]) if has_acc else (None, refs)
    refs = refs[n_behind:]
    outs, (acc_ref, lhs_ref) = refs[:-2], refs[-2:]
    at = 0
    for piece in pieces:
        lhs_ref[at : at + piece.shape[0], :] = piece[...]
        at += piece.shape[0]
    lhs_ref[at:, :] = jnp.zeros_like(lhs_ref[at:, :])
    total = at
    for a, b in pieces_of(acc_ref.shape[1], 2 * TILE):
        part = prev_ref[:, a:b] if has_acc else 0.0
        at = 0
        for sign, start, depth in segments:
            rows = pl.ds(pl.multiple_of(sign * where[0] + start, TILE) if sign else start, depth)
            product = jnp.dot(lhs_ref[:, at : at + depth], down_ref[rows, a:b], preferred_element_type=jnp.float32)
            part += product[:total]
            at += depth
        acc_ref[:, a:b] = part
    if last:
        for d, out in enumerate(outs):
            source = pl.multiple_of(place(where[1], d) * ROWS, ROWS)
            out[...] = acc_ref[pl.ds(source, ROWS), :].astype(out.dtype)


def down(pieces, down_weight, prev, segments, last, behind):
    width = down_weight.shape[1]
    total = 4 * ROWS
    args = [*pieces, down_weight] + ([] if prev is None else [prev])
    sums = jax.ShapeDtypeStruct((total, width), jnp.float32)
    scratch = [pltpu.VMEM((max(total, 128), pieces[0].shape[1]), jnp.bfloat16)]
    if last:
        scratch = [pltpu.VMEM(sums.shape, sums.dtype)] + scratch
    return pl.pallas_call(
        functools.partial(down_kernel, len(pieces), len(behind), prev is not None, last, segments),
        in_specs=[spec(pltpu.VMEM)] * len(args) + [spec(pl.ANY)] * len(behind),
        out_specs=[spec(pltpu.VMEM)] * 4 if last else spec(pltpu.VMEM),
        scratch_shapes=scratch,
        out_shape=[jax.ShapeDtypeStruct((ROWS, width), jnp.bfloat16)] * 4 if last else sums,
        compiler_params=params(4),
        cost_estimate=COST,
        name="down",
    )(*args, *behind)


def split_by_rep(tokens, gate_weight, up_weight, down_weight):
    f32, bf16 = jnp.float32, jnp.bfloat16
    half = gate_weight.shape[1] // 2

    def swap(x, axis, step):
        n = {"rep": 2, "hid": 4, "wid": 4}[axis]
        return lax.ppermute(x, axis, [(i, i ^ step) for i in range(n)])

    tiles = half // TILE
    bounds = [0, (tiles - LAST) // 2 * TILE, (tiles - LAST) * TILE, half]
    widths = [b - a for a, b in zip(bounds[:-1], bounds[1:])]
    gate_weight, up_weight, hbm_tokens = (
        pltpu.with_memory_space_constraint(w, pltpu.HBM) for w in (gate_weight, up_weight, tokens)
    )
    down_weight = pltpu.with_memory_space_constraint(down_weight, pltpu.VMEM)

    far_own = swap(tokens, "rep", 1)
    by_hid = [swap(tokens, "hid", d) for d in (3, 2, 1)][::-1]
    early = [fetch(gate_weight, up_weight, hbm_tokens, bounds[c], widths[c]) for c in range(2)]
    own = early[0][2]
    near = join(by_hid, [own, far_own])
    far = swap(near, "rep", 1)

    weights = [w for fetched in early for w in fetched[:2]]
    mine, theirs = gate_up([own, near, far_own, far], weights, [], [])
    got = swap(theirs, "wid", 1)
    to_chip = pair_sum(mine, got, [])
    from_chip = swap(to_chip, "wid", 2)
    segments = [(bounds[2], widths[2]), (half + bounds[2], widths[2])]
    last_mine, theirs = gate_up([own, near], [gate_weight, up_weight], segments, [to_chip])
    last_got = swap(theirs, "wid", 1)
    keep, give = combine(mine, got, from_chip, [], [])
    far_columns = swap(give, "rep", 1)
    last_to_chip = pair_sum(last_mine, last_got, [give])
    last_from_chip = swap(last_to_chip, "wid", 2)
    (rest,) = combine(last_mine, last_got, last_from_chip, [], [])

    def gather(hidden, behind):
        other = swap(hidden, "wid", 2)
        held = join([other], behind)
        return (hidden, other, swap(hidden, "wid", 1), swap(held, "wid", 1)), [held]

    first, _ = gather(keep, [rest])
    second, held = gather(later(far_columns, [rest]), [])
    acc = down(first, down_weight, None, [(1, 0, bounds[2])], False, held)
    third, held = gather(rest, [acc])
    acc = down(second, down_weight, acc, [(-1, half, bounds[2])], False, held)
    acc = down(third, down_weight, acc, [(0, start, width) for start, width in segments], True, [])

    mixed = acc[0].astype(f32)
    for d in (2, 3, 1):
        mixed = mixed + swap(acc[d], "hid", d).astype(f32)
    return mixed.astype(bf16)


def solution(mesh):
    n_rep, n_hid, n_wid = (mesh.shape[a] for a in ("rep", "hid", "wid"))

    def on_device(tokens, gate_weight, up_weight, down_weight):
        fits = (
            (n_rep, n_hid, n_wid) == (2, 4, 4)
            and gate_weight.shape[1] % (n_rep * TILE) == 0
            and tokens.shape[0] == ROWS
        )
        if not fits:
            return plain(tokens, gate_weight, up_weight, down_weight)
        return split_by_rep(tokens, gate_weight, up_weight, down_weight)

    return jax.shard_map(
        on_device,
        mesh=mesh,
        in_specs=(P(("rep", "hid"), "wid"), P("wid", "hid"), P("wid", "hid"), P("hid", "wid")),
        out_specs=P(("rep", "hid"), "wid"),
        check_vma=False,
    )
```

```python
import functools

import jax
import jax.numpy as jnp
from jax import lax
from jax.experimental import pallas as pl
from jax.experimental.pallas import tpu as pltpu
from jax.sharding import PartitionSpec as P

TILE = 256
LAST = 3
ROWS = 16
COST = pl.CostEstimate(flops=0, bytes_accessed=1024, transcendentals=0)


def plain(tokens, gate_weight, up_weight, down_weight):
    piece = lax.all_gather(tokens, "hid", axis=0, tiled=True)
    gate_rows = jnp.dot(piece, gate_weight, preferred_element_type=jnp.float32)
    up_rows = jnp.dot(piece, up_weight, preferred_element_type=jnp.float32)
    partial_terms = jnp.stack([gate_rows, up_rows], 0)
    summed = lax.psum(partial_terms.astype(jnp.bfloat16), "wid").astype(jnp.float32)
    hidden = (jax.nn.silu(summed[0]) * summed[1]).astype(jnp.bfloat16)
    return lax.psum_scatter(
        jnp.dot(hidden, down_weight, preferred_element_type=jnp.float32).astype(jnp.bfloat16),
        "hid",
        scatter_dimension=0,
        tiled=True,
    )


def pieces_of(width, most):
    first = width % most
    edges = ([0] if first else []) + list(range(first, width + 1, most))
    return list(zip(edges[:-1], edges[1:]))


def place(wid, d):
    step = wid ^ d
    return (step % 2) * 2 + step // 2


def here(half):
    return lax.axis_index("rep") * half, lax.axis_index("wid")


def spec(space):
    return pl.BlockSpec(memory_space=space)


def params(mib):
    return pltpu.CompilerParams(vmem_limit_bytes=mib * 2**20)


def column_copies(source_ref, out_ref, segments, sems):
    copies, cuts, at = [], [], 0
    for start, width in segments:
        for a, b in pieces_of(width, 2 * TILE):
            source = source_ref.at[:, pl.ds(pl.multiple_of(start + a, TILE), b - a)]
            copies.append(pltpu.make_async_copy(source, out_ref.at[:, at + a : at + b], sems.at[len(copies)]))
            cuts.append((at + a, at + b))
        at += width
    return copies, cuts


def fetch_kernel(first, gate_ref, up_ref, tokens_ref, gate_out, up_out, tokens_out, sems):
    where = here(gate_ref.shape[1] // 2)
    copies = [pltpu.make_async_copy(tokens_ref, tokens_out, sems.at[2, 0])]
    for k, (source, out) in enumerate(((gate_ref, gate_out), (up_ref, up_out))):
        copies += column_copies(source, out, [(where[0] + first, out.shape[1])], sems.at[k])[0]
    for copy in copies:
        copy.start()
    for copy in copies:
        copy.wait()


def fetch(gate, up, tokens, first, width):
    depth = gate.shape[0]
    return pl.pallas_call(
        functools.partial(fetch_kernel, first),
        in_specs=[spec(pltpu.HBM)] * 3,
        out_specs=[spec(pltpu.VMEM)] * 3,
        out_shape=[pltpu.VMEM(x, jnp.bfloat16) for x in ((depth, width), (depth, width), tokens.shape)],
        scratch_shapes=[pltpu.SemaphoreType.DMA((3, len(pieces_of(width, 2 * TILE))))],
        compiler_params=params(1),
        cost_estimate=COST,
        name="fetch",
    )(gate, up, tokens)


def join_kernel(n, first, *refs):
    out_ref, at = refs[-1], 0
    for ref in refs[:n]:
        out_ref[at : at + ref.shape[0], :] = ref[:, first : first + out_ref.shape[1]]
        at += ref.shape[0]


def join(arrays, behind, first=0, width=None):
    rows, width = sum(a.shape[0] for a in arrays), width or arrays[0].shape[1]
    return pl.pallas_call(
        functools.partial(join_kernel, len(arrays), first),
        in_specs=[spec(pltpu.VMEM)] * len(arrays) + [spec(pl.ANY)] * len(behind),
        out_specs=spec(pltpu.VMEM),
        out_shape=jax.ShapeDtypeStruct((rows, width), arrays[0].dtype),
        compiler_params=params(1),
        cost_estimate=COST,
        name="join",
    )(*arrays, *behind)


def gate_up_kernel(n_arrays, n_pairs, segments, *refs):
    where = here(0)
    arrays, weights = refs[:n_arrays], refs[n_arrays : n_arrays + 2 * n_pairs]
    if segments:
        mine_ref, theirs_ref, x_ref, w_ref, sems = refs[-5:]
        copies = [column_copies(weights[k], w_ref.at[k], segments, sems.at[k]) for k in range(2)]
        cuts = copies[0][1]
        for i in range(len(cuts)):
            for k in range(2):
                copies[k][0][i].start()
    else:
        mine_ref, theirs_ref, x_ref = refs[-3:]
        step = weights[0].shape[1]
        cuts = [(p * step + a, p * step + b) for p in range(n_pairs) for a, b in pieces_of(step, 2 * TILE)]
    per = x_ref.shape[0] // (4 * ROWS)
    b = 0
    for array in arrays:
        for at in range(0, array.shape[0], ROWS):
            to = (place(where[1], b % 4) * per + b // 4) * ROWS
            x_ref[pl.ds(pl.multiple_of(to, ROWS), ROWS), :] = array[at : at + ROWS, :]
            b += 1
    half = x_ref.shape[0] // 2
    for i, (a, b) in enumerate(cuts):
        for k in range(2):
            if segments:
                copies[k][0][i].wait()
                weight = w_ref[k, :, a:b]
            else:
                p = a // step
                weight = weights[2 * p + k][:, a - p * step : b - p * step]
            part = jnp.dot(x_ref[...], weight, preferred_element_type=jnp.float32).astype(jnp.bfloat16)
            mine_ref[k, :, a:b] = part[:half]
            theirs_ref[k, :, a:b] = part[half:]


def gate_up(arrays, weights, segments, behind):
    depth = weights[0].shape[0]
    width = sum(w for _, w in segments) if segments else sum(w.shape[1] for w in weights[::2])
    total = sum(a.shape[0] for a in arrays)
    scratch = [pltpu.VMEM((total, depth), jnp.bfloat16)]
    if segments:
        n_cuts = sum(len(pieces_of(w, 2 * TILE)) for _, w in segments)
        scratch.append(pltpu.VMEM((2, depth, width), jnp.bfloat16))
        scratch.append(pltpu.SemaphoreType.DMA((2, n_cuts)))
    return pl.pallas_call(
        functools.partial(gate_up_kernel, len(arrays), len(weights) // 2, segments),
        in_specs=[spec(pltpu.VMEM)] * len(arrays)
        + [spec(pltpu.HBM if segments else pltpu.VMEM)] * len(weights)
        + [spec(pl.ANY)] * len(behind),
        out_specs=[spec(pltpu.VMEM)] * 2,
        scratch_shapes=scratch,
        out_shape=[jax.ShapeDtypeStruct((2, total // 2, width), jnp.bfloat16)] * 2,
        compiler_params=params(16 if segments else 4),
        cost_estimate=COST,
        name="gate_up",
    )(*arrays, *weights, *behind)


def pair_sum_kernel(n_parts, *refs):
    out_ref, at = refs[2 * n_parts], 0
    rows = out_ref.shape[1]
    for mine_ref, got_ref in zip(refs[:n_parts], refs[n_parts : 2 * n_parts]):
        width = got_ref.shape[2]
        for k in range(2):
            total = mine_ref[k, rows:].astype(jnp.float32) + got_ref[k, rows:].astype(jnp.float32)
            out_ref[k, :, at : at + width] = total.astype(out_ref.dtype)
        at += width


def pair_sum(mines, gots, behind):
    _, rows, _ = mines[0].shape
    width = sum(x.shape[2] for x in gots)

    def kernel(*refs):
        inputs, rest = refs[: 2 * len(mines)], refs[2 * len(mines) + len(behind) :]
        pair_sum_kernel(len(mines), *inputs, *rest)

    return pl.pallas_call(
        kernel,
        in_specs=[spec(pltpu.VMEM)] * (2 * len(mines)) + [spec(pl.ANY)] * len(behind),
        out_specs=spec(pltpu.VMEM),
        out_shape=jax.ShapeDtypeStruct((2, rows // 2, width), jnp.bfloat16),
        compiler_params=params(2),
        cost_estimate=COST,
        name="pair_sum",
    )(*mines, *gots, *behind)


def later_kernel(array_ref, *refs):
    refs[-1][...] = array_ref[...]


def later(array, behind):
    return pl.pallas_call(
        later_kernel,
        in_specs=[spec(pltpu.VMEM)] + [spec(pl.ANY)] * len(behind),
        out_specs=spec(pltpu.VMEM),
        out_shape=jax.ShapeDtypeStruct(array.shape, array.dtype),
        compiler_params=params(1),
        cost_estimate=COST,
        name="later",
    )(array, *behind)


def combine_kernel(n_parts, n_left, n_outs, *refs):
    mines, gots, chip_ref, refs = refs[:n_parts], refs[n_parts : 2 * n_parts], refs[2 * n_parts], refs[2 * n_parts + 1 :]
    lefts, outs = refs[:n_left], refs[n_left:]
    rows, at = chip_ref.shape[1], 0
    for left in lefts:
        outs[0][:, : left.shape[1]] = left[...]
    first = sum(left.shape[1] for left in lefts)
    for mine_ref, got_ref in zip(mines, gots):
        for a, b in pieces_of(got_ref.shape[2], TILE):
            gate, up = (
                mine_ref[k, :rows, a:b].astype(jnp.float32)
                + got_ref[k, :rows, a:b].astype(jnp.float32)
                + chip_ref[k, :, at + a : at + b].astype(jnp.float32)
                for k in range(2)
            )
            hidden = (gate / (1 + jnp.exp(-gate)) * up).astype(jnp.bfloat16)
            for i, out in enumerate(outs):
                out[:, first + at + a : first + at + b] = hidden[i * ROWS : (i + 1) * ROWS]
        at += got_ref.shape[2]


def combine(mines, gots, from_chip, left):
    _, rows, width = from_chip.shape
    n_outs = rows // ROWS
    width += sum(x.shape[1] for x in left)
    args = [*mines, *gots, from_chip, *left]
    return pl.pallas_call(
        functools.partial(combine_kernel, len(mines), len(left), n_outs),
        in_specs=[spec(pltpu.VMEM)] * len(args),
        out_specs=[spec(pltpu.VMEM)] * n_outs,
        out_shape=[jax.ShapeDtypeStruct((ROWS, width), jnp.bfloat16)] * n_outs,
        compiler_params=params(2),
        cost_estimate=COST,
        name="combine",
    )(*args)


def down_kernel(n_pieces, has_acc, last, segments, *refs):
    pieces, refs = refs[:n_pieces], refs[n_pieces:]
    down_ref, refs = refs[0], refs[1:]
    where = here(down_ref.shape[0] // 2)
    prev_ref, refs = (refs[0], refs[1:]) if has_acc else (None, refs)
    outs, (acc_ref, lhs_ref) = refs[:-2], refs[-2:]
    at = 0
    for piece in pieces:
        lhs_ref[at : at + piece.shape[0], :] = piece[...]
        at += piece.shape[0]
    lhs_ref[at:, :] = jnp.zeros_like(lhs_ref[at:, :])
    total = at
    for a, b in pieces_of(acc_ref.shape[1], 2 * TILE):
        part = prev_ref[:, a:b] if has_acc else 0.0
        at = 0
        for sign, start, depth in segments:
            rows = pl.ds(pl.multiple_of(sign * where[0] + start, TILE) if sign else start, depth)
            product = jnp.dot(lhs_ref[:, at : at + depth], down_ref[rows, a:b], preferred_element_type=jnp.float32)
            part += product[:total]
            at += depth
        acc_ref[:, a:b] = part
    if last:
        for d, out in enumerate(outs):
            source = pl.multiple_of(place(where[1], d) * ROWS, ROWS)
            out[...] = acc_ref[pl.ds(source, ROWS), :].astype(out.dtype)


def down(pieces, down_weight, prev, segments, last):
    width = down_weight.shape[1]
    total = 4 * ROWS
    args = [*pieces, down_weight] + ([] if prev is None else [prev])
    sums = jax.ShapeDtypeStruct((total, width), jnp.float32)
    scratch = [pltpu.VMEM((max(total, 128), pieces[0].shape[1]), jnp.bfloat16)]
    if last:
        scratch = [pltpu.VMEM(sums.shape, sums.dtype)] + scratch
    return pl.pallas_call(
        functools.partial(down_kernel, len(pieces), prev is not None, last, segments),
        in_specs=[spec(pltpu.VMEM)] * len(args),
        out_specs=[spec(pltpu.VMEM)] * 4 if last else spec(pltpu.VMEM),
        scratch_shapes=scratch,
        out_shape=[jax.ShapeDtypeStruct((ROWS, width), jnp.bfloat16)] * 4 if last else sums,
        compiler_params=params(4),
        cost_estimate=COST,
        name="down",
    )(*args)


def split_by_rep(tokens, gate_weight, up_weight, down_weight):
    f32, bf16 = jnp.float32, jnp.bfloat16
    half = gate_weight.shape[1] // 2

    def swap(x, axis, step):
        n = {"rep": 2, "hid": 4, "wid": 4}[axis]
        return lax.ppermute(x, axis, [(i, i ^ step) for i in range(n)])

    tiles = half // TILE
    bounds = [0, (tiles - LAST) // 2 * TILE, (tiles - LAST) * TILE, half]
    widths = [b - a for a, b in zip(bounds[:-1], bounds[1:])]
    gate_weight, up_weight, hbm_tokens = (
        pltpu.with_memory_space_constraint(w, pltpu.HBM) for w in (gate_weight, up_weight, tokens)
    )
    down_weight = pltpu.with_memory_space_constraint(down_weight, pltpu.VMEM)

    far_own = swap(tokens, "rep", 1)
    by_hid = [swap(tokens, "hid", d) for d in (3, 2, 1)][::-1]
    early = [fetch(gate_weight, up_weight, hbm_tokens, bounds[c], widths[c]) for c in range(2)]
    own = early[0][2]
    near = join(by_hid, [own, far_own])
    far = swap(near, "rep", 1)

    arrays = [own, near, far_own, far]
    mine_0, theirs = gate_up(arrays, early[0][:2], [], [early[1][0]])
    got_0 = swap(theirs, "wid", 1)
    mine_1, theirs = gate_up(arrays, early[1][:2], [], [mine_0])
    got_1 = swap(later(theirs, [got_0]), "wid", 1)
    mines, gots = [mine_0, mine_1], [got_0, got_1]
    to_chip = pair_sum(mines, gots, [])
    from_chip = swap(to_chip, "wid", 2)
    segments = [(bounds[2], widths[2]), (half + bounds[2], widths[2])]
    last_mine, theirs = gate_up(arrays[:2], [gate_weight, up_weight], segments, [to_chip])
    last_got = swap(theirs, "wid", 1)

    keep, give = combine(mines, gots, from_chip, [])
    last_to_chip = pair_sum([last_mine], [last_got], [give])
    last_from_chip = swap(last_to_chip, "wid", 2)
    (rest,) = combine([last_mine], [last_got], last_from_chip, [swap(give, "rep", 1)])

    def gather(hidden, behind):
        other = swap(hidden, "wid", 2)
        return [hidden, other, swap(hidden, "wid", 1), swap(join([other], behind), "wid", 1)]

    acc = down(gather(keep, [rest]), down_weight, None, [(1, 0, bounds[2])], False)
    rest_segments = [(-1, half, bounds[2])] + [(0, start, width) for start, width in segments]
    acc = down(gather(rest, [acc]), down_weight, acc, rest_segments, True)

    mixed = acc[0].astype(f32)
    for d in (3, 2, 1):
        mixed = mixed + swap(acc[d], "hid", d).astype(f32)
    return mixed.astype(bf16)


def solution(mesh):
    n_rep, n_hid, n_wid = (mesh.shape[a] for a in ("rep", "hid", "wid"))

    def on_device(tokens, gate_weight, up_weight, down_weight):
        fits = (
            (n_rep, n_hid, n_wid) == (2, 4, 4)
            and gate_weight.shape[1] % (n_rep * TILE) == 0
            and tokens.shape[0] == ROWS
        )
        if not fits:
            return plain(tokens, gate_weight, up_weight, down_weight)
        return split_by_rep(tokens, gate_weight, up_weight, down_weight)

    return jax.shard_map(
        on_device,
        mesh=mesh,
        in_specs=(P(("rep", "hid"), "wid"), P("wid", "hid"), P("wid", "hid"), P("hid", "wid")),
        out_specs=P(("rep", "hid"), "wid"),
        check_vma=False,
    )
```

```python
import functools

import jax
import jax.numpy as jnp
from jax import lax
from jax.experimental import pallas as pl
from jax.experimental.pallas import tpu as pltpu
from jax.sharding import PartitionSpec as P

TILE = 256
LAST = 3
ROWS = 16
COST = pl.CostEstimate(flops=0, bytes_accessed=1024, transcendentals=0)


def plain(tokens, gate_weight, up_weight, down_weight):
    piece = lax.all_gather(tokens, "hid", axis=0, tiled=True)
    gate_rows = jnp.dot(piece, gate_weight, preferred_element_type=jnp.float32)
    up_rows = jnp.dot(piece, up_weight, preferred_element_type=jnp.float32)
    partial_terms = jnp.stack([gate_rows, up_rows], 0)
    summed = lax.psum(partial_terms.astype(jnp.bfloat16), "wid").astype(jnp.float32)
    hidden = (jax.nn.silu(summed[0]) * summed[1]).astype(jnp.bfloat16)
    return lax.psum_scatter(
        jnp.dot(hidden, down_weight, preferred_element_type=jnp.float32).astype(jnp.bfloat16),
        "hid",
        scatter_dimension=0,
        tiled=True,
    )


def pieces_of(width, most):
    first = width % most
    edges = ([0] if first else []) + list(range(first, width + 1, most))
    return list(zip(edges[:-1], edges[1:]))


def place(wid, d):
    step = wid ^ d
    return (step % 2) * 2 + step // 2


def here(half):
    return lax.axis_index("rep") * half, lax.axis_index("wid")


def spec(space):
    return pl.BlockSpec(memory_space=space)


def params(mib):
    return pltpu.CompilerParams(vmem_limit_bytes=mib * 2**20)


def column_copies(source_ref, out_ref, segments, sems):
    copies, cuts, at = [], [], 0
    for start, width in segments:
        for a, b in pieces_of(width, 2 * TILE):
            source = source_ref.at[:, pl.ds(pl.multiple_of(start + a, TILE), b - a)]
            copies.append(pltpu.make_async_copy(source, out_ref.at[:, at + a : at + b], sems.at[len(copies)]))
            cuts.append((at + a, at + b))
        at += width
    return copies, cuts


def fetch_kernel(first, gate_ref, up_ref, tokens_ref, gate_out, up_out, tokens_out, sems):
    where = here(gate_ref.shape[1] // 2)
    copies = [pltpu.make_async_copy(tokens_ref, tokens_out, sems.at[2, 0])]
    for k, (source, out) in enumerate(((gate_ref, gate_out), (up_ref, up_out))):
        copies += column_copies(source, out, [(where[0] + first, out.shape[1])], sems.at[k])[0]
    for copy in copies:
        copy.start()
    for copy in copies:
        copy.wait()


def fetch(gate, up, tokens, first, width):
    depth = gate.shape[0]
    return pl.pallas_call(
        functools.partial(fetch_kernel, first),
        in_specs=[spec(pltpu.HBM)] * 3,
        out_specs=[spec(pltpu.VMEM)] * 3,
        out_shape=[pltpu.VMEM(x, jnp.bfloat16) for x in ((depth, width), (depth, width), tokens.shape)],
        scratch_shapes=[pltpu.SemaphoreType.DMA((3, len(pieces_of(width, 2 * TILE))))],
        compiler_params=params(1),
        cost_estimate=COST,
        name="fetch",
    )(gate, up, tokens)


def join_kernel(n, first, *refs):
    out_ref, at = refs[-1], 0
    for ref in refs[:n]:
        out_ref[at : at + ref.shape[0], :] = ref[:, first : first + out_ref.shape[1]]
        at += ref.shape[0]


def join(arrays, behind, first=0, width=None):
    rows, width = sum(a.shape[0] for a in arrays), width or arrays[0].shape[1]
    return pl.pallas_call(
        functools.partial(join_kernel, len(arrays), first),
        in_specs=[spec(pltpu.VMEM)] * len(arrays) + [spec(pl.ANY)] * len(behind),
        out_specs=spec(pltpu.VMEM),
        out_shape=jax.ShapeDtypeStruct((rows, width), arrays[0].dtype),
        compiler_params=params(1),
        cost_estimate=COST,
        name="join",
    )(*arrays, *behind)


def gate_up_kernel(n_arrays, n_pairs, segments, *refs):
    where = here(0)
    arrays, weights = refs[:n_arrays], refs[n_arrays : n_arrays + 2 * n_pairs]
    if segments:
        mine_ref, theirs_ref, x_ref, w_ref, sems = refs[-5:]
        copies = [column_copies(weights[k], w_ref.at[k], segments, sems.at[k]) for k in range(2)]
        cuts = copies[0][1]
        for i in range(len(cuts)):
            for k in range(2):
                copies[k][0][i].start()
    else:
        mine_ref, theirs_ref, x_ref = refs[-3:]
        step = weights[0].shape[1]
        cuts = [(p * step + a, p * step + b) for p in range(n_pairs) for a, b in pieces_of(step, 2 * TILE)]
    per = x_ref.shape[0] // (4 * ROWS)
    b = 0
    for array in arrays:
        for at in range(0, array.shape[0], ROWS):
            to = (place(where[1], b % 4) * per + b // 4) * ROWS
            x_ref[pl.ds(pl.multiple_of(to, ROWS), ROWS), :] = array[at : at + ROWS, :]
            b += 1
    half = x_ref.shape[0] // 2
    for i, (a, b) in enumerate(cuts):
        for k in range(2):
            if segments:
                copies[k][0][i].wait()
                weight = w_ref[k, :, a:b]
            else:
                p = a // step
                weight = weights[2 * p + k][:, a - p * step : b - p * step]
            part = jnp.dot(x_ref[...], weight, preferred_element_type=jnp.float32).astype(jnp.bfloat16)
            mine_ref[k, :, a:b] = part[:half]
            theirs_ref[k, :, a:b] = part[half:]


def gate_up(arrays, weights, segments, behind):
    depth = weights[0].shape[0]
    width = sum(w for _, w in segments) if segments else sum(w.shape[1] for w in weights[::2])
    total = sum(a.shape[0] for a in arrays)
    scratch = [pltpu.VMEM((total, depth), jnp.bfloat16)]
    if segments:
        n_cuts = sum(len(pieces_of(w, 2 * TILE)) for _, w in segments)
        scratch.append(pltpu.VMEM((2, depth, width), jnp.bfloat16))
        scratch.append(pltpu.SemaphoreType.DMA((2, n_cuts)))
    return pl.pallas_call(
        functools.partial(gate_up_kernel, len(arrays), len(weights) // 2, segments),
        in_specs=[spec(pltpu.VMEM)] * len(arrays)
        + [spec(pltpu.HBM if segments else pltpu.VMEM)] * len(weights)
        + [spec(pl.ANY)] * len(behind),
        out_specs=[spec(pltpu.VMEM)] * 2,
        scratch_shapes=scratch,
        out_shape=[jax.ShapeDtypeStruct((2, total // 2, width), jnp.bfloat16)] * 2,
        compiler_params=params(16 if segments else 4),
        cost_estimate=COST,
        name="gate_up",
    )(*arrays, *weights, *behind)


def pair_sum_kernel(n_parts, *refs):
    out_ref, at = refs[2 * n_parts], 0
    rows = out_ref.shape[1]
    for mine_ref, got_ref in zip(refs[:n_parts], refs[n_parts : 2 * n_parts]):
        width = got_ref.shape[2]
        for k in range(2):
            total = mine_ref[k, rows:].astype(jnp.float32) + got_ref[k, rows:].astype(jnp.float32)
            out_ref[k, :, at : at + width] = total.astype(out_ref.dtype)
        at += width


def pair_sum(mines, gots, behind):
    _, rows, _ = mines[0].shape
    width = sum(x.shape[2] for x in gots)

    def kernel(*refs):
        inputs, rest = refs[: 2 * len(mines)], refs[2 * len(mines) + len(behind) :]
        pair_sum_kernel(len(mines), *inputs, *rest)

    return pl.pallas_call(
        kernel,
        in_specs=[spec(pltpu.VMEM)] * (2 * len(mines)) + [spec(pl.ANY)] * len(behind),
        out_specs=spec(pltpu.VMEM),
        out_shape=jax.ShapeDtypeStruct((2, rows // 2, width), jnp.bfloat16),
        compiler_params=params(2),
        cost_estimate=COST,
        name="pair_sum",
    )(*mines, *gots, *behind)


def later_kernel(array_ref, *refs):
    refs[-1][...] = array_ref[...]


def later(array, behind):
    return pl.pallas_call(
        later_kernel,
        in_specs=[spec(pltpu.VMEM)] + [spec(pl.ANY)] * len(behind),
        out_specs=spec(pltpu.VMEM),
        out_shape=jax.ShapeDtypeStruct(array.shape, array.dtype),
        compiler_params=params(1),
        cost_estimate=COST,
        name="later",
    )(array, *behind)


def combine_kernel(n_parts, n_left, n_outs, *refs):
    mines, gots, chip_ref, refs = refs[:n_parts], refs[n_parts : 2 * n_parts], refs[2 * n_parts], refs[2 * n_parts + 1 :]
    lefts, outs = refs[:n_left], refs[n_left:]
    rows, at = chip_ref.shape[1], 0
    for left in lefts:
        outs[0][:, : left.shape[1]] = left[...]
    first = sum(left.shape[1] for left in lefts)
    for mine_ref, got_ref in zip(mines, gots):
        for a, b in pieces_of(got_ref.shape[2], TILE):
            gate, up = (
                mine_ref[k, :rows, a:b].astype(jnp.float32)
                + got_ref[k, :rows, a:b].astype(jnp.float32)
                + chip_ref[k, :, at + a : at + b].astype(jnp.float32)
                for k in range(2)
            )
            hidden = (gate / (1 + jnp.exp(-gate)) * up).astype(jnp.bfloat16)
            for i, out in enumerate(outs):
                out[:, first + at + a : first + at + b] = hidden[i * ROWS : (i + 1) * ROWS]
        at += got_ref.shape[2]


def combine(mines, gots, from_chip, left):
    _, rows, width = from_chip.shape
    n_outs = rows // ROWS
    width += sum(x.shape[1] for x in left)
    args = [*mines, *gots, from_chip, *left]
    return pl.pallas_call(
        functools.partial(combine_kernel, len(mines), len(left), n_outs),
        in_specs=[spec(pltpu.VMEM)] * len(args),
        out_specs=[spec(pltpu.VMEM)] * n_outs,
        out_shape=[jax.ShapeDtypeStruct((ROWS, width), jnp.bfloat16)] * n_outs,
        compiler_params=params(2),
        cost_estimate=COST,
        name="combine",
    )(*args)


def down_kernel(n_pieces, has_acc, last, segments, *refs):
    pieces, refs = refs[:n_pieces], refs[n_pieces:]
    down_ref, refs = refs[0], refs[1:]
    where = here(down_ref.shape[0] // 2)
    prev_ref, refs = (refs[0], refs[1:]) if has_acc else (None, refs)
    outs, (acc_ref, lhs_ref) = refs[:-2], refs[-2:]
    at = 0
    for piece in pieces:
        lhs_ref[at : at + piece.shape[0], :] = piece[...]
        at += piece.shape[0]
    lhs_ref[at:, :] = jnp.zeros_like(lhs_ref[at:, :])
    total = at
    for a, b in pieces_of(acc_ref.shape[1], 2 * TILE):
        part = prev_ref[:, a:b] if has_acc else 0.0
        at = 0
        for sign, start, depth in segments:
            rows = pl.ds(pl.multiple_of(sign * where[0] + start, TILE) if sign else start, depth)
            product = jnp.dot(lhs_ref[:, at : at + depth], down_ref[rows, a:b], preferred_element_type=jnp.float32)
            part += product[:total]
            at += depth
        acc_ref[:, a:b] = part
    if last:
        for d, out in enumerate(outs):
            source = pl.multiple_of(place(where[1], d) * ROWS, ROWS)
            out[...] = acc_ref[pl.ds(source, ROWS), :].astype(out.dtype)


def down(pieces, down_weight, prev, segments, last):
    width = down_weight.shape[1]
    total = 4 * ROWS
    args = [*pieces, down_weight] + ([] if prev is None else [prev])
    sums = jax.ShapeDtypeStruct((total, width), jnp.float32)
    scratch = [pltpu.VMEM((max(total, 128), pieces[0].shape[1]), jnp.bfloat16)]
    if last:
        scratch = [pltpu.VMEM(sums.shape, sums.dtype)] + scratch
    return pl.pallas_call(
        functools.partial(down_kernel, len(pieces), prev is not None, last, segments),
        in_specs=[spec(pltpu.VMEM)] * len(args),
        out_specs=[spec(pltpu.VMEM)] * 4 if last else spec(pltpu.VMEM),
        scratch_shapes=scratch,
        out_shape=[jax.ShapeDtypeStruct((ROWS, width), jnp.bfloat16)] * 4 if last else sums,
        compiler_params=params(4),
        cost_estimate=COST,
        name="down",
    )(*args)


def split_by_rep(tokens, gate_weight, up_weight, down_weight):
    f32, bf16 = jnp.float32, jnp.bfloat16
    half = gate_weight.shape[1] // 2

    def swap(x, axis, step):
        n = {"rep": 2, "hid": 4, "wid": 4}[axis]
        return lax.ppermute(x, axis, [(i, i ^ step) for i in range(n)])

    tiles = half // TILE
    bounds = [0, (tiles - LAST) // 2 * TILE, (tiles - LAST) * TILE, half]
    widths = [b - a for a, b in zip(bounds[:-1], bounds[1:])]
    gate_weight, up_weight, hbm_tokens = (
        pltpu.with_memory_space_constraint(w, pltpu.HBM) for w in (gate_weight, up_weight, tokens)
    )
    down_weight = pltpu.with_memory_space_constraint(down_weight, pltpu.VMEM)

    far_own = swap(tokens, "rep", 1)
    by_hid = [swap(tokens, "hid", d) for d in (3, 2, 1)][::-1]
    early = [fetch(gate_weight, up_weight, hbm_tokens, bounds[c], widths[c]) for c in range(2)]
    own = early[0][2]
    near = join(by_hid, [own, far_own])
    far = swap(near, "rep", 1)

    arrays = [own, near, far_own, far]
    mine_0, theirs = gate_up(arrays, early[0][:2], [], [early[1][0]])
    got_0 = swap(theirs, "wid", 1)
    mine_1, theirs = gate_up(arrays, early[1][:2], [], [mine_0])
    got_1 = swap(later(theirs, [got_0]), "wid", 1)
    mines, gots = [mine_0, mine_1], [got_0, got_1]
    to_chips = [pair_sum([mine], [got], []) for mine, got in zip(mines, gots)]
    from_chips = [swap(x, "wid", 2) for x in to_chips]
    segments = [(bounds[2], widths[2]), (half + bounds[2], widths[2])]
    last_mine, theirs = gate_up(arrays[:2], [gate_weight, up_weight], segments, to_chips)
    last_got = swap(later(theirs, from_chips), "wid", 1)

    keep, give = combine(mines, gots, jnp.concatenate(from_chips, 2), [])
    last_to_chip = pair_sum([last_mine], [last_got], [give])
    last_from_chip = swap(last_to_chip, "wid", 2)
    (rest,) = combine([last_mine], [last_got], last_from_chip, [swap(give, "rep", 1)])

    def gather(hidden, behind):
        other = swap(hidden, "wid", 2)
        return [hidden, other, swap(hidden, "wid", 1), swap(join([other], behind), "wid", 1)]

    acc = down(gather(keep, [rest]), down_weight, None, [(1, 0, bounds[2])], False)
    rest_segments = [(-1, half, bounds[2])] + [(0, start, width) for start, width in segments]
    acc = down(gather(rest, [acc]), down_weight, acc, rest_segments, True)

    mixed = acc[0].astype(f32)
    for d in (3, 2, 1):
        mixed = mixed + swap(acc[d], "hid", d).astype(f32)
    return mixed.astype(bf16)


def solution(mesh):
    n_rep, n_hid, n_wid = (mesh.shape[a] for a in ("rep", "hid", "wid"))

    def on_device(tokens, gate_weight, up_weight, down_weight):
        fits = (
            (n_rep, n_hid, n_wid) == (2, 4, 4)
            and gate_weight.shape[1] % (n_rep * TILE) == 0
            and tokens.shape[0] == ROWS
        )
        if not fits:
            return plain(tokens, gate_weight, up_weight, down_weight)
        return split_by_rep(tokens, gate_weight, up_weight, down_weight)

    return jax.shard_map(
        on_device,
        mesh=mesh,
        in_specs=(P(("rep", "hid"), "wid"), P("wid", "hid"), P("wid", "hid"), P("hid", "wid")),
        out_specs=P(("rep", "hid"), "wid"),
        check_vma=False,
    )
```

```python
import functools

import jax
import jax.numpy as jnp
from jax import lax
from jax.experimental import pallas as pl
from jax.experimental.pallas import tpu as pltpu
from jax.sharding import PartitionSpec as P

TILE = 256
LAST = 3
ROWS = 16
COST = pl.CostEstimate(flops=0, bytes_accessed=1024, transcendentals=0)


def plain(tokens, gate_weight, up_weight, down_weight):
    piece = lax.all_gather(tokens, "hid", axis=0, tiled=True)
    gate_rows = jnp.dot(piece, gate_weight, preferred_element_type=jnp.float32)
    up_rows = jnp.dot(piece, up_weight, preferred_element_type=jnp.float32)
    partial_terms = jnp.stack([gate_rows, up_rows], 0)
    summed = lax.psum(partial_terms.astype(jnp.bfloat16), "wid").astype(jnp.float32)
    hidden = (jax.nn.silu(summed[0]) * summed[1]).astype(jnp.bfloat16)
    return lax.psum_scatter(
        jnp.dot(hidden, down_weight, preferred_element_type=jnp.float32).astype(jnp.bfloat16),
        "hid",
        scatter_dimension=0,
        tiled=True,
    )


def pieces_of(width, most):
    first = width % most
    edges = ([0] if first else []) + list(range(first, width + 1, most))
    return list(zip(edges[:-1], edges[1:]))


def place(wid, d):
    step = wid ^ d
    return (step % 2) * 2 + step // 2


def here(half):
    return lax.axis_index("rep") * half, lax.axis_index("wid")


def spec(space):
    return pl.BlockSpec(memory_space=space)


def params(mib):
    return pltpu.CompilerParams(vmem_limit_bytes=mib * 2**20)


def column_copies(source_ref, out_ref, segments, sems):
    copies, cuts, at = [], [], 0
    for start, width in segments:
        for a, b in pieces_of(width, 2 * TILE):
            source = source_ref.at[:, pl.ds(pl.multiple_of(start + a, TILE), b - a)]
            copies.append(pltpu.make_async_copy(source, out_ref.at[:, at + a : at + b], sems.at[len(copies)]))
            cuts.append((at + a, at + b))
        at += width
    return copies, cuts


def fetch_kernel(first, gate_ref, up_ref, tokens_ref, gate_out, up_out, tokens_out, sems):
    where = here(gate_ref.shape[1] // 2)
    copies = [pltpu.make_async_copy(tokens_ref, tokens_out, sems.at[2, 0])]
    for k, (source, out) in enumerate(((gate_ref, gate_out), (up_ref, up_out))):
        copies += column_copies(source, out, [(where[0] + first, out.shape[1])], sems.at[k])[0]
    for copy in copies:
        copy.start()
    for copy in copies:
        copy.wait()


def fetch(gate, up, tokens, first, width):
    depth = gate.shape[0]
    return pl.pallas_call(
        functools.partial(fetch_kernel, first),
        in_specs=[spec(pltpu.HBM)] * 3,
        out_specs=[spec(pltpu.VMEM)] * 3,
        out_shape=[pltpu.VMEM(x, jnp.bfloat16) for x in ((depth, width), (depth, width), tokens.shape)],
        scratch_shapes=[pltpu.SemaphoreType.DMA((3, len(pieces_of(width, 2 * TILE))))],
        compiler_params=params(1),
        cost_estimate=COST,
        name="fetch",
    )(gate, up, tokens)


def join_kernel(n, first, *refs):
    out_ref, at = refs[-1], 0
    for ref in refs[:n]:
        out_ref[at : at + ref.shape[0], :] = ref[:, first : first + out_ref.shape[1]]
        at += ref.shape[0]


def join(arrays, behind, first=0, width=None):
    rows, width = sum(a.shape[0] for a in arrays), width or arrays[0].shape[1]
    return pl.pallas_call(
        functools.partial(join_kernel, len(arrays), first),
        in_specs=[spec(pltpu.VMEM)] * len(arrays) + [spec(pl.ANY)] * len(behind),
        out_specs=spec(pltpu.VMEM),
        out_shape=jax.ShapeDtypeStruct((rows, width), arrays[0].dtype),
        compiler_params=params(1),
        cost_estimate=COST,
        name="join",
    )(*arrays, *behind)


def gate_up_kernel(n_arrays, n_pairs, segments, *refs):
    where = here(0)
    arrays, weights = refs[:n_arrays], refs[n_arrays : n_arrays + 2 * n_pairs]
    if segments:
        mine_ref, theirs_ref, x_ref, w_ref, sems = refs[-5:]
        copies = [column_copies(weights[k], w_ref.at[k], segments, sems.at[k]) for k in range(2)]
        cuts = copies[0][1]
        for i in range(len(cuts)):
            for k in range(2):
                copies[k][0][i].start()
    else:
        mine_ref, theirs_ref, x_ref = refs[-3:]
        step = weights[0].shape[1]
        cuts = [(p * step + a, p * step + b) for p in range(n_pairs) for a, b in pieces_of(step, 2 * TILE)]
    per = x_ref.shape[0] // (4 * ROWS)
    b = 0
    for array in arrays:
        for at in range(0, array.shape[0], ROWS):
            to = (place(where[1], b % 4) * per + b // 4) * ROWS
            x_ref[pl.ds(pl.multiple_of(to, ROWS), ROWS), :] = array[at : at + ROWS, :]
            b += 1
    half = x_ref.shape[0] // 2
    for i, (a, b) in enumerate(cuts):
        for k in range(2):
            if segments:
                copies[k][0][i].wait()
                weight = w_ref[k, :, a:b]
            else:
                p = a // step
                weight = weights[2 * p + k][:, a - p * step : b - p * step]
            part = jnp.dot(x_ref[...], weight, preferred_element_type=jnp.float32).astype(jnp.bfloat16)
            mine_ref[k, :, a:b] = part[:half]
            theirs_ref[k, :, a:b] = part[half:]


def gate_up(arrays, weights, segments, behind):
    depth = weights[0].shape[0]
    width = sum(w for _, w in segments) if segments else sum(w.shape[1] for w in weights[::2])
    total = sum(a.shape[0] for a in arrays)
    scratch = [pltpu.VMEM((total, depth), jnp.bfloat16)]
    if segments:
        n_cuts = sum(len(pieces_of(w, 2 * TILE)) for _, w in segments)
        scratch.append(pltpu.VMEM((2, depth, width), jnp.bfloat16))
        scratch.append(pltpu.SemaphoreType.DMA((2, n_cuts)))
    return pl.pallas_call(
        functools.partial(gate_up_kernel, len(arrays), len(weights) // 2, segments),
        in_specs=[spec(pltpu.VMEM)] * len(arrays)
        + [spec(pltpu.HBM if segments else pltpu.VMEM)] * len(weights)
        + [spec(pl.ANY)] * len(behind),
        out_specs=[spec(pltpu.VMEM)] * 2,
        scratch_shapes=scratch,
        out_shape=[jax.ShapeDtypeStruct((2, total // 2, width), jnp.bfloat16)] * 2,
        compiler_params=params(16 if segments else 4),
        cost_estimate=COST,
        name="gate_up",
    )(*arrays, *weights, *behind)


def pair_sum_kernel(n_parts, *refs):
    out_ref, at = refs[2 * n_parts], 0
    rows = out_ref.shape[1]
    for mine_ref, got_ref in zip(refs[:n_parts], refs[n_parts : 2 * n_parts]):
        width = got_ref.shape[2]
        for k in range(2):
            total = mine_ref[k, rows:].astype(jnp.float32) + got_ref[k, rows:].astype(jnp.float32)
            out_ref[k, :, at : at + width] = total.astype(out_ref.dtype)
        at += width


def pair_sum(mines, gots, behind):
    _, rows, _ = mines[0].shape
    width = sum(x.shape[2] for x in gots)

    def kernel(*refs):
        inputs, rest = refs[: 2 * len(mines)], refs[2 * len(mines) + len(behind) :]
        pair_sum_kernel(len(mines), *inputs, *rest)

    return pl.pallas_call(
        kernel,
        in_specs=[spec(pltpu.VMEM)] * (2 * len(mines)) + [spec(pl.ANY)] * len(behind),
        out_specs=spec(pltpu.VMEM),
        out_shape=jax.ShapeDtypeStruct((2, rows // 2, width), jnp.bfloat16),
        compiler_params=params(2),
        cost_estimate=COST,
        name="pair_sum",
    )(*mines, *gots, *behind)


def later_kernel(array_ref, *refs):
    refs[-1][...] = array_ref[...]


def later(array, behind):
    return pl.pallas_call(
        later_kernel,
        in_specs=[spec(pltpu.VMEM)] + [spec(pl.ANY)] * len(behind),
        out_specs=spec(pltpu.VMEM),
        out_shape=jax.ShapeDtypeStruct(array.shape, array.dtype),
        compiler_params=params(1),
        cost_estimate=COST,
        name="later",
    )(array, *behind)


def combine_kernel(n_parts, n_left, n_outs, *refs):
    mines, gots, chip_ref, refs = refs[:n_parts], refs[n_parts : 2 * n_parts], refs[2 * n_parts], refs[2 * n_parts + 1 :]
    lefts, outs = refs[:n_left], refs[n_left:]
    rows, at = chip_ref.shape[1], 0
    for left in lefts:
        outs[0][:, : left.shape[1]] = left[...]
    first = sum(left.shape[1] for left in lefts)
    for mine_ref, got_ref in zip(mines, gots):
        for a, b in pieces_of(got_ref.shape[2], TILE):
            gate, up = (
                mine_ref[k, :rows, a:b].astype(jnp.float32)
                + got_ref[k, :rows, a:b].astype(jnp.float32)
                + chip_ref[k, :, at + a : at + b].astype(jnp.float32)
                for k in range(2)
            )
            hidden = (gate / (1 + jnp.exp(-gate)) * up).astype(jnp.bfloat16)
            for i, out in enumerate(outs):
                out[:, first + at + a : first + at + b] = hidden[i * ROWS : (i + 1) * ROWS]
        at += got_ref.shape[2]


def combine(mines, gots, from_chip, left):
    _, rows, width = from_chip.shape
    n_outs = rows // ROWS
    width += sum(x.shape[1] for x in left)
    args = [*mines, *gots, from_chip, *left]
    return pl.pallas_call(
        functools.partial(combine_kernel, len(mines), len(left), n_outs),
        in_specs=[spec(pltpu.VMEM)] * len(args),
        out_specs=[spec(pltpu.VMEM)] * n_outs,
        out_shape=[jax.ShapeDtypeStruct((ROWS, width), jnp.bfloat16)] * n_outs,
        compiler_params=params(2),
        cost_estimate=COST,
        name="combine",
    )(*args)


def down_kernel(n_pieces, has_acc, last, segments, *refs):
    pieces, refs = refs[:n_pieces], refs[n_pieces:]
    down_ref, refs = refs[0], refs[1:]
    where = here(down_ref.shape[0] // 2)
    prev_ref, refs = (refs[0], refs[1:]) if has_acc else (None, refs)
    outs, (acc_ref, lhs_ref) = refs[:-2], refs[-2:]
    at = 0
    for piece in pieces:
        lhs_ref[at : at + piece.shape[0], :] = piece[...]
        at += piece.shape[0]
    lhs_ref[at:, :] = jnp.zeros_like(lhs_ref[at:, :])
    total = at
    for a, b in pieces_of(acc_ref.shape[1], 2 * TILE):
        part = prev_ref[:, a:b] if has_acc else 0.0
        at = 0
        for sign, start, depth in segments:
            rows = pl.ds(pl.multiple_of(sign * where[0] + start, TILE) if sign else start, depth)
            product = jnp.dot(lhs_ref[:, at : at + depth], down_ref[rows, a:b], preferred_element_type=jnp.float32)
            part += product[:total]
            at += depth
        acc_ref[:, a:b] = part
    if last:
        for d, out in enumerate(outs):
            source = pl.multiple_of(place(where[1], d) * ROWS, ROWS)
            out[...] = acc_ref[pl.ds(source, ROWS), :].astype(out.dtype)


def down(pieces, down_weight, prev, segments, last):
    width = down_weight.shape[1]
    total = 4 * ROWS
    args = [*pieces, down_weight] + ([] if prev is None else [prev])
    sums = jax.ShapeDtypeStruct((total, width), jnp.float32)
    scratch = [pltpu.VMEM((max(total, 128), pieces[0].shape[1]), jnp.bfloat16)]
    if last:
        scratch = [pltpu.VMEM(sums.shape, sums.dtype)] + scratch
    return pl.pallas_call(
        functools.partial(down_kernel, len(pieces), prev is not None, last, segments),
        in_specs=[spec(pltpu.VMEM)] * len(args),
        out_specs=[spec(pltpu.VMEM)] * 4 if last else spec(pltpu.VMEM),
        scratch_shapes=scratch,
        out_shape=[jax.ShapeDtypeStruct((ROWS, width), jnp.bfloat16)] * 4 if last else sums,
        compiler_params=params(4),
        cost_estimate=COST,
        name="down",
    )(*args)


def split_by_rep(tokens, gate_weight, up_weight, down_weight):
    f32, bf16 = jnp.float32, jnp.bfloat16
    half = gate_weight.shape[1] // 2

    def swap(x, axis, step):
        n = {"rep": 2, "hid": 4, "wid": 4}[axis]
        return lax.ppermute(x, axis, [(i, i ^ step) for i in range(n)])

    tiles = half // TILE
    bounds = [0, (tiles - LAST) // 2 * TILE, (tiles - LAST) * TILE, half]
    widths = [b - a for a, b in zip(bounds[:-1], bounds[1:])]
    gate_weight, up_weight, hbm_tokens = (
        pltpu.with_memory_space_constraint(w, pltpu.HBM) for w in (gate_weight, up_weight, tokens)
    )
    down_weight = pltpu.with_memory_space_constraint(down_weight, pltpu.VMEM)

    far_own = swap(tokens, "rep", 1)
    by_hid = [swap(tokens, "hid", d) for d in (3, 2, 1)][::-1]
    early = [fetch(gate_weight, up_weight, hbm_tokens, bounds[c], widths[c]) for c in range(2)]
    own = early[0][2]
    near = join(by_hid, [own, far_own])
    far = swap(near, "rep", 1)

    arrays = [own, near, far_own, far]
    mine_0, theirs = gate_up(arrays, early[0][:2], [], [early[1][0]])
    got_0 = swap(theirs, "wid", 1)
    mine_1, theirs = gate_up(arrays, early[1][:2], [], [mine_0])
    got_1 = swap(later(theirs, [got_0]), "wid", 1)
    mines, gots = [mine_0, mine_1], [got_0, got_1]
    to_chips = [pair_sum([mine], [got], []) for mine, got in zip(mines, gots)]
    from_chips = [swap(x, "wid", 2) for x in to_chips]
    segments = [(bounds[2], widths[2]), (half + bounds[2], widths[2])]
    last_mine, theirs = gate_up(arrays[:2], [gate_weight, up_weight], segments, to_chips)
    last_got = swap(later(theirs, from_chips[:1]), "wid", 1)

    keep, give = combine(mines, gots, jnp.concatenate(from_chips, 2), [])
    last_to_chip = pair_sum([last_mine], [last_got], [give])
    last_from_chip = swap(last_to_chip, "wid", 2)
    (rest,) = combine([last_mine], [last_got], last_from_chip, [swap(give, "rep", 1)])

    def gather(hidden, behind):
        other = swap(hidden, "wid", 2)
        return [hidden, other, swap(hidden, "wid", 1), swap(join([other], behind), "wid", 1)]

    acc = down(gather(keep, [rest]), down_weight, None, [(1, 0, bounds[2])], False)
    rest_segments = [(-1, half, bounds[2])] + [(0, start, width) for start, width in segments]
    acc = down(gather(rest, [acc]), down_weight, acc, rest_segments, True)

    mixed = acc[0].astype(f32)
    for d in (3, 2, 1):
        mixed = mixed + swap(acc[d], "hid", d).astype(f32)
    return mixed.astype(bf16)


def solution(mesh):
    n_rep, n_hid, n_wid = (mesh.shape[a] for a in ("rep", "hid", "wid"))

    def on_device(tokens, gate_weight, up_weight, down_weight):
        fits = (
            (n_rep, n_hid, n_wid) == (2, 4, 4)
            and gate_weight.shape[1] % (n_rep * TILE) == 0
            and tokens.shape[0] == ROWS
        )
        if not fits:
            return plain(tokens, gate_weight, up_weight, down_weight)
        return split_by_rep(tokens, gate_weight, up_weight, down_weight)

    return jax.shard_map(
        on_device,
        mesh=mesh,
        in_specs=(P(("rep", "hid"), "wid"), P("wid", "hid"), P("wid", "hid"), P("hid", "wid")),
        out_specs=P(("rep", "hid"), "wid"),
        check_vma=False,
    )
```
